32 devices in a mesh: wide: 8 (over z, x), narrow: 4 (over y, core).
Axes of the slice: x: 2, y: 2, z: 4, core: 2. Of those that a mesh axis runs over, the one named last changes fastest.
Arguments:
- block_in: bfloat16 [51840, 2048], P(('wide', 'narrow')), may hold values from -6 to 6
- weight_reduce: bfloat16 [2048, 512], replicated, may hold values from -0.125 to 0.125
- gain_reduce: float32 [512], replicated, may hold values from 0.5 to 1.5
- shift_reduce: float32 [512], replicated, may hold values from -3 to 3
- weight_spatial: bfloat16 [4608, 512], replicated, may hold values from -0.09375 to 0.09375
- gain_spatial: float32 [512], replicated, may hold values from 0.5 to 1.5
- shift_spatial: float32 [512], replicated, may hold values from -3 to 3
- weight_expand: bfloat16 [512, 2048], replicated, may hold values from -0.25 to 0.25
- gain_expand: float32 [2048], replicated, may hold values from 0.5 to 1.5
- shift_expand: float32 [2048], replicated, may hold values from -3 to 3
- head_weight: bfloat16 [2048, 128], replicated, may hold values from -0.25 to 0.25
- head_bias: float32 [128], replicated, may hold values from -3 to 3
- jigsaw_weight: bfloat16 [1152, 128], replicated, may hold values from -0.1875 to 0.1875
- jigsaw_bias: float32 [128], replicated, may hold values from -3 to 3
- resolution: int32 [640], replicated, may hold values from 0 to 1
- tile_slot: int32 [8, 720], P('wide'), may hold values from 0 to 719, each once within a row
- jigsaw_perm: int32 [640, 9], P('wide'), may hold values from 0 to 8, each once within a row
- cotangent: bfloat16 [640, 128], P('wide'), may hold values from -6 to 6
Outputs:
- block_out: bfloat16 [51840, 2048], P(('wide', 'narrow'))
- jigsaw_out: float32 [640, 128], P(('wide', 'narrow'))
- gradient_input: bfloat16 [51840, 2048], P(('wide', 'narrow'))
- gradient_reduce: float32 [2048, 512], replicated
- gradient_gain_reduce: float32 [512], replicated
- gradient_shift_reduce: float32 [512], replicated
- gradient_spatial: float32 [4608, 512], replicated
- gradient_gain_spatial: float32 [512], replicated
- gradient_shift_spatial: float32 [512], replicated
- gradient_expand: float32 [512, 2048], replicated
- gradient_gain_expand: float32 [2048], replicated
- gradient_shift_expand: float32 [2048], replicated
- gradient_head_weight: float32 [2048, 128], replicated
- gradient_head_bias: float32 [128], replicated
- gradient_jigsaw_weight: float32 [1152, 128], replicated
- gradient_jigsaw_bias: float32 [128], replicated
The draws below stay inside these ranges and needn't reach their ends.
Inputs may be any that keep to these rules, and one draw needn't show every extreme that they name: Each row of tile_slot is a permutation of the 720 tiles of one group: entry s names image-within-group times 9 plus piece. `jigsaw_perm`: each row is a permutation of the nine pieces. `resolution`: 1 for an image whose tiles have 3 x 3 maps, 0 for 2 x 2 maps.
All inputs are finite; a program needn't handle non-finite values.
Results may differ from the reference program's by a relative error of at most 0.0094.
Values may be sent and summed in bfloat16 or wider, within the bound.
No kernel may reach another device: no remote copies, remote signals or barrier semaphores. Data moves between devices by JAX's collectives and lax.ppermute only.
A program may use at most 256 MiB of HBM per device.

```python
import jax
import jax.numpy as jnp
from jax import lax

D = 2048
MID = 512
EMB = 128
PIX = 9
PIECES = 9
TILES_GROUP = 720
IMG_GROUP = 80
GROUPS = 8
IMAGES = 640
TILES = 5760
ROWS = 51840


def set_ends(drawn, rng, low, largest):
    extent = drawn.shape
    place = [jax.random.randint(jax.random.fold_in(rng, axis), (), 0, extent[axis]) for axis in range(len(extent))]
    drawn = drawn.at[tuple(place)].set(low)
    longest = extent.index(max(extent))
    place[longest] = (place[longest] + 1) % extent[longest]
    return drawn.at[tuple(place)].set(largest)


def level_of(stream_key, dims, split, least, high):
    level = 1.0
    for dim, parts in split:
        draws = jax.random.uniform(jax.random.fold_in(jax.random.fold_in(stream_key, 6), dim), (parts,), jnp.float32, least / len(split), high / len(split))
        level = level * jnp.repeat(jnp.exp(draws), dims[dim] // parts).reshape((-1,) + (1,) * (len(dims) - 1 - dim))
    return level


def centred(rng, shape, width, limit, cuts=(), held_as=jnp.bfloat16):
    result = jax.random.normal(rng, shape, jnp.float32) * width
    if len(cuts) > 0:
        result = level_of(rng, shape, cuts, -0.22, 0.18) * result
    return jnp.clip(result, min=-limit, max=limit).astype(held_as)


def setup_inputs(seed: int = 0) -> dict:
    key_list = jax.random.split(jax.random.key(seed), 19)
    block_in = centred(key_list[0], (ROWS, D), 1.0, 6.0, ((0, 32),))
    weight_reduce = centred(key_list[1], (D, MID), D ** -0.5, 0.125)
    gain_reduce = jnp.clip(1.0 + 0.1 * jax.random.normal(key_list[2], (MID,), jnp.float32), 0.5, 1.5)
    shift_reduce = centred(key_list[3], (MID,), 0.5, 3.0, (), jnp.float32)
    weight_spatial = centred(key_list[4], (PIX * MID, MID), (PIX * MID) ** -0.5, 0.09375)
    gain_spatial = jnp.clip(1.0 + 0.1 * jax.random.normal(key_list[5], (MID,), jnp.float32), 0.5, 1.5)
    shift_spatial = centred(key_list[6], (MID,), 0.5, 3.0, (), jnp.float32)
    weight_expand = centred(key_list[7], (MID, D), MID ** -0.5, 0.25)
    gain_expand = jnp.clip(1.0 + 0.1 * jax.random.normal(key_list[8], (D,), jnp.float32), 0.5, 1.5)
    shift_expand = centred(key_list[9], (D,), 0.5, 3.0, (), jnp.float32)
    head_weight = centred(key_list[10], (D, EMB), (D // 4) ** -0.5, 0.25)
    head_bias = centred(key_list[11], (EMB,), 0.5, 3.0, (), jnp.float32)
    jigsaw_weight = centred(key_list[12], (PIECES * EMB, EMB), (PIECES * EMB) ** -0.5, 0.1875)
    jigsaw_bias = centred(key_list[13], (EMB,), 0.5, 3.0, (), jnp.float32)
    resolution = set_ends(jax.random.randint(key_list[14], (IMAGES,), 0, 2), jax.random.fold_in(key_list[14], 1), 0, 1).astype(jnp.int32)
    tile_slot = jax.vmap(lambda own: jax.random.permutation(own, TILES_GROUP))(jax.random.split(key_list[15], GROUPS)).reshape((GROUPS, TILES_GROUP)).astype(jnp.int32)
    jigsaw_perm = jax.vmap(lambda own: jax.random.permutation(own, PIECES))(jax.random.split(key_list[16], IMAGES)).reshape((IMAGES, PIECES)).astype(jnp.int32)
    cotangent = centred(key_list[17], (IMAGES, EMB), 1.0, 6.0, ((0, 8),))
    return dict(block_in=block_in, weight_reduce=weight_reduce, gain_reduce=gain_reduce, shift_reduce=shift_reduce, weight_spatial=weight_spatial, gain_spatial=gain_spatial, shift_spatial=shift_spatial, weight_expand=weight_expand, gain_expand=gain_expand, shift_expand=shift_expand, head_weight=head_weight, head_bias=head_bias, jigsaw_weight=jigsaw_weight, jigsaw_bias=jigsaw_bias, resolution=resolution, tile_slot=tile_slot, jigsaw_perm=jigsaw_perm, cotangent=cotangent)


EPS = 1e-05

@jax.custom_vjp
def low(v):
    return lax.optimization_barrier(v.astype(jnp.bfloat16)).astype(jnp.float32)

@jax.custom_vjp
def low_back(v):
    return v

def low_keep(v):
    return (low(v), None)

def low_pass(kept, grad):
    return (grad,)

def back_keep(v):
    return (v, None)

def back_low(kept, grad):
    return (low(grad),)
low.defvjp(low_keep, low_pass)
low_back.defvjp(back_keep, back_low)

def smooth(activation):
    return jax.nn.gelu(activation, approximate=True)

def matmul_high(first_operand, second_operand):
    return jnp.dot(first_operand, second_operand, precision=lax.Precision.HIGHEST, preferred_element_type=jnp.float32)

def batch_norm(pre_norm, valid_rows, total_cells, gain, shift):
    average = lax.optimization_barrier(jnp.sum(pre_norm * valid_rows, 0)) / total_cells
    spread = lax.optimization_barrier(jnp.sum(pre_norm * pre_norm * valid_rows, 0)) / total_cells - average * average
    return (pre_norm - average) * lax.rsqrt(spread + EPS) * gain + shift

def windows(feature_map, tile_count):
    channels = feature_map.shape[-1]
    tile_grid = feature_map.reshape(tile_count, 3, 3, channels)
    padded = jnp.pad(tile_grid, ((0, 0), (1, 1), (1, 1), (0, 0)))
    patches = [padded[:, offset_row:offset_row + 3, offset_col:offset_col + 3, :] for offset_row in range(3) for offset_col in range(3)]
    return jnp.concatenate(patches, -1).reshape(tile_count * 9, 9 * channels)

def reference(block_in, weight_reduce, gain_reduce, shift_reduce, weight_spatial, gain_spatial, shift_spatial, weight_expand, gain_expand, shift_expand, head_weight, head_bias, jigsaw_weight, jigsaw_bias, resolution, tile_slot, jigsaw_perm, cotangent):
    tile_ids = tile_slot.reshape(-1)
    group_of = jnp.arange(TILES, dtype=jnp.int32) // TILES_GROUP
    image_index = group_of * IMG_GROUP + tile_ids // PIECES
    large_tile = resolution[image_index]
    position = jnp.arange(PIX, dtype=jnp.int32)
    corner = (position // 3 < 2) & (position % 3 < 2)
    valid_rows = ((large_tile[:, None] > 0) | corner[None, :]).astype(jnp.float32).reshape(ROWS, 1)
    tile_cells = (4 + 5 * large_tile).astype(jnp.float32)
    total_cells = jnp.sum((4 + 5 * resolution).astype(jnp.float32)) * 9.0
    group_rows = jnp.arange(GROUPS, dtype=jnp.int32)[:, None]
    slot_numbers = jnp.broadcast_to(jnp.arange(TILES_GROUP, dtype=jnp.int32)[None, :], (GROUPS, TILES_GROUP))
    slot_of = jnp.zeros((GROUPS, TILES_GROUP), jnp.int32).at[group_rows, tile_slot].set(slot_numbers)
    image_group = jnp.arange(IMAGES, dtype=jnp.int32) // IMG_GROUP
    image_local = jnp.arange(IMAGES, dtype=jnp.int32) % IMG_GROUP
    wanted = image_local[:, None] * PIECES + jigsaw_perm
    slot_index = (image_group[:, None] * TILES_GROUP + slot_of[image_group[:, None], wanted]).reshape(-1)

    def forward(inputs, weight_one, gain_one, shift_one, weight_two, gain_two, shift_two, weight_three, gain_three, shift_three, weight_head, bias_head, weight_jig, bias_jig):
        pre_one = low_back(matmul_high(inputs, weight_one))
        hidden_one = low(smooth(batch_norm(pre_one, valid_rows, total_cells, gain_one, shift_one)) * valid_rows)
        pre_two = low_back(matmul_high(windows(hidden_one, TILES), weight_two))
        hidden_two = low(smooth(batch_norm(pre_two, valid_rows, total_cells, gain_two, shift_two)) * valid_rows)
        pre_three = low_back(matmul_high(hidden_two, weight_three))
        summed = batch_norm(pre_three, valid_rows, total_cells, gain_three, shift_three) + inputs
        mapped = smooth(summed) * valid_rows
        pooled = low(lax.optimization_barrier(jnp.sum(mapped.reshape(TILES, PIX, D), 1)) / tile_cells[:, None])
        embedded = low(low_back(matmul_high(pooled, weight_head) + bias_head))
        ordered = embedded[slot_index].reshape(IMAGES, PIECES * EMB)
        return (mapped, matmul_high(ordered, weight_jig) + bias_jig)
    floats = tuple((item.astype(jnp.float32) for item in (block_in, weight_reduce, gain_reduce, shift_reduce, weight_spatial, gain_spatial, shift_spatial, weight_expand, gain_expand, shift_expand, head_weight, head_bias, jigsaw_weight, jigsaw_bias)))
    (mapped, jig_out), pullback = jax.vjp(forward, *floats)
    gradients = pullback((jnp.zeros_like(mapped), cotangent.astype(jnp.float32)))
    return (mapped.astype(jnp.bfloat16), jig_out, gradients[0].astype(jnp.bfloat16), gradients[1], gradients[2], gradients[3], gradients[4], gradients[5], gradients[6], gradients[7], gradients[8], gradients[9], gradients[10], gradients[11], gradients[12], gradients[13])
```

```python
import functools

import jax
import jax.numpy as jnp
from jax import lax
from jax.experimental import pallas as pl
from jax.experimental.pallas import tpu as pltpu
from jax.sharding import PartitionSpec as P

BF = jnp.bfloat16
F32 = jnp.float32
EPS = 1e-05
AXES = ("wide", "narrow")
PIX = 9
CHUNK = 48
SUB = 16
C1 = 0.7978845608028654
C2 = C1 * 0.044715
VMEM = pl.BlockSpec(memory_space=pltpu.VMEM)
HBM = pl.BlockSpec(memory_space=pltpu.HBM)
SMEM = pl.BlockSpec(memory_space=pltpu.SMEM)


def dot(a, b, ca=1, cb=0):
    return lax.dot_general(a, b, (((ca,), (cb,)), ((), ())), preferred_element_type=F32)


def dot_rows(row, b, cb=0):
    high = row.astype(BF)
    rest = row - high.astype(F32)
    mid = rest.astype(BF)
    low = (rest - mid.astype(F32)).astype(BF)
    stack = jnp.concatenate([high, mid, low, jnp.zeros((13, row.shape[1]), BF)], 0)
    return jnp.sum(dot(stack, b, 1, cb), 0, keepdims=True)


def spread(mask, width):
    return jnp.concatenate([mask] * (width // 128), 1)


def gelu(v):
    squared = v * v
    half = 0.5 * v
    return half + half * jnp.tanh(v * (C1 + C2 * squared))


def gelu_both(v):
    squared = v * v
    gate = 0.5 * jnp.tanh(v * (C1 + C2 * squared)) + 0.5
    value = v * gate
    return value, gate + value * (1.0 - gate) * (2.0 * C1 + 6.0 * C2 * squared)


def gelu_slope(v):
    return gelu_both(v)[1]


def spans(offset):
    down, right = offset // 3 - 1, offset % 3 - 1
    rows = [r for r in range(3) if 0 <= r + down < 3]
    if right == 0:
        return [(rows[0] * 3, (rows[0] + down) * 3, 3 * len(rows))]
    start = max(0, -right)
    return [(r * 3 + start, (r + down) * 3 + start + right, 2) for r in rows]


OFFSETS = (4, 1, 7, 3, 5, 0, 2, 6, 8)


def places(ref, first, count):
    chunks, _, width = ref.shape
    return ref[:, first * CHUNK : (first + count) * CHUNK, :].reshape(
        chunks * count * CHUNK, width
    )


def add_places(ref, first, count, value, start):
    chunks, _, width = ref.shape
    rows = pl.ds(first * CHUNK, count * CHUNK)
    value = value.reshape(chunks, count * CHUNK, width)
    if start:
        ref[:, rows, :] = value
    else:
        ref[:, rows, :] = ref[:, rows, :] + value


def moments(payload, count):
    total = jnp.sum(payload[...], 0)
    mean = total[0:1] / count
    inv = lax.rsqrt(total[1:2] / count - mean * mean + EPS)
    return total, mean, inv


def reduce_kernel(
    x_ref, w_ref, slots_ref, res_ref, perm_ref, cot_ref, jw_ref, dev_ref,
    xp_ref, pre_ref, pay_ref, mask_ref, pick_ref, back_ref, count_ref,
    buf, flat, sems, *, tiles, own,
):
    rows, depth = x_ref.shape
    chunks, chunk_rows, _ = xp_ref.shape
    padded = chunks * CHUNK
    block = buf.shape[2]
    blocks = depth // block
    lanes = block // 128

    def copy(d):
        return pltpu.make_async_copy(
            x_ref.at[:, pl.ds(d * block, block)], buf.at[d % 2], sems.at[d % 2]
        )

    copy(0).start()
    ids = slots_ref[...]
    image = lax.shift_right_arithmetic(ids * 7282, 16)
    piece = ids - 9 * image
    images = perm_ref.shape[0]
    here = jnp.where(image < 0, -1, image + dev_ref[0] * images)
    all_images = res_ref.shape[1]
    hit_all = lax.broadcasted_iota(jnp.int32, (all_images, padded), 0) == here
    res = res_ref[...].astype(F32)
    flags = dot(
        jnp.broadcast_to(res, (16, all_images)).astype(BF), jnp.where(hit_all, 1.0, 0.0).astype(BF)
    )[0:1]
    eye = lax.broadcasted_iota(jnp.int32, (padded, padded), 0) == lax.broadcasted_iota(
        jnp.int32, (padded, padded), 1
    )
    large = dot(jnp.where(eye, flags, 0.0).astype(BF), jnp.ones((padded, 128), BF))
    exists = lax.broadcasted_iota(jnp.int32, (padded, 128), 0) < tiles
    mask_ref[0] = jnp.where(exists, 1.0, 0.0)
    mask_ref[1] = large
    mask_ref[2] = 1.0 / (4.0 + 5.0 * large)
    total = 9.0 * (4.0 * all_images + 5.0 * jnp.sum(res, 1, keepdims=True))
    count_ref[...] = jnp.broadcast_to(total, (8, 128))
    hit = lax.broadcasted_iota(jnp.int32, (images, padded), 0) == image
    rows_back = dot(cot_ref[...], jw_ref[...], 1, 1).astype(BF)
    back = jnp.zeros((padded, 128), F32)
    for k in range(PIX):
        chosen = jnp.where(hit & (perm_ref[:, k : k + 1] == piece), 1.0, 0.0).astype(BF)
        pick_ref[k * images : (k + 1) * images, :] = chosen
        back = back + dot(chosen, rows_back[:, k * 128 : (k + 1) * 128], 0, 0)
    back = back.astype(BF)
    back_ref[...] = back
    tail = rows - (chunks - 1) * chunk_rows
    for d in range(blocks):
        if d + 1 < blocks:
            copy(d + 1).start()
        copy(d).wait()
        cols = slice(d * block, (d + 1) * block)
        for c in range(chunks):
            size = chunk_rows if c + 1 < chunks else tail
            for lane in range(lanes):
                flat[lane, 0:size, :] = buf[
                    d % 2, c * chunk_rows : c * chunk_rows + size, lane * 128 : (lane + 1) * 128
                ].astype(F32)
                if size < chunk_rows:
                    flat[lane, size:, :] = jnp.zeros((chunk_rows - size, 128), F32)
            for p in range(PIX):
                xp_ref[c, p * CHUNK : (p + 1) * CHUNK, cols] = jnp.concatenate(
                    [flat[lane, pl.ds(p, CHUNK, stride=PIX), :] for lane in range(lanes)], 1
                ).astype(BF)
        part = dot(
            xp_ref[:, :, cols].reshape(chunks * chunk_rows, block), w_ref[cols, :]
        ).reshape(pre_ref.shape)
        pre_ref[...] = part if d == 0 else pre_ref[...] + part
    width = pre_ref.shape[2]

    def sums(c, carry):
        first, second = carry
        for p in range(PIX):
            a = pre_ref[c, p * CHUNK : (p + 1) * CHUNK, :]
            if p not in (0, 1, 3, 4):
                m = spread(mask_ref[1, pl.ds(pl.multiple_of(c * CHUNK, CHUNK), CHUNK), :], width)
                a = a * m
            first = first + jnp.sum(a.reshape(CHUNK // 8, 8, width), 0)
            second = second + jnp.sum((a * a).reshape(CHUNK // 8, 8, width), 0)
        return first, second

    zero = jnp.zeros((8, width), F32)
    first, second = lax.fori_loop(0, chunks, sums, (zero, zero))
    own_cot = jnp.where(
        lax.broadcasted_iota(jnp.int32, cot_ref.shape, 0) // own == dev_ref[1],
        cot_ref[...].astype(F32),
        0.0,
    )
    biases = jnp.concatenate(
        [
            jnp.sum(own_cot, 0, keepdims=True),
            jnp.sum(back.astype(F32), 0, keepdims=True),
            jnp.zeros((1, width - 256), F32),
        ],
        1,
    )
    packed = jnp.concatenate(
        [jnp.sum(first, 0, keepdims=True), jnp.sum(second, 0, keepdims=True), biases], 0
    )
    pay_ref[...] = jnp.broadcast_to(packed[None], pay_ref.shape)


def masks(mask_ref, c, p, width):
    kind = 0 if p in (0, 1, 3, 4) else 1
    return spread(mask_ref[kind, pl.ds(pl.multiple_of(c * CHUNK, CHUNK), CHUNK), :], width)


def spatial_kernel(
    pay_ref, pre_ref, w_ref, gain_ref, shift_ref, mask_ref, count_ref,
    hid_ref, out_ref, next_ref, stat_ref,
):
    chunks, chunk_rows, width = pre_ref.shape
    count = count_ref[0:1, 0:1]
    total, mean, inv = moments(pay_ref, count)
    scale = gain_ref[...] * inv
    base = shift_ref[...] - mean * scale
    stat_ref[...] = jnp.concatenate(
        [mean, inv, scale, base, total[2:3], jnp.zeros((3, width), F32)], 0
    )

    def act(c, _):
        for p in range(PIX):
            rows = slice(p * CHUNK, (p + 1) * CHUNK)
            a = pre_ref[c, rows, :] * scale + base
            hid_ref[c, rows, :] = (gelu(a) * masks(mask_ref, c, p, width)).astype(BF)
        return 0

    lax.fori_loop(0, chunks, act, 0)
    for k in OFFSETS:
        for first_out, first_in, n in spans(k):
            for s in range(0, n, 3):
                m = min(3, n - s)
                part = dot(places(hid_ref, first_in + s, m), w_ref[k])
                add_places(out_ref, first_out + s, m, part, k == OFFSETS[0])

    def sums(c, carry):
        first, second = carry
        for p in range(PIX):
            a = out_ref[c, p * CHUNK : (p + 1) * CHUNK, :]
            if p not in (0, 1, 3, 4):
                a = a * masks(mask_ref, c, p, width)
            first = first + jnp.sum(a.reshape(CHUNK // 8, 8, width), 0)
            second = second + jnp.sum((a * a).reshape(CHUNK // 8, 8, width), 0)
        return first, second

    zero = jnp.zeros((8, width), F32)
    first, second = lax.fori_loop(0, chunks, sums, (zero, zero))
    packed = jnp.concatenate(
        [jnp.sum(first, 0, keepdims=True), jnp.sum(second, 0, keepdims=True)], 0
    )
    next_ref[...] = jnp.broadcast_to(packed[None], next_ref.shape)


def expand_kernel(
    pay_ref, pre_ref, w_ref, gain_ref, shift_ref, mask_ref, count_ref,
    hid_ref, gram_ref, next_ref, stat_ref,
):
    chunks, chunk_rows, width = pre_ref.shape
    depth = w_ref.shape[1]
    count = count_ref[0:1, 0:1]
    _, mean, inv = moments(pay_ref, count)
    scale = gain_ref[...] * inv
    base = shift_ref[...] - mean * scale

    def act(c, column):
        for p in range(PIX):
            rows = slice(p * CHUNK, (p + 1) * CHUNK)
            a = pre_ref[c, rows, :] * scale + base
            h = (gelu(a) * masks(mask_ref, c, p, width)).astype(BF)
            hid_ref[c, rows, :] = h
            column = column + jnp.sum(h.astype(F32).reshape(CHUNK // 8, 8, width), 0)
        return column

    column = lax.fori_loop(0, chunks, act, jnp.zeros((8, width), F32))
    column = jnp.sum(column, 0, keepdims=True)
    stat_ref[...] = jnp.concatenate(
        [mean, inv, scale, base, column, jnp.zeros((3, width), F32)], 0
    )
    flat = hid_ref[...].reshape(chunks * chunk_rows, width)
    gram = dot(flat, flat, 0, 0)
    high = gram.astype(BF)
    low = (gram - high.astype(F32)).astype(BF)
    first = dot_rows(column, w_ref[...])
    block = 512
    for d in range(0, depth, block):
        w = w_ref[:, d : d + block]
        product = dot(high, w) + dot(low, w)
        gram_ref[:, d : d + block] = product.astype(BF)
        second = jnp.sum(product * w.astype(F32), 0, keepdims=True)
        packed = jnp.concatenate([first[:, d : d + block], second], 0)
        next_ref[:, :, d : d + block] = jnp.broadcast_to(
            packed[None], (next_ref.shape[0], 2, block)
        )


def output_kernel(
    pay_ref, hid_ref, xp_ref, w_ref, gain_ref, shift_ref, hw_ref, back_ref, mask_ref, count_ref,
    out_ref, dy_ref, up_ref, part_ref, emb_ref, head_ref, next_ref, stat_ref,
    pre, flat, obuf, sems, *, rows,
):
    chunks, chunk_rows, depth = xp_ref.shape
    width = hid_ref.shape[2]
    padded = chunks * CHUNK
    block = pre.shape[1]
    lanes = block // 128
    blocks = depth // block
    tail = rows - (chunks - 1) * chunk_rows
    count = count_ref[0:1, 0:1]

    def copy(d, slot):
        return pltpu.make_async_copy(
            obuf.at[slot], out_ref.at[:, pl.ds(pl.multiple_of(d * block, block), block)], sems.at[slot]
        )

    def step(d, _):
        slot = d % 2
        cols = pl.ds(pl.multiple_of(d * block, block), block)
        total = jnp.sum(pay_ref[:, :, cols], 0)
        mean = total[0:1] / count
        inv = lax.rsqrt(total[1:2] / count - mean * mean + EPS)
        scale = gain_ref[:, cols] * inv
        base = shift_ref[:, cols] - mean * scale
        stat_ref[:, cols] = jnp.concatenate([mean, inv, scale, base, jnp.zeros((4, block), F32)], 0)
        w = w_ref[:, cols]
        hw = hw_ref[cols, :]
        cells = spread(mask_ref[2], block)
        back_pool = dot(back_ref[...], hw, 1, 1) * cells
        back_large = back_pool * spread(mask_ref[1], block)
        scaled = (w.astype(F32) * scale).astype(BF)

        @pl.when(d >= 2)
        def _():
            copy(d - 2, slot).wait()

        pools = []
        first = jnp.zeros((SUB, block), F32)
        for c in range(chunks):
            pre[...] = dot(hid_ref[c], w)
            for s in range(0, CHUNK, SUB):
                pool = jnp.zeros((SUB, block), F32)
                bp_small = back_pool[c * CHUNK + s : c * CHUNK + s + SUB]
                bp_large = back_large[c * CHUNK + s : c * CHUNK + s + SUB]
                m_large = spread(mask_ref[1, c * CHUNK + s : c * CHUNK + s + SUB, :], block)
                for p in range(PIX):
                    at = p * CHUNK + s
                    v = pre[at : at + SUB, :] * scale + base + xp_ref[c, at : at + SUB, cols].astype(F32)
                    value, slope = gelu_both(v)
                    if p in (0, 1, 3, 4):
                        dy = slope * bp_small
                    else:
                        value = value * m_large
                        dy = slope * bp_large
                    pool = pool + value
                    first = first + dy
                    dy_ref[c, at : at + SUB, cols] = dy.astype(BF)
                    for lane in range(lanes):
                        flat[lane, pl.ds(s * PIX + p, SUB, stride=PIX), :] = value[
                            :, lane * 128 : (lane + 1) * 128
                        ]
                pools.append(pool)
            size = chunk_rows if c + 1 < chunks else tail
            for lane in range(lanes):
                obuf[
                    slot, c * chunk_rows : c * chunk_rows + size, lane * 128 : (lane + 1) * 128
                ] = flat[lane, 0:size, :].astype(BF)
        copy(d, slot).start()
        dy = dy_ref[:, :, cols].reshape(chunks * chunk_rows, block)
        up = dot(dy, scaled, 1, 1).reshape(up_ref.shape)
        part = dot(hid_ref[...].reshape(chunks * chunk_rows, width), dy, 0, 0)
        part_ref[:, cols] = part
        first = jnp.sum(first, 0, keepdims=True)
        second = inv * (jnp.sum(part * w.astype(F32), 0, keepdims=True) - mean * first)
        next_ref[:, :, cols] = jnp.broadcast_to(
            jnp.concatenate([second, first], 0)[None], (next_ref.shape[0], 2, block)
        )
        pooled = (jnp.concatenate(pools, 0) * cells).astype(BF)
        emb = dot(pooled, hw)
        head_ref[cols, :] = dot(pooled, back_ref[...], 0, 0).astype(BF)

        @pl.when(d == 0)
        def _():
            up_ref[...] = up
            emb_ref[...] = emb

        @pl.when(d > 0)
        def _():
            up_ref[...] = up_ref[...] + up
            emb_ref[...] = emb_ref[...] + emb

        return 0

    lax.fori_loop(0, blocks, step, 0)
    copy(blocks - 2, (blocks - 2) % 2).wait()
    copy(blocks - 1, (blocks - 1) % 2).wait()


def expand_back_kernel(
    pay_ref, stat_ref, gain_ref, up_ref, hid_ref, w_ref, part_ref, gram_ref, head_ref,
    pre_ref, stat2_ref, mask_ref, count_ref, emb_ref, hb_ref, pick_ref, jw_ref, cot_ref, dev_ref,
    grad_ref, dgain_ref, dshift_ref, dy_ref, next_ref, *, own, narrow,
):
    chunks, chunk_rows, width = pre_ref.shape
    depth = w_ref.shape[1]
    count = count_ref[0:1, 0:1]
    total = jnp.sum(pay_ref[...], 0)
    dgain, dshift = total[0:1], total[1:2]
    dgain_ref[...] = dgain
    dshift_ref[...] = dshift
    mean, inv, scale = stat_ref[0:1], stat_ref[1:2], stat_ref[2:3]
    slope = scale * inv * dgain / count
    level = scale * dshift / count - mean * slope
    cross = jnp.zeros((width, width), F32)
    column = jnp.reshape(stat2_ref[4:5], (1, width))
    tall = dot_rows_t(column, level)
    block = 512
    for i, d in enumerate(range(0, depth, block)):
        cols = slice(d, d + block)
        w = w_ref[:, cols]
        cross = cross + dot((w.astype(F32) * slope[:, cols]).astype(BF), w, 1, 1)
        grad = (
            part_ref[:, cols] * scale[:, cols]
            - tall[:, cols]
            - gram_ref[:, cols].astype(F32) * slope[:, cols]
        )
        grad_ref[i * width : (i + 1) * width, :] = grad.astype(BF)
    constant = dot_rows(level, w_ref[...], 1)
    cross = cross.astype(BF)
    mean2, inv2, scale2, base2 = (stat2_ref[i : i + 1] for i in range(4))

    def step(c, carry):
        first, second = carry
        fix = dot(hid_ref[c], cross)
        for p in range(PIX):
            rows = slice(p * CHUNK, (p + 1) * CHUNK)
            a = pre_ref[c, rows, :]
            g = up_ref[c, rows, :] - fix[rows] - constant
            dy = gelu_slope(a * scale2 + base2) * g * masks(mask_ref, c, p, width)
            dy_ref[c, rows, :] = dy
            first = first + jnp.sum(dy.reshape(CHUNK // 8, 8, width), 0)
            second = second + jnp.sum(
                (dy * ((a - mean2) * inv2)).reshape(CHUNK // 8, 8, width), 0
            )
        return first, second

    zero = jnp.zeros((8, width), F32)
    first, second = lax.fori_loop(0, chunks, step, (zero, zero))
    next_ref[...] = jnp.zeros(next_ref.shape, F32)
    packed = jnp.concatenate(
        [jnp.sum(second, 0, keepdims=True), jnp.sum(first, 0, keepdims=True)], 0
    )
    next_ref[:, 0:2, :] = jnp.broadcast_to(packed[None], (next_ref.shape[0], 2, width))
    at = depth // block * width
    quarter = head_ref.shape[0] // 4
    for i in range(4):
        grad_ref[at : at + quarter, i * 128 : (i + 1) * 128] = head_ref[
            i * quarter : (i + 1) * quarter, :
        ]
    at += quarter
    embedded = (emb_ref[...] + hb_ref[...]).astype(BF)
    images = cot_ref.shape[0]
    ordered = dot(pick_ref[...], embedded).astype(BF)
    scores = jnp.zeros((images, 128), F32)
    jig = []
    for k in range(PIX):
        mine = ordered[k * images : (k + 1) * images]
        scores = scores + dot(mine, jw_ref[k * 128 : (k + 1) * 128, :])
        jig.append(dot(mine, cot_ref[...], 0, 0))
    jig = jnp.concatenate(jig, 0).astype(BF)
    quarter = jig.shape[0] // 4
    for i in range(4):
        grad_ref[at : at + quarter, i * 128 : (i + 1) * 128] = jig[i * quarter : (i + 1) * quarter]
    at += quarter
    if at < grad_ref.shape[0]:
        grad_ref[at:, :] = jnp.zeros((grad_ref.shape[0] - at, width), BF)
    lines = own // 4
    for j in range(narrow):
        line = scores[j * own : (j + 1) * own]
        line = jnp.concatenate([line[i * lines : (i + 1) * lines] for i in range(4)], 1)
        next_ref[dev_ref[0] * narrow + j, 2 : 2 + lines, :] = line


def dot_rows_t(column, row):
    n = column.shape[1]
    m = row.shape[1]
    tall = jnp.transpose(jnp.broadcast_to(column, (8, n)))[:, 0:1]
    return tall * jnp.broadcast_to(row, (n, m))


def spatial_grad_kernel(
    pay_ref, stat_ref, pre_ref, dy_ref, hid_ref, mask_ref, count_ref,
    back_ref, grad_ref, tot_ref,
):
    chunks, chunk_rows, width = pre_ref.shape
    count = count_ref[0:1, 0:1]
    total = jnp.sum(pay_ref[...], 0)
    tot_ref[...] = total
    dgain, dshift = total[0:1], total[1:2]
    mean, inv, scale = stat_ref[0:1], stat_ref[1:2], stat_ref[2:3]
    slope = scale * inv * dgain / count
    level = scale * dshift / count - mean * slope

    def step(c, _):
        for p in range(PIX):
            rows = slice(p * CHUNK, (p + 1) * CHUNK)
            b = dy_ref[c, rows, :] * scale - level - pre_ref[c, rows, :] * slope
            back_ref[c, rows, :] = (b * masks(mask_ref, c, p, width)).astype(BF)
        return 0

    lax.fori_loop(0, chunks, step, 0)
    for k in range(PIX):
        grad = None
        for first_out, first_in, n in spans(k):
            part = dot(places(hid_ref, first_in, n), places(back_ref, first_out, n), 0, 0)
            grad = part if grad is None else grad + part
        grad_ref[k * width : (k + 1) * width, :] = grad.astype(BF)


def spatial_back_kernel(
    back_ref, w_ref, pre_ref, stat_ref, mask_ref,
    dy_ref, next_ref,
):
    chunks, chunk_rows, width = pre_ref.shape
    mean, inv, scale, base = (stat_ref[i : i + 1] for i in range(4))
    for k in OFFSETS:
        for first_out, first_in, n in spans(k):
            for s in range(0, n, 3):
                m = min(3, n - s)
                part = dot(places(back_ref, first_out + s, m), w_ref[k], 1, 1)
                add_places(dy_ref, first_in + s, m, part, k == OFFSETS[0])

    def step(c, carry):
        first, second = carry
        for p in range(PIX):
            rows = slice(p * CHUNK, (p + 1) * CHUNK)
            a = pre_ref[c, rows, :]
            dy = gelu_slope(a * scale + base) * dy_ref[c, rows, :] * masks(mask_ref, c, p, width)
            dy_ref[c, rows, :] = dy
            first = first + jnp.sum(dy.reshape(CHUNK // 8, 8, width), 0)
            second = second + jnp.sum((dy * ((a - mean) * inv)).reshape(CHUNK // 8, 8, width), 0)
        return first, second

    zero = jnp.zeros((8, width), F32)
    first, second = lax.fori_loop(0, chunks, step, (zero, zero))
    packed = jnp.concatenate(
        [jnp.sum(second, 0, keepdims=True), jnp.sum(first, 0, keepdims=True)], 0
    )
    next_ref[...] = jnp.broadcast_to(packed[None], next_ref.shape)


def reduce_back_kernel(
    pay_ref, stat_ref, pre_ref, dy_ref, xp_ref, w_ref, res_ref, mask_ref, count_ref,
    gin_ref, grad_ref, tot_ref,
    back, flat, obuf, sems, *, rows,
):
    chunks, chunk_rows, width = pre_ref.shape
    depth = xp_ref.shape[2]
    block = obuf.shape[2]
    lanes = block // 128
    blocks = depth // block
    tail = rows - (chunks - 1) * chunk_rows
    count = count_ref[0:1, 0:1]
    total = jnp.sum(pay_ref[...], 0)
    tot_ref[...] = total
    dgain, dshift = total[0:1], total[1:2]
    mean, inv, scale = stat_ref[0:1], stat_ref[1:2], stat_ref[2:3]
    slope = scale * inv * dgain / count
    level = scale * dshift / count - mean * slope

    def step(c, _):
        for p in range(PIX):
            at = slice(p * CHUNK, (p + 1) * CHUNK)
            b = dy_ref[c, at, :] * scale - level - pre_ref[c, at, :] * slope
            back[c, at, :] = (b * masks(mask_ref, c, p, width)).astype(BF)
        return 0

    lax.fori_loop(0, chunks, step, 0)
    flat_back = back[...].reshape(chunks * chunk_rows, width)

    def copy(d):
        return pltpu.make_async_copy(
            obuf.at[d % 2], gin_ref.at[:, pl.ds(d * block, block)], sems.at[d % 2]
        )

    for d in range(blocks):
        cols = slice(d * block, (d + 1) * block)
        grad_ref[cols, :] = dot(
            xp_ref[:, :, cols].reshape(chunks * chunk_rows, block), flat_back, 0, 0
        ).astype(BF)
        if d >= 2:
            copy(d - 2).wait()
        for c in range(chunks):
            part = dot(back[c], w_ref[cols, :], 1, 1)
            for p in range(PIX):
                at = slice(p * CHUNK, (p + 1) * CHUNK)
                value = part[at] + res_ref[c, at, cols].astype(F32)
                for lane in range(lanes):
                    flat[lane, pl.ds(p, CHUNK, stride=PIX), :] = value[
                        :, lane * 128 : (lane + 1) * 128
                    ]
            size = chunk_rows if c + 1 < chunks else tail
            for lane in range(lanes):
                obuf[
                    d % 2, c * chunk_rows : c * chunk_rows + size, lane * 128 : (lane + 1) * 128
                ] = flat[lane, 0:size, :].astype(BF)
        copy(d).start()
    copy(blocks - 2).wait()
    copy(blocks - 1).wait()


def shape(dims, dtype):
    return jax.ShapeDtypeStruct(dims, dtype)


def exchange(payload):
    return lax.all_to_all(payload, AXES, 0, 0)


def device_index():
    return lax.axis_index("wide") * lax.axis_size("narrow") + lax.axis_index("narrow")


def partner(value, bit):
    n = lax.axis_size("wide") * lax.axis_size("narrow")
    return lax.ppermute(value, AXES, [(i, i ^ bit) for i in range(n)])


def scatter_sum(value, order):
    me = device_index()
    for bit in order:
        half = value.shape[0] // 2
        side = (me // bit) % 2
        keep = lax.dynamic_slice_in_dim(value, side * half, half)
        send = lax.dynamic_slice_in_dim(value, (1 - side) * half, half)
        value = (keep.astype(F32) + partner(send, bit).astype(F32)).astype(BF)
    return value


def gather(value, order):
    me = device_index()
    for bit in reversed(order):
        other = partner(value, bit)
        low = (me // bit) % 2 == 0
        value = jnp.concatenate([jnp.where(low, value, other), jnp.where(low, other, value)])
    return value


def total_sum(value, order):
    return gather(scatter_sum(value, order), order)


def call(kernel, out_shape, in_specs, out_specs, scratch=(), limit=24, flops=0, bytes_accessed=0):
    return pl.pallas_call(
        kernel,
        out_shape=out_shape,
        in_specs=in_specs,
        out_specs=out_specs,
        scratch_shapes=list(scratch),
        compiler_params=pltpu.CompilerParams(vmem_limit_bytes=limit << 20),
        cost_estimate=pl.CostEstimate(
            flops=int(flops), bytes_accessed=int(bytes_accessed), transcendentals=0
        ),
    )


def body(
    block_in,
    weight_reduce,
    gain_reduce,
    shift_reduce,
    weight_spatial,
    gain_spatial,
    shift_spatial,
    weight_expand,
    gain_expand,
    shift_expand,
    head_weight,
    head_bias,
    jigsaw_weight,
    jigsaw_bias,
    resolution,
    tile_slot,
    jigsaw_perm,
    cotangent,
):
    rows, depth = block_in.shape
    width = weight_reduce.shape[1]
    tiles = rows // PIX
    chunks = -(-tiles // CHUNK)
    padded = chunks * CHUNK
    chunk_rows = CHUNK * PIX
    wide, narrow = lax.axis_size("wide"), lax.axis_size("narrow")
    n = wide * narrow
    images = jigsaw_perm.shape[0]
    own = images // narrow
    unit = 16 * n
    wide_rank, narrow_rank = lax.axis_index("wide"), lax.axis_index("narrow")
    slots = lax.dynamic_slice_in_dim(tile_slot, narrow_rank * tiles, tiles, 1)
    slots = jnp.pad(slots, ((0, 0), (0, padded - tiles)), constant_values=-1)
    dev = jnp.stack([wide_rank, narrow_rank]).astype(jnp.int32)
    row = lambda v: v.reshape(1, -1)
    block3 = lambda last, dtype: shape((chunks, chunk_rows, last), dtype)
    flops = 2 * padded * PIX * width * depth

    xp, pre_one, pay, mask, pick, back_emb, count = call(
        functools.partial(reduce_kernel, tiles=tiles, own=own),
        [
            block3(depth, BF),
            block3(width, F32),
            shape((n, 3, width), F32),
            shape((3, padded, 128), F32),
            shape((PIX * images, padded), BF),
            shape((padded, 128), BF),
            shape((8, 128), F32),
        ],
        [HBM, VMEM, VMEM, VMEM, VMEM, VMEM, VMEM, SMEM],
        [VMEM] * 7,
        [
            pltpu.VMEM((2, rows, 256), BF),
            pltpu.VMEM((2, chunk_rows, 128), F32),
            pltpu.SemaphoreType.DMA((2,)),
        ],
        flops=flops,
    )(block_in, weight_reduce, slots, row(resolution), jigsaw_perm, cotangent, jigsaw_weight, dev)

    w_spatial = weight_spatial.reshape(PIX, width, width)
    hid_one, pre_two, pay, stat_one = call(
        spatial_kernel,
        [block3(width, BF), block3(width, F32), shape((n, 2, width), F32), shape((8, width), F32)],
        [VMEM] * 7,
        [VMEM] * 4,
        flops=flops * 1.4,
    )(exchange(pay), pre_one, w_spatial, row(gain_reduce), row(shift_reduce), mask, count)

    hid_two, gram, pay, stat_two = call(
        expand_kernel,
        [
            block3(width, BF),
            shape((width, depth), BF),
            shape((n, 2, depth), F32),
            shape((8, width), F32),
        ],
        [VMEM] * 7,
        [VMEM] * 4,
        flops=flops,
    )(exchange(pay), pre_two, weight_expand, row(gain_spatial), row(shift_spatial), mask, count)

    block_out, dy_three, up, part, emb, head, pay, stat_three = call(
        functools.partial(output_kernel, rows=rows),
        [
            shape((rows, depth), BF),
            block3(depth, BF),
            block3(width, F32),
            shape((width, depth), F32),
            shape((padded, 128), F32),
            shape((depth, 128), BF),
            shape((n, 2, depth), F32),
            shape((8, depth), F32),
        ],
        [VMEM] * 10,
        [HBM] + [VMEM] * 7,
        [
            pltpu.VMEM((chunk_rows, 256), F32),
            pltpu.VMEM((2, chunk_rows, 128), F32),
            pltpu.VMEM((2, rows, 256), BF),
            pltpu.SemaphoreType.DMA((2,)),
        ],
        flops=flops * 4,
        limit=42,
    )(
        exchange(pay), hid_two, xp, weight_expand, row(gain_expand), row(shift_expand),
        head_weight, back_emb, mask, count,
    )

    used = width * depth // width + depth // 4 + PIX * 128 // 4
    grad_rows = -(-used // unit) * unit
    lines = own // 4
    grad_expand, gain_three, shift_three, dy_two, pay = call(
        functools.partial(expand_back_kernel, own=own, narrow=narrow),
        [
            shape((grad_rows, width), BF),
            shape((1, depth), F32),
            shape((1, depth), F32),
            block3(width, F32),
            shape((n, 2 + lines, width), F32),
        ],
        [VMEM] * 18 + [SMEM],
        [VMEM] * 5,
        flops=flops,
        limit=36,
    )(
        exchange(pay), stat_three, row(gain_expand), up, hid_two, weight_expand, part, gram, head,
        pre_two, stat_two, mask, count, emb, row(head_bias), pick, jigsaw_weight, cotangent, dev,
    )

    back_spatial, grad_spatial, total_two = call(
        spatial_grad_kernel,
        [block3(width, BF), shape((PIX * width, width), BF), shape((2 + lines, width), F32)],
        [VMEM] * 7,
        [VMEM] * 3,
        flops=flops * 1.6,
    )(exchange(pay), stat_two, pre_two, dy_two, hid_one, mask, count)

    dy_one, pay = call(
        spatial_back_kernel,
        [block3(width, F32), shape((n, 2, width), F32)],
        [VMEM] * 5,
        [VMEM] * 2,
        flops=flops * 1.4,
    )(back_spatial, w_spatial, pre_one, stat_one, mask)

    gradient_input, grad_reduce, total_one = call(
        functools.partial(reduce_back_kernel, rows=rows),
        [shape((rows, depth), BF), shape((depth, width), BF), shape((2, width), F32)],
        [VMEM] * 9,
        [HBM, VMEM, VMEM],
        [
            pltpu.VMEM((chunks, chunk_rows, width), BF),
            pltpu.VMEM((4, chunk_rows, 128), F32),
            pltpu.VMEM((2, rows, 512), BF),
            pltpu.SemaphoreType.DMA((2,)),
        ],
        flops=flops * 2,
        limit=42,
    )(exchange(pay), stat_one, pre_one, dy_one, xp, weight_reduce, dy_three, mask, count)

    bits = [1 << i for i in range(n.bit_length() - 1)]
    turn = lambda k: tuple(bits[:1] + bits[1 + k :] + bits[1 : 1 + k])
    sum_expand = total_sum(grad_expand, turn(0))
    third = grad_spatial.shape[0] // 3 // (n) * n
    if grad_spatial.shape[0] % n == 0 and third > 0:
        cuts = [0, third, 2 * third, grad_spatial.shape[0]]
    else:
        cuts = [0, grad_spatial.shape[0]]
    pieces = []
    for i in range(len(cuts) - 1):
        piece = grad_spatial[cuts[i] : cuts[i + 1]]
        size = piece.shape[0]
        whole = -(-size // n) * n
        piece = jnp.pad(piece, ((0, whole - size), (0, 0)))
        pieces.append(total_sum(piece, turn(i))[:size])
    sum_reduce = total_sum(grad_reduce, turn(0))

    at = depth
    gradient_expand = (
        sum_expand[:at].reshape(depth // width, width, width).transpose(1, 0, 2).reshape(width, depth)
    )
    unquarter = lambda v: v.reshape(-1, 4, 128).transpose(1, 0, 2).reshape(-1, 128)
    gradient_head = unquarter(sum_expand[at : at + depth // 4])
    at += depth // 4
    gradient_jigsaw = unquarter(sum_expand[at : at + PIX * 32])
    scores = total_two[2:].reshape(lines, 4, 128).transpose(1, 0, 2).reshape(own, 128) + jigsaw_bias
    biases = stat_one[4]
    return (
        block_out,
        scores,
        gradient_input,
        sum_reduce.astype(F32),
        total_one[0],
        total_one[1],
        jnp.concatenate(pieces).astype(F32),
        total_two[0],
        total_two[1],
        gradient_expand.astype(F32),
        gain_three[0],
        shift_three[0],
        gradient_head.astype(F32),
        biases[128:256],
        gradient_jigsaw.astype(F32),
        biases[0:128],
    )


def solution(mesh):
    placed = (P(AXES, None),) + (P(),) * 14 + (P("wide", None),) * 3
    return jax.shard_map(
        body,
        mesh=mesh,
        in_specs=placed,
        out_specs=(P(AXES, None),) * 3 + (P(),) * 13,
        check_vma=False,
    )
```

```python
import functools

import jax
import jax.numpy as jnp
from jax import lax
from jax.experimental import pallas as pl
from jax.experimental.pallas import tpu as pltpu
from jax.sharding import PartitionSpec as P

BF = jnp.bfloat16
F32 = jnp.float32
EPS = 1e-05
AXES = ("wide", "narrow")
PIX = 9
CHUNK = 48
SUB = 16
C1 = 0.7978845608028654
C2 = C1 * 0.044715
VMEM = pl.BlockSpec(memory_space=pltpu.VMEM)
HBM = pl.BlockSpec(memory_space=pltpu.HBM)
SMEM = pl.BlockSpec(memory_space=pltpu.SMEM)
ANY = pl.BlockSpec(memory_space=pl.ANY)


def dot(a, b, ca=1, cb=0):
    return lax.dot_general(a, b, (((ca,), (cb,)), ((), ())), preferred_element_type=F32)


def dot_rows(row, b, cb=0):
    high = row.astype(BF)
    rest = row - high.astype(F32)
    mid = rest.astype(BF)
    low = (rest - mid.astype(F32)).astype(BF)
    stack = jnp.concatenate([high, mid, low, jnp.zeros((13, row.shape[1]), BF)], 0)
    return jnp.sum(dot(stack, b, 1, cb), 0, keepdims=True)


def spread(mask, width):
    return jnp.concatenate([mask] * (width // 128), 1)


def gelu(v):
    squared = v * v
    half = 0.5 * v
    return half + half * jnp.tanh(v * (C1 + C2 * squared))


def gelu_both(v):
    squared = v * v
    gate = 0.5 * jnp.tanh(v * (C1 + C2 * squared)) + 0.5
    value = v * gate
    return value, gate + value * (1.0 - gate) * (2.0 * C1 + 6.0 * C2 * squared)


def gelu_slope(v):
    return gelu_both(v)[1]


def spans(offset):
    down, right = offset // 3 - 1, offset % 3 - 1
    rows = [r for r in range(3) if 0 <= r + down < 3]
    if right == 0:
        return [(rows[0] * 3, (rows[0] + down) * 3, 3 * len(rows))]
    start = max(0, -right)
    return [(r * 3 + start, (r + down) * 3 + start + right, 2) for r in rows]


OFFSETS = (4, 1, 7, 3, 5, 0, 2, 6, 8)


def places(ref, first, count):
    chunks, _, width = ref.shape
    return ref[:, first * CHUNK : (first + count) * CHUNK, :].reshape(
        chunks * count * CHUNK, width
    )


def add_places(ref, first, count, value, start):
    chunks, _, width = ref.shape
    rows = pl.ds(first * CHUNK, count * CHUNK)
    value = value.reshape(chunks, count * CHUNK, width)
    if start:
        ref[:, rows, :] = value
    else:
        ref[:, rows, :] = ref[:, rows, :] + value


def put(keep, send, side, start, value, lane=0):
    half = keep.shape[0]
    lanes = slice(lane, lane + value.shape[1])
    for i in range(2):
        low, high = max(start, i * half), min(start + value.shape[0], (i + 1) * half)
        if low < high:
            piece = value[low - start : high - start]
            rows = slice(low - i * half, high - i * half)

            @pl.when(side == i)
            def _():
                keep[rows, lanes] = piece

            @pl.when(side != i)
            def _():
                send[rows, lanes] = piece


def moments(payload, count):
    total = jnp.sum(payload[...], 0)
    mean = total[0:1] / count
    inv = lax.rsqrt(total[1:2] / count - mean * mean + EPS)
    return total, mean, inv


def reduce_kernel(
    x_ref, w_ref, slots_ref, res_ref, perm_ref, cot_ref, jw_ref, dev_ref,
    xp_ref, pre_ref, pay_ref, mask_ref, pick_ref, back_ref, count_ref,
    buf, wbuf, flat, sems, wsems, *, tiles, own,
):
    rows, depth = x_ref.shape
    chunks, chunk_rows, _ = xp_ref.shape
    padded = chunks * CHUNK
    block = buf.shape[2]
    blocks = depth // block
    lanes = block // 128

    def copy(d):
        return pltpu.make_async_copy(
            x_ref.at[:, pl.ds(d * block, block)], buf.at[d % 2], sems.at[d % 2]
        )

    def copy_w(d):
        return pltpu.make_async_copy(
            w_ref.at[pl.ds(d * block, block), :], wbuf.at[d % 2], wsems.at[d % 2]
        )

    for d in range(2):
        copy(d).start()
        copy_w(d).start()
    ids = slots_ref[...]
    image = lax.shift_right_arithmetic(ids * 7282, 16)
    piece = ids - 9 * image
    images = perm_ref.shape[1]
    here = jnp.where(image < 0, -1, image + dev_ref[0] * images)
    all_images = res_ref.shape[1]
    hit_all = lax.broadcasted_iota(jnp.int32, (all_images, padded), 0) == here
    res = res_ref[...].astype(F32)
    flags = dot(
        jnp.broadcast_to(res, (16, all_images)).astype(BF), jnp.where(hit_all, 1.0, 0.0).astype(BF)
    )[0:1]
    eye = lax.broadcasted_iota(jnp.int32, (padded, padded), 0) == lax.broadcasted_iota(
        jnp.int32, (padded, padded), 1
    )
    large = dot(jnp.where(eye, flags, 0.0).astype(BF), jnp.ones((padded, 128), BF))
    exists = lax.broadcasted_iota(jnp.int32, (padded, 128), 0) < tiles
    mask_ref[0] = jnp.where(exists, 1.0, 0.0)
    mask_ref[1] = large
    mask_ref[2] = 1.0 / (4.0 + 5.0 * large)
    total = 9.0 * (4.0 * all_images + 5.0 * jnp.sum(res, 1, keepdims=True))
    count_ref[...] = jnp.broadcast_to(total, (8, 128))
    hit = lax.broadcasted_iota(jnp.int32, (images, padded), 0) == image
    rows_back = dot(cot_ref[...], jw_ref[...], 1, 1).astype(BF)
    back = jnp.zeros((padded, 128), F32)
    small_eye = lax.broadcasted_iota(jnp.int32, (images, images), 0) == lax.broadcasted_iota(
        jnp.int32, (images, images), 1
    )
    perm = dot(jnp.where(small_eye, 1.0, 0.0).astype(BF), perm_ref[...].astype(F32).astype(BF), 1, 1)
    piece = piece.astype(F32)
    for k in range(PIX):
        chosen = jnp.where(hit & (perm[:, k : k + 1] == piece), 1.0, 0.0).astype(BF)
        pick_ref[k * images : (k + 1) * images, :] = chosen
        back = back + dot(chosen, rows_back[:, k * 128 : (k + 1) * 128], 0, 0)
    back = back.astype(BF)
    back_ref[...] = back
    tail = rows - (chunks - 1) * chunk_rows

    def product(d):
        part = dot(
            xp_ref[:, :, d * block : (d + 1) * block].reshape(chunks * chunk_rows, block),
            wbuf[d % 2],
        ).reshape(pre_ref.shape)
        pre_ref[...] = part if d == 0 else pre_ref[...] + part

    for d in range(blocks):
        copy(d).wait()
        if d > 0:
            copy_w(d - 1).wait()
            product(d - 1)
        cols = slice(d * block, (d + 1) * block)
        for c in range(chunks):
            size = chunk_rows if c + 1 < chunks else tail
            for lane in range(lanes):
                flat[c % 2, lane, 0:size, :] = buf[
                    d % 2, c * chunk_rows : c * chunk_rows + size, lane * 128 : (lane + 1) * 128
                ].astype(F32)
                if size < chunk_rows:
                    flat[c % 2, lane, size:, :] = jnp.zeros((chunk_rows - size, 128), F32)
            for p in range(PIX):
                xp_ref[c, p * CHUNK : (p + 1) * CHUNK, cols] = jnp.concatenate(
                    [flat[c % 2, lane, pl.ds(p, CHUNK, stride=PIX), :] for lane in range(lanes)], 1
                ).astype(BF)
        if d + 2 < blocks:
            copy(d + 2).start()
        if 0 < d < blocks - 1:
            copy_w(d + 1).start()
    copy_w(blocks - 1).wait()
    product(blocks - 1)
    width = pre_ref.shape[2]

    def sums(c, carry):
        first, second = carry
        for p in range(PIX):
            a = pre_ref[c, p * CHUNK : (p + 1) * CHUNK, :]
            if p not in (0, 1, 3, 4):
                m = spread(mask_ref[1, pl.ds(pl.multiple_of(c * CHUNK, CHUNK), CHUNK), :], width)
                a = a * m
            first = first + jnp.sum(a.reshape(CHUNK // 8, 8, width), 0)
            second = second + jnp.sum((a * a).reshape(CHUNK // 8, 8, width), 0)
        return first, second

    zero = jnp.zeros((8, width), F32)
    first, second = lax.fori_loop(0, chunks, sums, (zero, zero))
    own_cot = jnp.where(
        lax.broadcasted_iota(jnp.int32, cot_ref.shape, 0) // own == dev_ref[1],
        cot_ref[...].astype(F32),
        0.0,
    )
    biases = jnp.concatenate(
        [
            jnp.sum(own_cot, 0, keepdims=True),
            jnp.sum(back.astype(F32), 0, keepdims=True),
            jnp.zeros((1, width - 256), F32),
        ],
        1,
    )
    packed = jnp.concatenate(
        [jnp.sum(first, 0, keepdims=True), jnp.sum(second, 0, keepdims=True), biases], 0
    )
    pay_ref[...] = jnp.broadcast_to(packed[None], pay_ref.shape)


def masks(mask_ref, c, p, width):
    kind = 0 if p in (0, 1, 3, 4) else 1
    return spread(mask_ref[kind, pl.ds(pl.multiple_of(c * CHUNK, CHUNK), CHUNK), :], width)


def load_offsets(w_ref, wbuf, sems):
    loads = {k: pltpu.make_async_copy(w_ref.at[k], wbuf.at[k], sems.at[k]) for k in OFFSETS}
    for k in OFFSETS:
        loads[k].start()
    return loads


def spatial_kernel(
    pay_ref, pre_ref, w_ref, gain_ref, shift_ref, mask_ref, count_ref,
    hid_ref, out_ref, next_ref, stat_ref, wbuf, sems,
):
    chunks, chunk_rows, width = pre_ref.shape
    loads = load_offsets(w_ref, wbuf, sems)
    count = count_ref[0:1, 0:1]
    total, mean, inv = moments(pay_ref, count)
    scale = gain_ref[...] * inv
    base = shift_ref[...] - mean * scale
    stat_ref[...] = jnp.concatenate(
        [mean, inv, scale, base, total[2:3], jnp.zeros((3, width), F32)], 0
    )

    def act(c, _):
        for p in range(PIX):
            rows = slice(p * CHUNK, (p + 1) * CHUNK)
            a = pre_ref[c, rows, :] * scale + base
            hid_ref[c, rows, :] = (gelu(a) * masks(mask_ref, c, p, width)).astype(BF)
        return 0

    lax.fori_loop(0, chunks, act, 0)
    for k in OFFSETS:
        loads[k].wait()
        for first_out, first_in, n in spans(k):
            for s in range(0, n, 3):
                m = min(3, n - s)
                part = dot(places(hid_ref, first_in + s, m), wbuf[k])
                add_places(out_ref, first_out + s, m, part, k == OFFSETS[0])

    def sums(c, carry):
        first, second = carry
        for p in range(PIX):
            a = out_ref[c, p * CHUNK : (p + 1) * CHUNK, :]
            if p not in (0, 1, 3, 4):
                a = a * masks(mask_ref, c, p, width)
            first = first + jnp.sum(a.reshape(CHUNK // 8, 8, width), 0)
            second = second + jnp.sum((a * a).reshape(CHUNK // 8, 8, width), 0)
        return first, second

    zero = jnp.zeros((8, width), F32)
    first, second = lax.fori_loop(0, chunks, sums, (zero, zero))
    packed = jnp.concatenate(
        [jnp.sum(first, 0, keepdims=True), jnp.sum(second, 0, keepdims=True)], 0
    )
    next_ref[...] = jnp.broadcast_to(packed[None], next_ref.shape)


def expand_kernel(
    pay_ref, pre_ref, w_ref, gain_ref, shift_ref, mask_ref, count_ref,
    hid_ref, gram_ref, next_ref, stat_ref,
):
    chunks, chunk_rows, width = pre_ref.shape
    depth = w_ref.shape[1]
    count = count_ref[0:1, 0:1]
    _, mean, inv = moments(pay_ref, count)
    scale = gain_ref[...] * inv
    base = shift_ref[...] - mean * scale

    def act(c, column):
        for p in range(PIX):
            rows = slice(p * CHUNK, (p + 1) * CHUNK)
            a = pre_ref[c, rows, :] * scale + base
            h = (gelu(a) * masks(mask_ref, c, p, width)).astype(BF)
            hid_ref[c, rows, :] = h
            column = column + jnp.sum(h.astype(F32).reshape(CHUNK // 8, 8, width), 0)
        return column

    column = lax.fori_loop(0, chunks, act, jnp.zeros((8, width), F32))
    column = jnp.sum(column, 0, keepdims=True)
    stat_ref[...] = jnp.concatenate(
        [mean, inv, scale, base, column, jnp.zeros((3, width), F32)], 0
    )
    flat = hid_ref[...].reshape(chunks * chunk_rows, width)
    gram = dot(flat, flat, 0, 0)
    high = gram.astype(BF)
    low = (gram - high.astype(F32)).astype(BF)
    block = width
    packed = [column]
    for d in range(0, depth, block):
        w = w_ref[:, d : d + block]
        product = dot(high, w) + dot(low, w)
        gram_ref[:, d : d + block] = product.astype(BF)
        second = jnp.sum(product * w.astype(F32), 0, keepdims=True)
        packed.append(second)
    packed = jnp.concatenate(packed, 1)
    half = packed.shape[1] // 2
    packed = jnp.concatenate([packed[:, :half], packed[:, half:]], 0)
    next_ref[...] = jnp.broadcast_to(packed[None], next_ref.shape)


def output_kernel(
    pay_ref, hid_ref, xp_ref, w_ref, gain_ref, shift_ref, hw_ref, back_ref, mask_ref, count_ref,
    out_ref, dy_ref, up_ref, part_ref, emb_ref, head_ref, next_ref, stat_ref,
    pre, flat, obuf, dy_even, dy_odd, pool_ref, first_ref, sems, *, rows,
):
    chunks, chunk_rows, depth = xp_ref.shape
    width = hid_ref.shape[2]
    block = pre.shape[2]
    lanes = block // 128
    blocks = depth // block
    tail = rows - (chunks - 1) * chunk_rows
    count = count_ref[0:1, 0:1]

    def copy(d, slot):
        return pltpu.make_async_copy(
            obuf.at[slot], out_ref.at[:, pl.ds(pl.multiple_of(d * block, block), block)], sems.at[slot]
        )

    total = jnp.sum(pay_ref[...], 0)
    total = jnp.concatenate([total[0:1], total[1:2]], 1)
    mean_all = dot_rows(total[:, :width], w_ref[...]) / count
    square_all = total[:, width:] / count
    inv_all = lax.rsqrt(square_all - mean_all * mean_all + EPS)
    scale_all = gain_ref[...] * inv_all
    stat_ref[...] = jnp.concatenate(
        [
            mean_all,
            inv_all,
            scale_all,
            shift_ref[...] - mean_all * scale_all,
            jnp.zeros((4, depth), F32),
        ],
        0,
    )
    dy_bufs = (dy_even, dy_odd)
    up_ref[...] = jnp.zeros(up_ref.shape, F32)
    emb_ref[...] = jnp.zeros(emb_ref.shape, F32)
    cells = spread(mask_ref[2], block)

    def columns(d):
        return pl.ds(pl.multiple_of(d * block, block), block)

    def forward(d, slot):
        dy_buf = dy_bufs[slot]
        cols = columns(d)
        scale = stat_ref[2:3, cols]
        base = stat_ref[3:4, cols]
        w = w_ref[:, cols]
        back_pool = dot(back_ref[...], hw_ref[cols, :], 1, 1) * cells
        back_large = back_pool * spread(mask_ref[1], block)
        pools = []
        first = jnp.zeros((SUB, block), F32)
        for c in range(chunks):
            pre[c % 2] = dot(hid_ref[c], w)
            for s in range(0, CHUNK, SUB):
                pool = jnp.zeros((SUB, block), F32)
                bp_small = back_pool[c * CHUNK + s : c * CHUNK + s + SUB]
                bp_large = back_large[c * CHUNK + s : c * CHUNK + s + SUB]
                m_large = spread(mask_ref[1, c * CHUNK + s : c * CHUNK + s + SUB, :], block)
                for p in range(PIX):
                    at = p * CHUNK + s
                    v = (
                        pre[c % 2, at : at + SUB, :] * scale
                        + base
                        + xp_ref[c, at : at + SUB, cols].astype(F32)
                    )
                    value, slope = gelu_both(v)
                    if p in (0, 1, 3, 4):
                        dy = slope * bp_small
                    else:
                        value = value * m_large
                        dy = slope * bp_large
                    pool = pool + value
                    first = first + dy
                    dy = dy.astype(BF)
                    dy_ref[c, at : at + SUB, cols] = dy
                    dy_buf[c, at : at + SUB, :] = dy
                    for lane in range(lanes):
                        flat[c % 2, lane, pl.ds(s * PIX + p, SUB, stride=PIX), :] = value[
                            :, lane * 128 : (lane + 1) * 128
                        ]
                pools.append(pool)
            size = chunk_rows if c + 1 < chunks else tail
            for lane in range(lanes):
                obuf[
                    slot, c * chunk_rows : c * chunk_rows + size, lane * 128 : (lane + 1) * 128
                ] = flat[c % 2, lane, 0:size, :].astype(BF)
        pool_ref[slot] = (jnp.concatenate(pools, 0) * cells).astype(BF)
        first_ref[slot] = first

    def backward(d, slot):
        dy_buf = dy_bufs[slot]
        cols = columns(d)
        w = w_ref[:, cols].astype(F32)
        scaled = (w * stat_ref[2:3, cols]).astype(BF)
        for c in range(chunks):
            up_ref[c] = up_ref[c] + dot(dy_buf[c], scaled, 1, 1)
        dy = dy_buf[...].reshape(chunks * chunk_rows, block)
        part = dot(hid_ref[...].reshape(chunks * chunk_rows, width), dy, 0, 0)
        part_ref[:, cols] = part
        first = jnp.sum(first_ref[slot], 0, keepdims=True)
        second = stat_ref[1:2, cols] * (
            jnp.sum(part * w, 0, keepdims=True) - stat_ref[0:1, cols] * first
        )
        next_ref[:, :, cols] = jnp.broadcast_to(
            jnp.concatenate([second, first], 0).astype(BF)[None], (next_ref.shape[0], 2, block)
        )
        pooled = pool_ref[slot]
        emb_ref[...] = emb_ref[...] + dot(pooled, hw_ref[cols, :])
        head_ref[cols, :] = dot(pooled, back_ref[...], 0, 0).astype(BF)

    def pair(i, _):
        for slot in range(2):
            d = 2 * i + slot
            copy(d - 2, slot).wait()
            backward(d - 1, 1 - slot)
            forward(d, slot)
            copy(d, slot).start()
        return 0

    forward(0, 0)
    copy(0, 0).start()
    backward(0, 0)
    forward(1, 1)
    copy(1, 1).start()
    lax.fori_loop(1, blocks // 2, pair, 0)
    backward(blocks - 1, 1)
    copy(blocks - 2, 0).wait()
    copy(blocks - 1, 1).wait()


def backward_terms(pay_ref, stat_ref, count):
    total = jnp.sum(pay_ref[...].astype(F32), 0)
    dgain, dshift = total[0:1], total[1:2]
    mean, inv, scale = stat_ref[0:1], stat_ref[1:2], stat_ref[2:3]
    slope = scale * inv * dgain / count
    level = scale * dshift / count - mean * slope
    return total, scale, slope, level


def expand_back_kernel(
    pay_ref, stat_ref, up_ref, hid_ref, w_ref,
    pre_ref, stat2_ref, mask_ref, count_ref, emb_ref, hb_ref, pick_ref, jw_ref, cot_ref,
    total_ref, term_ref, jig_ref, score_ref, dy_ref, next_ref,
):
    chunks, chunk_rows, width = pre_ref.shape
    depth = w_ref.shape[1]
    count = count_ref[0:1, 0:1]
    total, scale, slope, level = backward_terms(pay_ref, stat_ref, count)
    total_ref[...] = total
    term_ref[...] = jnp.concatenate([scale, slope, level, jnp.zeros((5, depth), F32)], 0)
    cross = jnp.zeros((width, width), F32)
    block = 512
    for d in range(0, depth, block):
        cols = slice(d, d + block)
        w = w_ref[:, cols]
        cross = cross + dot((w.astype(F32) * slope[:, cols]).astype(BF), w, 1, 1)
    constant = dot_rows(level, w_ref[...], 1)
    cross = cross.astype(BF)
    mean2, inv2, scale2, base2 = (stat2_ref[i : i + 1] for i in range(4))

    def step(c, carry):
        first, second = carry
        fix = dot(hid_ref[c], cross)
        for p in range(PIX):
            rows = slice(p * CHUNK, (p + 1) * CHUNK)
            a = pre_ref[c, rows, :]
            g = up_ref[c, rows, :] - fix[rows] - constant
            dy = gelu_slope(a * scale2 + base2) * g * masks(mask_ref, c, p, width)
            dy_ref[c, rows, :] = dy
            first = first + jnp.sum(dy.reshape(CHUNK // 8, 8, width), 0)
            second = second + jnp.sum(
                (dy * ((a - mean2) * inv2)).reshape(CHUNK // 8, 8, width), 0
            )
        return first, second

    zero = jnp.zeros((8, width), F32)
    first, second = lax.fori_loop(0, chunks, step, (zero, zero))
    packed = jnp.concatenate(
        [jnp.sum(second, 0, keepdims=True), jnp.sum(first, 0, keepdims=True)], 0
    )
    embedded = (emb_ref[...] + hb_ref[...]).astype(BF)
    images = cot_ref.shape[0]
    ordered = dot(pick_ref[...], embedded).astype(BF)
    scores = jnp.zeros((images, 128), F32)
    for k in range(PIX):
        mine = ordered[k * images : (k + 1) * images]
        scores = scores + dot(mine, jw_ref[k * 128 : (k + 1) * 128, :])
        jig_ref[k * 128 : (k + 1) * 128, :] = dot(mine, cot_ref[...], 0, 0).astype(BF)
    lines = images // 4
    score_ref[...] = jnp.concatenate([scores[i * lines : (i + 1) * lines] for i in range(4)], 1)
    next_ref[...] = jnp.broadcast_to(packed[None], next_ref.shape)


def expand_grad_kernel(
    term_ref, stat2_ref, part_ref, gram_ref, head_ref, jig_ref, score_ref, dev_ref,
    keep_ref, send_ref, *, wide,
):
    width, depth = part_ref.shape
    put_rows = functools.partial(put, keep_ref, send_ref, dev_ref[2])
    scale, slope, level = (term_ref[i : i + 1] for i in range(3))
    tall = dot_rows_t(stat2_ref[4:5], level)
    block = 512
    at = 0
    for d in range(0, depth, block):
        cols = slice(d, d + block)
        grad = (
            part_ref[:, cols] * scale[:, cols]
            - tall[:, cols]
            - gram_ref[:, cols].astype(F32) * slope[:, cols]
        )
        put_rows(at, grad.astype(BF))
        at += width
    for ref in (head_ref, jig_ref):
        quarter = ref.shape[0] // 4
        for i in range(4):
            put_rows(at, ref[i * quarter : (i + 1) * quarter, :], i * 128)
        at += quarter
    scores = score_ref[...]
    scores = [jnp.where(dev_ref[0] == g, scores, 0.0) for g in range(wide)]
    left = 2 * keep_ref.shape[0] - at - wide * score_ref.shape[0]
    if left > 0:
        scores.append(jnp.zeros((left, width), F32))
    put_rows(at, jnp.concatenate(scores, 0).astype(BF))


def dot_rows_t(column, row):
    n = column.shape[1]
    m = row.shape[1]
    tall = jnp.transpose(jnp.broadcast_to(column, (8, n)))[:, 0:1]
    return tall * jnp.broadcast_to(row, (n, m))


def spatial_grad_kernel(
    pay_ref, stat_ref, pre_ref, dy_ref, hid_ref, mask_ref, count_ref,
    dev_ref, back_ref, keep_ref, send_ref, tot_ref,
):
    chunks, chunk_rows, width = pre_ref.shape
    count = count_ref[0:1, 0:1]
    total, scale, slope, level = backward_terms(pay_ref, stat_ref, count)
    tot_ref[...] = total

    def step(c, _):
        for p in range(PIX):
            rows = slice(p * CHUNK, (p + 1) * CHUNK)
            b = dy_ref[c, rows, :] * scale - level - pre_ref[c, rows, :] * slope
            back_ref[c, rows, :] = (b * masks(mask_ref, c, p, width)).astype(BF)
        return 0

    lax.fori_loop(0, chunks, step, 0)
    for k in range(PIX):
        runs = spans(k)
        grad = dot(
            jnp.concatenate([places(hid_ref, first_in, n) for _, first_in, n in runs], 0),
            jnp.concatenate([places(back_ref, first_out, n) for first_out, _, n in runs], 0),
            0,
            0,
        )
        put(keep_ref, send_ref, dev_ref[2], k * width, grad.astype(BF))
    left = 2 * keep_ref.shape[0] - PIX * width
    if left > 0:
        put(keep_ref, send_ref, dev_ref[2], PIX * width, jnp.zeros((left, width), BF))


def spatial_back_kernel(
    back_ref, w_ref, pre_ref, stat_ref, mask_ref,
    dy_ref, next_ref,
):
    chunks, chunk_rows, width = pre_ref.shape
    mean, inv, scale, base = (stat_ref[i : i + 1] for i in range(4))
    for k in OFFSETS:
        for first_out, first_in, n in spans(k):
            for s in range(0, n, 3):
                m = min(3, n - s)
                part = dot(places(back_ref, first_out + s, m), w_ref[k], 1, 1)
                add_places(dy_ref, first_in + s, m, part, k == OFFSETS[0])

    def step(c, carry):
        first, second = carry
        for p in range(PIX):
            rows = slice(p * CHUNK, (p + 1) * CHUNK)
            a = pre_ref[c, rows, :]
            dy = gelu_slope(a * scale + base) * dy_ref[c, rows, :] * masks(mask_ref, c, p, width)
            dy_ref[c, rows, :] = dy
            first = first + jnp.sum(dy.reshape(CHUNK // 8, 8, width), 0)
            second = second + jnp.sum((dy * ((a - mean) * inv)).reshape(CHUNK // 8, 8, width), 0)
        return first, second

    zero = jnp.zeros((8, width), F32)
    first, second = lax.fori_loop(0, chunks, step, (zero, zero))
    packed = jnp.concatenate(
        [jnp.sum(second, 0, keepdims=True), jnp.sum(first, 0, keepdims=True)], 0
    )
    next_ref[...] = packed


def payload_kernel(packed_ref, next_ref):
    next_ref[...] = jnp.broadcast_to(packed_ref[...][None], next_ref.shape)


def reduce_grad_kernel(
    pay_ref, stat_ref, pre_ref, dy_ref, xp_ref, mask_ref, count_ref, dev_ref,
    back_ref, keep_ref, send_ref, tot_ref,
):
    chunks, chunk_rows, width = pre_ref.shape
    depth = xp_ref.shape[2]
    count = count_ref[0:1, 0:1]
    total, scale, slope, level = backward_terms(pay_ref, stat_ref, count)
    tot_ref[...] = total

    def step(c, _):
        for p in range(PIX):
            at = slice(p * CHUNK, (p + 1) * CHUNK)
            b = dy_ref[c, at, :] * scale - level - pre_ref[c, at, :] * slope
            back_ref[c, at, :] = (b * masks(mask_ref, c, p, width)).astype(BF)
        return 0

    lax.fori_loop(0, chunks, step, 0)
    flat_back = back_ref[...].reshape(chunks * chunk_rows, width)
    block = 512
    for d in range(0, depth, block):
        grad = dot(
            xp_ref[:, :, d : d + block].reshape(chunks * chunk_rows, block), flat_back, 0, 0
        )
        put(keep_ref, send_ref, dev_ref[2], d, grad.astype(BF))


def input_kernel(back_ref, w_ref, res_ref, gin_ref, flat, obuf, sems, *, rows):
    chunks, chunk_rows, width = back_ref.shape
    depth = w_ref.shape[0]
    block = obuf.shape[2]
    lanes = block // 128
    blocks = depth // block
    tail = rows - (chunks - 1) * chunk_rows

    def copy(d):
        return pltpu.make_async_copy(
            obuf.at[d % 2], gin_ref.at[:, pl.ds(d * block, block)], sems.at[d % 2]
        )

    for d in range(blocks):
        cols = slice(d * block, (d + 1) * block)
        if d >= 2:
            copy(d - 2).wait()
        for c in range(chunks):
            part = dot(back_ref[c], w_ref[cols, :], 1, 1)
            for p in range(PIX):
                at = slice(p * CHUNK, (p + 1) * CHUNK)
                value = part[at] + res_ref[c, at, cols].astype(F32)
                for lane in range(lanes):
                    flat[c % 2, lane, pl.ds(p, CHUNK, stride=PIX), :] = value[
                        :, lane * 128 : (lane + 1) * 128
                    ]
            size = chunk_rows if c + 1 < chunks else tail
            for lane in range(lanes):
                obuf[
                    d % 2, c * chunk_rows : c * chunk_rows + size, lane * 128 : (lane + 1) * 128
                ] = flat[c % 2, lane, 0:size, :].astype(BF)
        copy(d).start()
    copy(blocks - 2).wait()
    copy(blocks - 1).wait()


def writer(stage, sems):
    pending = []
    slots = stage.shape[0]

    def write(value, target):
        slot = len(pending) % slots
        if len(pending) >= slots:
            pending[-slots].wait()
        part = stage.at[slot, pl.ds(0, value.shape[0]), pl.ds(0, value.shape[1])]
        part[...] = value
        copy = pltpu.make_async_copy(part, target, sems.at[slot])
        copy.start()
        pending.append(copy)

    def finish():
        for copy in pending[-slots:]:
            copy.wait()

    return write, finish


def unpack_plain_kernel(mine_ref, other_ref, dev_ref, out_ref, stage, sems):
    half = mine_ref.shape[0]
    write, finish = writer(stage, sems)
    step = half // 4
    for ref, side in ((mine_ref, dev_ref[2]), (other_ref, 1 - dev_ref[2])):
        for r in range(0, half, step):
            start = pl.multiple_of(side * half + r, 16)
            write(ref[r : r + step, :].astype(F32), out_ref.at[pl.ds(start, step), :])
    finish()


def unpack_plain(call, item, numbers, after=()):
    half, width = item.keep.shape
    return call(
        unpack_plain_kernel,
        shape((2 * half, width), F32),
        [VMEM, VMEM, SMEM],
        HBM,
        [pltpu.VMEM((4, half // 4, width), F32), pltpu.SemaphoreType.DMA((4,))],
        limit=8,
        after=after,
    )(item.keep, item.got, numbers)


def unpack_kernel(
    mine_ref, other_ref, dev_ref, expand_ref, head_ref, jig_ref, score_ref, rest, stage, sems,
    *, wide,
):
    half, width = mine_ref.shape
    write, finish = writer(stage, sems)
    for ref, side in ((mine_ref, dev_ref[2]), (other_ref, 1 - dev_ref[2])):
        rest[pl.ds(pl.multiple_of(side * half, 16), half), :] = ref[...]
    depth = expand_ref.shape[1]
    for i in range(depth // width):
        for r in range(0, width, 256):
            write(
                rest[i * width + r : i * width + r + 256, :].astype(F32),
                expand_ref.at[pl.ds(r, 256), pl.ds(i * width, width)],
            )
    at = depth
    quarter = depth // 4
    for i in range(4):
        for r in range(0, quarter, 256):
            write(
                rest[at + r : at + r + 256, i * 128 : (i + 1) * 128].astype(F32),
                head_ref.at[pl.ds(i * quarter + r, 256), :],
            )
    at += quarter
    quarter = jig_ref.shape[0] // 4
    for i in range(4):
        write(
            rest[at : at + quarter, i * 128 : (i + 1) * 128].astype(F32),
            jig_ref.at[pl.ds(i * quarter, quarter), :],
        )
    at += quarter
    lines = score_ref.shape[0]
    total = jnp.zeros(score_ref.shape, F32)
    for g in range(wide):
        total = total + jnp.where(
            dev_ref[0] == g, rest[at + g * lines : at + (g + 1) * lines, :].astype(F32), 0.0
        )
    score_ref[...] = total
    finish()


def shape(dims, dtype):
    return jax.ShapeDtypeStruct(dims, dtype)


def held(dims, dtype):
    return pltpu.VMEM(dims, dtype)


def exchange(payload):
    return lax.all_to_all(payload, AXES, 0, 0)


def device_index():
    return lax.axis_index("wide") * lax.axis_size("narrow") + lax.axis_index("narrow")


def swap(value, bits):
    n = lax.axis_size("wide") * lax.axis_size("narrow")
    return lax.ppermute(value, AXES, [(i, i ^ bits[i % 2]) for i in range(n)])


def side_of(bits):
    me = device_index()
    return (me // jnp.where(me % 2 == 1, bits[1], bits[0])) % 2


def halves(ref, side):
    half = ref.shape[0] // 2
    return ref[pl.ds(pl.multiple_of(side * half, 8), half), :]


def merge_kernel(*refs, plan):
    dev_ref = refs[0]
    inputs = iter(refs[1 : 1 + sum(1 + (kind != "pass") for kind, _ in plan)])
    outputs = iter(refs[1 + sum(1 + (kind != "pass") for kind, _ in plan) :])
    for kind, index in plan:
        mine = next(inputs)
        if kind == "pass":
            target = next(outputs)
            target[...] = mine[...]
            continue
        got = next(inputs)
        if kind == "split":
            side = dev_ref[index]
            keep, send = next(outputs), next(outputs)
            keep[...] = halves(mine, side).astype(F32) + halves(got, side).astype(F32)
            send[...] = (
                halves(mine, 1 - side).astype(F32) + halves(got, 1 - side).astype(F32)
            ).astype(BF)
        elif kind == "sum":
            target = next(outputs)
            target[...] = (mine[...].astype(F32) + got[...].astype(F32)).astype(BF)
        else:
            side = dev_ref[index]
            target = next(outputs)
            half = mine.shape[0]
            target[pl.ds(pl.multiple_of(side * half, 16), half), :] = mine[...]
            target[pl.ds(pl.multiple_of((1 - side) * half, 16), half), :] = got[...]


class Sum:
    def __init__(self, keep, send, pairs, first_side):
        self.keep, self.send, self.pairs, self.sides = keep, send, pairs, first_side
        self.at = 0
        self.got = None
        self.gathering = False

    def exchange(self):
        self.got = swap(self.send, self.pairs[self.at])
        return self.got

    def last(self):
        return self.gathering and self.at == 0

    def kind(self):
        if self.gathering:
            return "join", self.sides + self.at
        if self.at + 1 < len(self.pairs):
            return "split", self.sides + self.at + 1
        return "sum", 0

    def shapes(self):
        rows, width = self.got.shape
        kind = self.kind()[0]
        if kind == "split":
            return [shape((rows // 2, width), F32), shape((rows // 2, width), BF)]
        if kind == "sum":
            return [shape((rows, width), BF)]
        return [shape((2 * rows, width), BF)]

    def take(self, results):
        kind = self.kind()[0]
        if kind == "split":
            self.keep, self.send = results
            self.at += 1
        else:
            self.keep = self.send = results[0]
            if kind == "sum":
                self.gathering = True
            else:
                self.at -= 1


def merge(call, numbers, sums, after=()):
    shapes = [item.shapes() for item in sums]
    outs = call(
        functools.partial(merge_kernel, plan=tuple(item.kind() for item in sums)),
        [one for each in shapes for one in each],
        [SMEM] + [VMEM, VMEM] * len(sums),
        [VMEM] * sum(map(len, shapes)),
        after=after,
    )(numbers, *(value for item in sums for value in (item.keep, item.got)))
    outs = list(outs)
    for item, each in zip(sums, shapes):
        item.take(outs[: len(each)])
        outs = outs[len(each) :]


def is_in(value, values):
    return any(value is v for v in values)


def kernel_call(
    kernel, out_shape, in_specs, out_specs, scratch=(), limit=6, flops=0, bytes_accessed=0,
    after=(), resident=(), far=(),
):
    n_in, n_after = len(in_specs), len(after)
    spare = max(0, lax.axis_size("wide") * lax.axis_size("narrow") // 16 - 2)

    def run(*refs):
        kernel(*refs[:n_in], *refs[n_in + n_after :])

    made = pl.pallas_call(
        run,
        out_shape=out_shape,
        in_specs=list(in_specs) + [HBM if is_in(a, far) else ANY for a in after],
        out_specs=out_specs,
        scratch_shapes=list(scratch),
        compiler_params=pltpu.CompilerParams(vmem_limit_bytes=(limit + spare) << 20),
        cost_estimate=pl.CostEstimate(
            flops=int(flops), bytes_accessed=int(bytes_accessed), transcendentals=0
        ),
    )

    def placed(*args):
        fixed = []
        for a, spec in zip(args, in_specs):
            if spec is HBM:
                a = pltpu.with_memory_space_constraint(a, pltpu.HBM)
            elif spec is VMEM and is_in(a, resident):
                a = pltpu.with_memory_space_constraint(a, pltpu.VMEM)
            fixed.append(a)
        for a in after:
            fixed.append(pltpu.with_memory_space_constraint(a, pltpu.HBM) if is_in(a, far) else a)
        outs = made(*fixed)
        if isinstance(out_shape, list):
            for made_shape, spec, out in zip(out_shape, out_specs, outs):
                if not isinstance(made_shape, jax.ShapeDtypeStruct):
                    resident.append(out)
                if spec is HBM:
                    far.append(out)
        elif out_specs is HBM:
            far.append(outs)
        return outs

    return placed


def body(
    block_in,
    weight_reduce,
    gain_reduce,
    shift_reduce,
    weight_spatial,
    gain_spatial,
    shift_spatial,
    weight_expand,
    gain_expand,
    shift_expand,
    head_weight,
    head_bias,
    jigsaw_weight,
    jigsaw_bias,
    resolution,
    tile_slot,
    jigsaw_perm,
    cotangent,
):
    rows, depth = block_in.shape
    width = weight_reduce.shape[1]
    tiles = rows // PIX
    chunks = -(-tiles // CHUNK)
    padded = chunks * CHUNK
    chunk_rows = CHUNK * PIX
    wide, narrow = lax.axis_size("wide"), lax.axis_size("narrow")
    n = wide * narrow
    images = jigsaw_perm.shape[0]
    own = images // narrow
    unit = 16 * n
    wide_rank, narrow_rank = lax.axis_index("wide"), lax.axis_index("narrow")
    slots = lax.dynamic_slice_in_dim(tile_slot, narrow_rank * tiles, tiles, 1)
    slots = jnp.pad(slots, ((0, 0), (0, padded - tiles)), constant_values=-1)
    bits = [1 << i for i in range(n.bit_length() - 1)]
    even = bits[:1] + bits[2:4] + bits[1:2] + bits[4:]
    odd = bits[:2] + bits[4:] + bits[2:4]
    pairs = list(zip(even, odd))
    first_side = 2
    dev = jnp.stack(
        [wide_rank, narrow_rank] + [side_of(b) for b in pairs]
    ).astype(jnp.int32)
    row = lambda v: v.reshape(1, -1)
    block3 = lambda last, dtype: held((chunks, chunk_rows, last), dtype)
    call = functools.partial(kernel_call, resident=[], far=[])
    flops = 2 * padded * PIX * width * depth

    xp, pre_one, pay, mask, pick, back_emb, count = call(
        functools.partial(reduce_kernel, tiles=tiles, own=own),
        [
            block3(depth, BF),
            block3(width, F32),
            shape((n, 3, width), F32),
            held((3, padded, 128), F32),
            held((PIX * images, padded), BF),
            held((padded, 128), BF),
            held((8, 128), F32),
        ],
        [HBM, HBM, VMEM, VMEM, VMEM, VMEM, VMEM, SMEM],
        [VMEM] * 7,
        [
            pltpu.VMEM((2, rows, 512), BF),
            pltpu.VMEM((2, 512, width), BF),
            pltpu.VMEM((2, 4, chunk_rows, 128), F32),
            pltpu.SemaphoreType.DMA((2,)),
            pltpu.SemaphoreType.DMA((2,)),
        ],
        limit=12,
        flops=flops,
    )(block_in, weight_reduce, slots, row(resolution), jigsaw_perm.T, cotangent, jigsaw_weight, dev)

    offset_scratch = [pltpu.VMEM((PIX, width, width), BF), pltpu.SemaphoreType.DMA((PIX,))]
    w_spatial = weight_spatial.reshape(PIX, width, width)
    hid_one, pre_two, pay, stat_one = call(
        spatial_kernel,
        [block3(width, BF), block3(width, F32), shape((n, 2, width), F32), held((8, width), F32)],
        [VMEM, VMEM, HBM] + [VMEM] * 4,
        [VMEM] * 4,
        offset_scratch,
        flops=flops * 1.4,
        limit=12,
    )(exchange(pay), pre_one, w_spatial, row(gain_reduce), row(shift_reduce), mask, count)

    hid_two, gram, pay, stat_two = call(
        expand_kernel,
        [
            block3(width, BF),
            held((width, depth), BF),
            shape((n, 2, (width + depth) // 2), F32),
            held((8, width), F32),
        ],
        [VMEM] * 7,
        [VMEM] * 4,
        flops=flops,
    )(exchange(pay), pre_two, weight_expand, row(gain_spatial), row(shift_spatial), mask, count)

    block_out, dy_three, up, part, emb, head, pay, stat_three = call(
        functools.partial(output_kernel, rows=rows),
        [
            shape((rows, depth), BF),
            block3(depth, BF),
            block3(width, F32),
            held((width, depth), F32),
            held((padded, 128), F32),
            held((depth, 128), BF),
            shape((n, 2, depth), BF),
            held((8, depth), F32),
        ],
        [VMEM] * 10,
        [HBM] + [VMEM] * 7,
        [
            pltpu.VMEM((2, chunk_rows, 256), F32),
            pltpu.VMEM((2, 2, chunk_rows, 128), F32),
            pltpu.VMEM((2, rows, 256), BF),
            pltpu.VMEM((chunks, chunk_rows, 256), BF),
            pltpu.VMEM((chunks, chunk_rows, 256), BF),
            pltpu.VMEM((2, padded, 256), BF),
            pltpu.VMEM((2, SUB, 256), F32),
            pltpu.SemaphoreType.DMA((2,)),
        ],
        flops=flops * 4,
        limit=14,
    )(
        exchange(pay), hid_two, xp, weight_expand, row(gain_expand), row(shift_expand),
        head_weight, back_emb, mask, count,
    )

    lines = images // 4
    total_three, terms, jig, scores, dy_two, pay = call(
        expand_back_kernel,
        [
            shape((2, depth), F32),
            held((8, depth), F32),
            held((PIX * 128, 128), BF),
            held((lines, width), F32),
            block3(width, F32),
            shape((n, 2, width), F32),
        ],
        [VMEM] * 14,
        [VMEM] * 6,
    )(
        exchange(pay), stat_three, up, hid_two, weight_expand,
        pre_two, stat_two, mask, count, emb, row(head_bias), pick, jigsaw_weight, cotangent,
    )
    pay = exchange(pay)

    used = depth + depth // 4 + PIX * 128 // 4 + wide * lines
    grad_rows = -(-used // unit) * unit
    keep, send = call(
        functools.partial(expand_grad_kernel, wide=wide),
        [shape((grad_rows // 2, width), BF)] * 2,
        [VMEM] * 7 + [SMEM],
        [VMEM] * 2,
        after=(pay,),
    )(terms, stat_two, part, gram, head, jig, scores, dev)
    one = Sum(keep, send, pairs, first_side)
    one.exchange()

    spatial_rows = -(-(PIX * width) // unit) * unit
    back_spatial, keep, send, total_two = call(
        spatial_grad_kernel,
        [
            block3(width, BF),
            shape((spatial_rows // 2, width), BF),
            shape((spatial_rows // 2, width), BF),
            shape((2, width), F32),
        ],
        [VMEM] * 7 + [SMEM],
        [VMEM] * 4,
        after=(one.send,),
    )(pay, stat_two, pre_two, dy_two, hid_one, mask, count, dev)
    two = Sum(keep, send, pairs, first_side)
    two.exchange()
    merge(call, dev, [one], (back_spatial,))
    one.exchange()

    dy_one, packed = call(
        spatial_back_kernel,
        [block3(width, F32), shape((2, width), F32)],
        [VMEM] * 5,
        [VMEM] * 2,
        after=(one.send,),
    )(back_spatial, w_spatial, pre_one, stat_one, mask)
    pay = call(
        payload_kernel,
        shape((n, 2, width), F32),
        [VMEM],
        VMEM,
        after=(one.got, two.got),
    )(packed)
    pay = exchange(pay)

    merge(call, dev, [one, two], (pay,))
    one.exchange()
    two.exchange()
    back_reduce, keep, send, total_one = call(
        reduce_grad_kernel,
        [
            block3(width, BF),
            shape((depth // 2, width), BF),
            shape((depth // 2, width), BF),
            shape((2, width), F32),
        ],
        [VMEM] * 7 + [SMEM],
        [VMEM] * 4,
        after=(one.send, two.send),
    )(pay, stat_one, pre_one, dy_one, xp, mask, count, dev)
    three = Sum(keep, send, pairs, first_side)
    three.exchange()
    gradient_input = call(
        functools.partial(input_kernel, rows=rows),
        shape((rows, depth), BF),
        [VMEM] * 3,
        HBM,
        [
            pltpu.VMEM((2, 4, chunk_rows, 128), F32),
            pltpu.VMEM((2, rows, 512), BF),
            pltpu.SemaphoreType.DMA((2,)),
        ],
        limit=8,
    )(back_reduce, weight_reduce, dy_three)

    late = (gradient_input,)
    active = [one, two, three]
    while active:
        merge(call, dev, active, late)
        for item in active:
            item.exchange()
        late = ()
        if one in active and one.last():
            gradient_expand, gradient_head, gradient_jigsaw, scores = call(
                functools.partial(unpack_kernel, wide=wide),
                [
                    shape((width, depth), F32),
                    shape((depth, 128), F32),
                    shape((PIX * 128, 128), F32),
                    shape((lines, width), F32),
                ],
                [VMEM, VMEM, SMEM],
                [HBM] * 3 + [VMEM],
                [
                    pltpu.VMEM((grad_rows, width), BF),
                    pltpu.VMEM((8, 288, width), F32),
                    pltpu.SemaphoreType.DMA((8,)),
                ],
                limit=max(12, grad_rows // 512 + 8),
            )(one.keep, one.got, dev)
            late = (gradient_expand,)
        if two in active and two.last():
            if spatial_rows == PIX * width:
                gradient_spatial = unpack_plain(call, two, dev)
            else:
                low = side_of(pairs[0]) == 0
                gradient_spatial = jnp.concatenate(
                    [jnp.where(low, two.keep, two.got), jnp.where(low, two.got, two.keep)]
                )[: PIX * width].astype(F32)
            late = (gradient_spatial,)
        active = [item for item in active if not item.last()]
    gradient_reduce = unpack_plain(call, three, dev, late)
    scores = scores.reshape(lines, 4, 128).transpose(1, 0, 2).reshape(images, 128)
    scores = lax.dynamic_slice_in_dim(scores, narrow_rank * own, own) + jigsaw_bias
    biases = stat_one[4]
    return (
        block_out,
        scores,
        gradient_input,
        gradient_reduce,
        total_one[0],
        total_one[1],
        gradient_spatial,
        total_two[0],
        total_two[1],
        gradient_expand,
        total_three[0],
        total_three[1],
        gradient_head,
        biases[128:256],
        gradient_jigsaw,
        biases[0:128],
    )


def solution(mesh):
    placed = (P(AXES, None),) + (P(),) * 14 + (P("wide", None),) * 3
    return jax.shard_map(
        body,
        mesh=mesh,
        in_specs=placed,
        out_specs=(P(AXES, None),) * 3 + (P(),) * 13,
        check_vma=False,
    )
```

```python
import functools

import jax
import jax.numpy as jnp
from jax import lax
from jax.experimental import pallas as pl
from jax.experimental.pallas import tpu as pltpu
from jax.sharding import PartitionSpec as P

BF = jnp.bfloat16
F32 = jnp.float32
EPS = 1e-05
AXES = ("wide", "narrow")
PIX = 9
CHUNK = 48
SUB = 16
C1 = 0.7978845608028654
C2 = C1 * 0.044715
VMEM = pl.BlockSpec(memory_space=pltpu.VMEM)
HBM = pl.BlockSpec(memory_space=pltpu.HBM)
SMEM = pl.BlockSpec(memory_space=pltpu.SMEM)
ANY = pl.BlockSpec(memory_space=pl.ANY)


def dot(a, b, ca=1, cb=0):
    return lax.dot_general(a, b, (((ca,), (cb,)), ((), ())), preferred_element_type=F32)


def dot_rows(row, b, cb=0):
    high = row.astype(BF)
    rest = row - high.astype(F32)
    mid = rest.astype(BF)
    low = (rest - mid.astype(F32)).astype(BF)
    stack = jnp.concatenate([high, mid, low, jnp.zeros((13, row.shape[1]), BF)], 0)
    return jnp.sum(dot(stack, b, 1, cb), 0, keepdims=True)


def spread(mask, width):
    return jnp.concatenate([mask] * (width // 128), 1)


def gelu(v):
    squared = v * v
    half = 0.5 * v
    return half + half * jnp.tanh(v * (C1 + C2 * squared))


def gelu_both(v):
    squared = v * v
    gate = 0.5 * jnp.tanh(v * (C1 + C2 * squared)) + 0.5
    value = v * gate
    return value, gate + value * (1.0 - gate) * (2.0 * C1 + 6.0 * C2 * squared)


def gelu_slope(v):
    return gelu_both(v)[1]


def spans(offset):
    down, right = offset // 3 - 1, offset % 3 - 1
    rows = [r for r in range(3) if 0 <= r + down < 3]
    if right == 0:
        return [(rows[0] * 3, (rows[0] + down) * 3, 3 * len(rows))]
    start = max(0, -right)
    return [(r * 3 + start, (r + down) * 3 + start + right, 2) for r in rows]


OFFSETS = (4, 1, 7, 3, 5, 0, 2, 6, 8)


def places(ref, first, count):
    chunks, _, width = ref.shape
    return ref[:, first * CHUNK : (first + count) * CHUNK, :].reshape(
        chunks * count * CHUNK, width
    )


def add_places(ref, first, count, value, start):
    chunks, _, width = ref.shape
    rows = pl.ds(first * CHUNK, count * CHUNK)
    value = value.reshape(chunks, count * CHUNK, width)
    if start:
        ref[:, rows, :] = value
    else:
        ref[:, rows, :] = ref[:, rows, :] + value


def put(keep, send, side, start, value, lane=0):
    half = keep.shape[0]
    lanes = slice(lane, lane + value.shape[1])
    for i in range(2):
        low, high = max(start, i * half), min(start + value.shape[0], (i + 1) * half)
        if low < high:
            piece = value[low - start : high - start]
            rows = slice(low - i * half, high - i * half)

            @pl.when(side == i)
            def _():
                keep[rows, lanes] = piece

            @pl.when(side != i)
            def _():
                send[rows, lanes] = piece


def moments(payload, count):
    total = jnp.sum(payload[...], 0)
    mean = total[0:1] / count
    inv = lax.rsqrt(total[1:2] / count - mean * mean + EPS)
    return total, mean, inv


def reduce_kernel(
    x_ref, w_ref, slots_ref, res_ref, perm_ref, cot_ref, jw_ref, dev_ref,
    xp_ref, pre_ref, pay_ref, mask_ref, pick_ref, back_ref, count_ref,
    buf, wbuf, flat, perm_buf, cot_buf, jw_buf, sems, wsems, ssems, *, tiles, own,
):
    rows, depth = x_ref.shape
    chunks, chunk_rows, _ = xp_ref.shape
    padded = chunks * CHUNK
    block = buf.shape[2]
    blocks = depth // block
    lanes = block // 128

    def copy(d):
        return pltpu.make_async_copy(
            x_ref.at[:, pl.ds(d * block, block)], buf.at[d % 2], sems.at[d % 2]
        )

    def copy_w(d):
        return pltpu.make_async_copy(
            w_ref.at[pl.ds(d * block, block), :], wbuf.at[d % 2], wsems.at[d % 2]
        )

    small = [
        pltpu.make_async_copy(source, target, ssems.at[i])
        for i, (source, target) in enumerate(
            ((perm_ref, perm_buf), (cot_ref, cot_buf), (jw_ref, jw_buf))
        )
    ]
    for one in small:
        one.start()
    for d in range(2):
        copy(d).start()
        copy_w(d).start()
    ids = slots_ref[...]
    image = lax.shift_right_arithmetic(ids * 7282, 16)
    piece = ids - 9 * image
    images = perm_ref.shape[1]
    here = jnp.where(image < 0, -1, image + dev_ref[0] * images)
    all_images = res_ref.shape[1]
    hit_all = lax.broadcasted_iota(jnp.int32, (all_images, padded), 0) == here
    res = res_ref[...].astype(F32)
    flags = dot(
        jnp.broadcast_to(res, (16, all_images)).astype(BF), jnp.where(hit_all, 1.0, 0.0).astype(BF)
    )[0:1]
    eye = lax.broadcasted_iota(jnp.int32, (padded, padded), 0) == lax.broadcasted_iota(
        jnp.int32, (padded, padded), 1
    )
    large = dot(jnp.where(eye, flags, 0.0).astype(BF), jnp.ones((padded, 128), BF))
    exists = lax.broadcasted_iota(jnp.int32, (padded, 128), 0) < tiles
    mask_ref[0] = jnp.where(exists, 1.0, 0.0)
    mask_ref[1] = large
    mask_ref[2] = 1.0 / (4.0 + 5.0 * large)
    total = 9.0 * (4.0 * all_images + 5.0 * jnp.sum(res, 1, keepdims=True))
    count_ref[...] = jnp.broadcast_to(total, (8, 128))
    for one in small:
        one.wait()
    perm_ref, cot_ref, jw_ref = perm_buf, cot_buf, jw_buf
    hit = lax.broadcasted_iota(jnp.int32, (images, padded), 0) == image
    rows_back = dot(cot_ref[...], jw_ref[...], 1, 1).astype(BF)
    back = jnp.zeros((padded, 128), F32)
    small_eye = lax.broadcasted_iota(jnp.int32, (images, images), 0) == lax.broadcasted_iota(
        jnp.int32, (images, images), 1
    )
    perm = dot(jnp.where(small_eye, 1.0, 0.0).astype(BF), perm_ref[...].astype(F32).astype(BF), 1, 1)
    piece = piece.astype(F32)
    for k in range(PIX):
        chosen = jnp.where(hit & (perm[:, k : k + 1] == piece), 1.0, 0.0).astype(BF)
        pick_ref[k * images : (k + 1) * images, :] = chosen
        back = back + dot(chosen, rows_back[:, k * 128 : (k + 1) * 128], 0, 0)
    back = back.astype(BF)
    back_ref[...] = back
    tail = rows - (chunks - 1) * chunk_rows

    def product(d):
        part = dot(
            xp_ref[:, :, d * block : (d + 1) * block].reshape(chunks * chunk_rows, block),
            wbuf[d % 2],
        ).reshape(pre_ref.shape)
        pre_ref[...] = part if d == 0 else pre_ref[...] + part

    for d in range(blocks):
        copy(d).wait()
        if d > 0:
            copy_w(d - 1).wait()
            product(d - 1)
        cols = slice(d * block, (d + 1) * block)
        for c in range(chunks):
            size = chunk_rows if c + 1 < chunks else tail
            for lane in range(lanes):
                flat[c % 2, lane, 0:size, :] = buf[
                    d % 2, c * chunk_rows : c * chunk_rows + size, lane * 128 : (lane + 1) * 128
                ].astype(F32)
                if size < chunk_rows:
                    flat[c % 2, lane, size:, :] = jnp.zeros((chunk_rows - size, 128), F32)
            for p in range(PIX):
                xp_ref[c, p * CHUNK : (p + 1) * CHUNK, cols] = jnp.concatenate(
                    [flat[c % 2, lane, pl.ds(p, CHUNK, stride=PIX), :] for lane in range(lanes)], 1
                ).astype(BF)
        if d + 2 < blocks:
            copy(d + 2).start()
        if 0 < d < blocks - 1:
            copy_w(d + 1).start()
    copy_w(blocks - 1).wait()
    product(blocks - 1)
    width = pre_ref.shape[2]

    def sums(c, carry):
        first, second = carry
        for p in range(PIX):
            a = pre_ref[c, p * CHUNK : (p + 1) * CHUNK, :]
            if p not in (0, 1, 3, 4):
                m = spread(mask_ref[1, pl.ds(pl.multiple_of(c * CHUNK, CHUNK), CHUNK), :], width)
                a = a * m
            first = first + jnp.sum(a.reshape(CHUNK // 8, 8, width), 0)
            second = second + jnp.sum((a * a).reshape(CHUNK // 8, 8, width), 0)
        return first, second

    zero = jnp.zeros((8, width), F32)
    first, second = lax.fori_loop(0, chunks, sums, (zero, zero))
    own_cot = jnp.where(
        lax.broadcasted_iota(jnp.int32, cot_ref.shape, 0) // own == dev_ref[1],
        cot_ref[...].astype(F32),
        0.0,
    )
    biases = jnp.concatenate(
        [
            jnp.sum(own_cot, 0, keepdims=True),
            jnp.sum(back.astype(F32), 0, keepdims=True),
            jnp.zeros((1, width - 256), F32),
        ],
        1,
    )
    packed = jnp.concatenate(
        [jnp.sum(first, 0, keepdims=True), jnp.sum(second, 0, keepdims=True), biases], 0
    )
    pay_ref[...] = jnp.broadcast_to(packed[None], pay_ref.shape)


def masks(mask_ref, c, p, width):
    kind = 0 if p in (0, 1, 3, 4) else 1
    return spread(mask_ref[kind, pl.ds(pl.multiple_of(c * CHUNK, CHUNK), CHUNK), :], width)


def load_offsets(w_ref, wbuf, sems):
    loads = {k: pltpu.make_async_copy(w_ref.at[k], wbuf.at[k], sems.at[k]) for k in OFFSETS}
    for k in OFFSETS:
        loads[k].start()
    return loads


def spatial_kernel(
    pay_ref, pre_ref, w_ref, gain_ref, shift_ref, mask_ref, count_ref,
    hid_ref, out_ref, next_ref, stat_ref, jig_ref, head_ref, wbuf, sems,
):
    chunks, chunk_rows, width = pre_ref.shape
    loads = load_offsets(w_ref, wbuf, sems)
    count = count_ref[0:1, 0:1]
    total, mean, inv = moments(pay_ref, count)
    scale = gain_ref[...] * inv
    base = shift_ref[...] - mean * scale
    stat_ref[...] = jnp.concatenate([mean, inv, scale, base, jnp.zeros((4, width), F32)], 0)
    jig_ref[...] = total[2:3, 0:128]
    head_ref[...] = total[2:3, 128:256]

    def act(c, _):
        for p in range(PIX):
            rows = slice(p * CHUNK, (p + 1) * CHUNK)
            a = pre_ref[c, rows, :] * scale + base
            hid_ref[c, rows, :] = (gelu(a) * masks(mask_ref, c, p, width)).astype(BF)
        return 0

    lax.fori_loop(0, chunks, act, 0)
    for k in OFFSETS:
        loads[k].wait()
        for first_out, first_in, n in spans(k):
            for s in range(0, n, 3):
                m = min(3, n - s)
                part = dot(places(hid_ref, first_in + s, m), wbuf[k])
                add_places(out_ref, first_out + s, m, part, k == OFFSETS[0])

    def sums(c, carry):
        first, second = carry
        for p in range(PIX):
            a = out_ref[c, p * CHUNK : (p + 1) * CHUNK, :]
            if p not in (0, 1, 3, 4):
                a = a * masks(mask_ref, c, p, width)
            first = first + jnp.sum(a.reshape(CHUNK // 8, 8, width), 0)
            second = second + jnp.sum((a * a).reshape(CHUNK // 8, 8, width), 0)
        return first, second

    zero = jnp.zeros((8, width), F32)
    first, second = lax.fori_loop(0, chunks, sums, (zero, zero))
    packed = jnp.concatenate(
        [jnp.sum(first, 0, keepdims=True), jnp.sum(second, 0, keepdims=True)], 0
    )
    next_ref[...] = jnp.broadcast_to(packed[None], next_ref.shape)


def expand_kernel(
    pay_ref, pre_ref, w_ref, gain_ref, shift_ref, mask_ref, count_ref,
    hid_ref, gram_ref, next_ref, stat_ref,
):
    chunks, chunk_rows, width = pre_ref.shape
    depth = w_ref.shape[1]
    count = count_ref[0:1, 0:1]
    _, mean, inv = moments(pay_ref, count)
    scale = gain_ref[...] * inv
    base = shift_ref[...] - mean * scale

    def act(c, column):
        for p in range(PIX):
            rows = slice(p * CHUNK, (p + 1) * CHUNK)
            a = pre_ref[c, rows, :] * scale + base
            h = (gelu(a) * masks(mask_ref, c, p, width)).astype(BF)
            hid_ref[c, rows, :] = h
            column = column + jnp.sum(h.astype(F32).reshape(CHUNK // 8, 8, width), 0)
        return column

    column = lax.fori_loop(0, chunks, act, jnp.zeros((8, width), F32))
    column = jnp.sum(column, 0, keepdims=True)
    stat_ref[...] = jnp.concatenate(
        [mean, inv, scale, base, column, jnp.zeros((3, width), F32)], 0
    )
    flat = hid_ref[...].reshape(chunks * chunk_rows, width)
    gram = dot(flat, flat, 0, 0)
    high = gram.astype(BF)
    low = (gram - high.astype(F32)).astype(BF)
    block = width
    packed = [column]
    for d in range(0, depth, block):
        w = w_ref[:, d : d + block]
        product = dot(high, w) + dot(low, w)
        gram_ref[:, d : d + block] = product.astype(BF)
        second = jnp.sum(product * w.astype(F32), 0, keepdims=True)
        packed.append(second)
    packed = jnp.concatenate(packed, 1)
    half = packed.shape[1] // 2
    packed = jnp.concatenate([packed[:, :half], packed[:, half:]], 0)
    next_ref[...] = jnp.broadcast_to(packed[None], next_ref.shape)


def output_kernel(
    pay_ref, hid_ref, xp_ref, w_ref, gain_ref, shift_ref, hw_ref, back_ref, mask_ref, count_ref,
    out_ref, dy_ref, up_ref, part_ref, emb_ref, head_ref, next_ref, stat_ref,
    pre, flat, obuf, dy_even, dy_odd, pool_ref, first_ref, sems, *, rows,
):
    chunks, chunk_rows, depth = xp_ref.shape
    width = hid_ref.shape[2]
    block = pre.shape[2]
    lanes = block // 128
    blocks = depth // block
    tail = rows - (chunks - 1) * chunk_rows
    count = count_ref[0:1, 0:1]

    def copy(d, slot):
        return pltpu.make_async_copy(
            obuf.at[slot], out_ref.at[:, pl.ds(pl.multiple_of(d * block, block), block)], sems.at[slot]
        )

    total = jnp.sum(pay_ref[...], 0)
    total = jnp.concatenate([total[0:1], total[1:2]], 1)
    mean_all = dot_rows(total[:, :width], w_ref[...]) / count
    square_all = total[:, width:] / count
    inv_all = lax.rsqrt(square_all - mean_all * mean_all + EPS)
    scale_all = gain_ref[...] * inv_all
    stat_ref[...] = jnp.concatenate(
        [
            mean_all,
            inv_all,
            scale_all,
            shift_ref[...] - mean_all * scale_all,
            jnp.concatenate([total[:, :width] / count, jnp.zeros((1, depth - width), F32)], 1),
            jnp.zeros((3, depth), F32),
        ],
        0,
    )
    dy_bufs = (dy_even, dy_odd)
    up_ref[...] = jnp.zeros(up_ref.shape, F32)
    emb_ref[...] = jnp.zeros(emb_ref.shape, F32)
    cells = spread(mask_ref[2], block)

    def columns(d):
        return pl.ds(pl.multiple_of(d * block, block), block)

    def forward(d, slot):
        dy_buf = dy_bufs[slot]
        cols = columns(d)
        scale = stat_ref[2:3, cols]
        base = stat_ref[3:4, cols]
        w = w_ref[:, cols]
        back_pool = dot(back_ref[...], hw_ref[cols, :], 1, 1) * cells
        back_large = back_pool * spread(mask_ref[1], block)
        pools = []
        first = jnp.zeros((SUB, block), F32)
        for c in range(chunks):
            pre[c % 2] = dot(hid_ref[c], w)
            for s in range(0, CHUNK, SUB):
                pool = jnp.zeros((SUB, block), F32)
                bp_small = back_pool[c * CHUNK + s : c * CHUNK + s + SUB]
                bp_large = back_large[c * CHUNK + s : c * CHUNK + s + SUB]
                m_large = spread(mask_ref[1, c * CHUNK + s : c * CHUNK + s + SUB, :], block)
                for p in range(PIX):
                    at = p * CHUNK + s
                    v = (
                        pre[c % 2, at : at + SUB, :] * scale
                        + base
                        + xp_ref[c, at : at + SUB, cols].astype(F32)
                    )
                    value, slope = gelu_both(v)
                    if p in (0, 1, 3, 4):
                        dy = slope * bp_small
                    else:
                        value = value * m_large
                        dy = slope * bp_large
                    pool = pool + value
                    first = first + dy
                    dy = dy.astype(BF)
                    dy_ref[c, at : at + SUB, cols] = dy
                    dy_buf[c, at : at + SUB, :] = dy
                    for lane in range(lanes):
                        flat[c % 2, lane, pl.ds(s * PIX + p, SUB, stride=PIX), :] = value[
                            :, lane * 128 : (lane + 1) * 128
                        ]
                pools.append(pool)
            size = chunk_rows if c + 1 < chunks else tail
            for lane in range(lanes):
                obuf[
                    slot, c * chunk_rows : c * chunk_rows + size, lane * 128 : (lane + 1) * 128
                ] = flat[c % 2, lane, 0:size, :].astype(BF)
        pool_ref[slot] = (jnp.concatenate(pools, 0) * cells).astype(BF)
        first_ref[slot] = first

    def backward(d, slot):
        dy_buf = dy_bufs[slot]
        cols = columns(d)
        w = w_ref[:, cols].astype(F32)
        scaled = (w * stat_ref[2:3, cols]).astype(BF)
        for c in range(chunks):
            up_ref[c] = up_ref[c] + dot(dy_buf[c], scaled, 1, 1)
        dy = dy_buf[...].reshape(chunks * chunk_rows, block)
        part = dot(hid_ref[...].reshape(chunks * chunk_rows, width), dy, 0, 0)
        part_ref[:, cols] = part
        first = jnp.sum(first_ref[slot], 0, keepdims=True)
        second = stat_ref[1:2, cols] * (
            jnp.sum(part * w, 0, keepdims=True) - stat_ref[0:1, cols] * first
        )
        next_ref[:, :, cols] = jnp.broadcast_to(
            jnp.concatenate([second, first], 0).astype(BF)[None], (next_ref.shape[0], 2, block)
        )
        pooled = pool_ref[slot]
        emb_ref[...] = emb_ref[...] + dot(pooled, hw_ref[cols, :])
        head_ref[cols, :] = dot(pooled, back_ref[...], 0, 0).astype(BF)

    def pair(i, _):
        for slot in range(2):
            d = 2 * i + slot
            copy(d - 2, slot).wait()
            backward(d - 1, 1 - slot)
            forward(d, slot)
            copy(d, slot).start()
        return 0

    forward(0, 0)
    copy(0, 0).start()
    backward(0, 0)
    forward(1, 1)
    copy(1, 1).start()
    lax.fori_loop(1, blocks // 2, pair, 0)
    backward(blocks - 1, 1)
    copy(blocks - 2, 0).wait()
    copy(blocks - 1, 1).wait()


def backward_terms(pay_ref, stat_ref, count):
    total = jnp.sum(pay_ref[...].astype(F32), 0)
    dgain, dshift = total[0:1], total[1:2]
    mean, inv, scale = stat_ref[0:1], stat_ref[1:2], stat_ref[2:3]
    slope = scale * inv * dgain / count
    level = scale * dshift / count - mean * slope
    return total, scale, slope, level


def expand_back_kernel(
    pay_ref, stat_ref, up_ref, hid_ref, w_ref,
    pre_ref, stat2_ref, mask_ref, count_ref,
    dgain_ref, dshift_ref, dy_ref, next_ref,
):
    chunks, chunk_rows, width = pre_ref.shape
    depth = w_ref.shape[1]
    count = count_ref[0:1, 0:1]
    total, scale, slope, level = backward_terms(pay_ref, stat_ref, count)
    dgain_ref[...] = total[0:1]
    dshift_ref[...] = total[1:2]
    cross = jnp.zeros((width, width), F32)
    block = 512
    per_std = stat_ref[1:2] * total[0:1] / count
    per_row = total[1:2] / count
    constant = jnp.zeros((1, width), F32)
    for d in range(0, depth, block):
        cols = slice(d, d + block)
        w = w_ref[:, cols].astype(F32)
        scaled = (w * scale[:, cols]).astype(BF)
        cross = cross + dot((w * per_std[:, cols]).astype(BF), scaled, 1, 1)
        constant = constant + dot_rows(per_row[:, cols], scaled, 1)
    cross = cross.astype(BF)
    constant = constant - dot_rows(stat_ref[4:5, :width], cross)
    mean2, inv2, scale2, base2 = (stat2_ref[i : i + 1] for i in range(4))

    def step(c, carry):
        first, second = carry
        fix = dot(hid_ref[c], cross)
        for p in range(PIX):
            rows = slice(p * CHUNK, (p + 1) * CHUNK)
            a = pre_ref[c, rows, :]
            g = up_ref[c, rows, :] - fix[rows] - constant
            dy = gelu_slope(a * scale2 + base2) * g * masks(mask_ref, c, p, width)
            dy_ref[c, rows, :] = dy
            first = first + jnp.sum(dy.reshape(CHUNK // 8, 8, width), 0)
            second = second + jnp.sum(
                (dy * ((a - mean2) * inv2)).reshape(CHUNK // 8, 8, width), 0
            )
        return first, second

    zero = jnp.zeros((8, width), F32)
    first, second = lax.fori_loop(0, chunks, step, (zero, zero))
    packed = jnp.concatenate(
        [jnp.sum(second, 0, keepdims=True), jnp.sum(first, 0, keepdims=True)], 0
    )
    next_ref[...] = packed


def expand_grad_kernel(
    pay_ref, stat_ref, count_ref, stat2_ref, part_ref, gram_ref, head_ref,
    emb_ref, hb_ref, pick_ref, jw_ref, cot_ref, dev_ref,
    keep_ref, send_ref, *, wide,
):
    width, depth = part_ref.shape
    put_rows = functools.partial(put, keep_ref, send_ref, dev_ref[2])
    _, scale, slope, level = backward_terms(pay_ref, stat_ref, count_ref[0:1, 0:1])
    tall = dot_rows_t(stat2_ref[4:5], level)
    block = 512
    at = 0
    for d in range(0, depth, block):
        cols = slice(d, d + block)
        grad = (
            part_ref[:, cols] * scale[:, cols]
            - tall[:, cols]
            - gram_ref[:, cols].astype(F32) * slope[:, cols]
        )
        put_rows(at, grad.astype(BF))
        at += width
    embedded = (emb_ref[...] + hb_ref[...]).astype(BF)
    images = cot_ref.shape[0]
    ordered = dot(pick_ref[...], embedded).astype(BF)
    scores = jnp.zeros((images, 128), F32)
    jigs = []
    for k in range(PIX):
        mine = ordered[k * images : (k + 1) * images]
        scores = scores + dot(mine, jw_ref[k * 128 : (k + 1) * 128, :])
        jigs.append(dot(mine, cot_ref[...], 0, 0).astype(BF))
    lines = images // 4
    scores = jnp.concatenate([scores[i * lines : (i + 1) * lines] for i in range(4)], 1)
    for value in (head_ref[...], jnp.concatenate(jigs, 0)):
        quarter = value.shape[0] // 4
        for i in range(4):
            put_rows(at, value[i * quarter : (i + 1) * quarter], i * 128)
        at += quarter
    left = 2 * keep_ref.shape[0] - at - wide * lines
    scores = [jnp.where(dev_ref[0] == g, scores, 0.0) for g in range(wide)]
    if left > 0:
        scores.append(jnp.zeros((left, width), F32))
    put_rows(at, jnp.concatenate(scores, 0).astype(BF))


def dot_rows_t(column, row):
    n = column.shape[1]
    m = row.shape[1]
    tall = jnp.transpose(jnp.broadcast_to(column, (8, n)))[:, 0:1]
    return tall * jnp.broadcast_to(row, (n, m))


def spatial_grad_kernel(
    pay_ref, stat_ref, pre_ref, dy_ref, hid_ref, mask_ref, count_ref,
    dev_ref, back_ref, keep_ref, send_ref, dgain_ref, dshift_ref,
):
    chunks, chunk_rows, width = pre_ref.shape
    count = count_ref[0:1, 0:1]
    total, scale, slope, level = backward_terms(pay_ref, stat_ref, count)
    dgain_ref[...] = total[0:1]
    dshift_ref[...] = total[1:2]

    def step(c, _):
        for p in range(PIX):
            rows = slice(p * CHUNK, (p + 1) * CHUNK)
            b = dy_ref[c, rows, :] * scale - level - pre_ref[c, rows, :] * slope
            back_ref[c, rows, :] = (b * masks(mask_ref, c, p, width)).astype(BF)
        return 0

    lax.fori_loop(0, chunks, step, 0)
    for k in range(PIX):
        runs = spans(k)
        grad = dot(
            jnp.concatenate([places(hid_ref, first_in, n) for _, first_in, n in runs], 0),
            jnp.concatenate([places(back_ref, first_out, n) for first_out, _, n in runs], 0),
            0,
            0,
        )
        put(keep_ref, send_ref, dev_ref[2], k * width, grad.astype(BF))
    left = 2 * keep_ref.shape[0] - PIX * width
    if left > 0:
        put(keep_ref, send_ref, dev_ref[2], PIX * width, jnp.zeros((left, width), BF))


def spread_back(back_ref, w_ref, dy_ref, offsets):
    for k in offsets:
        for first_out, first_in, n in spans(k):
            for s in range(0, n, 3):
                m = min(3, n - s)
                part = dot(places(back_ref, first_out + s, m), w_ref[k], 1, 1)
                add_places(dy_ref, first_in + s, m, part, k == OFFSETS[0])


def spatial_back_kernel(back_ref, w_ref, dy_ref):
    spread_back(back_ref, w_ref, dy_ref, OFFSETS[:5])


def spatial_back_end_kernel(
    back_ref, w_ref, pre_ref, stat_ref, mask_ref, _, dy_ref, next_ref,
):
    chunks, chunk_rows, width = pre_ref.shape
    mean, inv, scale, base = (stat_ref[i : i + 1] for i in range(4))
    spread_back(back_ref, w_ref, dy_ref, OFFSETS[5:])

    def step(c, carry):
        first, second = carry
        for p in range(PIX):
            rows = slice(p * CHUNK, (p + 1) * CHUNK)
            a = pre_ref[c, rows, :]
            dy = gelu_slope(a * scale + base) * dy_ref[c, rows, :] * masks(mask_ref, c, p, width)
            dy_ref[c, rows, :] = dy
            first = first + jnp.sum(dy.reshape(CHUNK // 8, 8, width), 0)
            second = second + jnp.sum((dy * ((a - mean) * inv)).reshape(CHUNK // 8, 8, width), 0)
        return first, second

    zero = jnp.zeros((8, width), F32)
    first, second = lax.fori_loop(0, chunks, step, (zero, zero))
    next_ref[...] = jnp.concatenate(
        [jnp.sum(second, 0, keepdims=True), jnp.sum(first, 0, keepdims=True)], 0
    )


def payload_kernel(packed_ref, next_ref):
    next_ref[...] = jnp.broadcast_to(packed_ref[...][None], next_ref.shape)


def reduce_grad_kernel(
    pay_ref, stat_ref, pre_ref, dy_ref, xp_ref, mask_ref, count_ref, dev_ref,
    back_ref, keep_ref, send_ref, dgain_ref, dshift_ref,
):
    chunks, chunk_rows, width = pre_ref.shape
    depth = xp_ref.shape[2]
    count = count_ref[0:1, 0:1]
    total, scale, slope, level = backward_terms(pay_ref, stat_ref, count)
    dgain_ref[...] = total[0:1]
    dshift_ref[...] = total[1:2]

    def step(c, _):
        for p in range(PIX):
            at = slice(p * CHUNK, (p + 1) * CHUNK)
            b = dy_ref[c, at, :] * scale - level - pre_ref[c, at, :] * slope
            back_ref[c, at, :] = (b * masks(mask_ref, c, p, width)).astype(BF)
        return 0

    lax.fori_loop(0, chunks, step, 0)
    flat_back = back_ref[...].reshape(chunks * chunk_rows, width)
    block = 512
    for d in range(0, depth, block):
        grad = dot(
            xp_ref[:, :, d : d + block].reshape(chunks * chunk_rows, block), flat_back, 0, 0
        )
        put(keep_ref, send_ref, dev_ref[2], d, grad.astype(BF))


def input_kernel(back_ref, w_ref, res_ref, gin_ref, flat, obuf, sems, *, rows):
    chunks, chunk_rows, width = back_ref.shape
    depth = w_ref.shape[0]
    block = obuf.shape[2]
    lanes = block // 128
    blocks = depth // block
    tail = rows - (chunks - 1) * chunk_rows

    def copy(d):
        return pltpu.make_async_copy(
            obuf.at[d % 2], gin_ref.at[:, pl.ds(d * block, block)], sems.at[d % 2]
        )

    for d in range(blocks):
        cols = slice(d * block, (d + 1) * block)
        if d >= 2:
            copy(d - 2).wait()
        for c in range(chunks):
            part = dot(back_ref[c], w_ref[cols, :], 1, 1)
            for p in range(PIX):
                at = slice(p * CHUNK, (p + 1) * CHUNK)
                value = part[at] + res_ref[c, at, cols].astype(F32)
                for lane in range(lanes):
                    flat[c % 2, lane, pl.ds(p, CHUNK, stride=PIX), :] = value[
                        :, lane * 128 : (lane + 1) * 128
                    ]
            size = chunk_rows if c + 1 < chunks else tail
            for lane in range(lanes):
                obuf[
                    d % 2, c * chunk_rows : c * chunk_rows + size, lane * 128 : (lane + 1) * 128
                ] = flat[c % 2, lane, 0:size, :].astype(BF)
        copy(d).start()
    copy(blocks - 2).wait()
    copy(blocks - 1).wait()


def writer(stage, sems):
    pending = []
    slots = stage.shape[0]

    def write(value, target):
        slot = len(pending) % slots
        if len(pending) >= slots:
            pending[-slots].wait()
        part = stage.at[slot, pl.ds(0, value.shape[0]), pl.ds(0, value.shape[1])]
        part[...] = value
        copy = pltpu.make_async_copy(part, target, sems.at[slot])
        copy.start()
        pending.append(copy)

    def finish():
        for copy in pending[-slots:]:
            copy.wait()

    return write, finish


def unpack_plain_kernel(mine_ref, other_ref, dev_ref, out_ref, stage, sems):
    half = mine_ref.shape[0]
    write, finish = writer(stage, sems)
    step = half // 4
    for ref, side in ((mine_ref, dev_ref[2]), (other_ref, 1 - dev_ref[2])):
        for r in range(0, half, step):
            start = pl.multiple_of(side * half + r, 16)
            write(ref[r : r + step, :].astype(F32), out_ref.at[pl.ds(start, step), :])
    finish()


def unpack_plain(call, item, numbers, after=()):
    half, width = item.keep.shape
    return call(
        unpack_plain_kernel,
        shape((2 * half, width), F32),
        [VMEM, VMEM, SMEM],
        HBM,
        [pltpu.VMEM((4, half // 4, width), F32), pltpu.SemaphoreType.DMA((4,))],
        limit=8,
        after=after,
    )(item.keep, item.got, numbers)


def unpack_kernel(
    mine_ref, other_ref, dev_ref, bias_ref, expand_ref, head_ref, jig_ref, score_ref,
    rest, stage, sems,
    *, wide,
):
    half, width = mine_ref.shape
    write, finish = writer(stage, sems)
    for ref, side in ((mine_ref, dev_ref[2]), (other_ref, 1 - dev_ref[2])):
        rest[pl.ds(pl.multiple_of(side * half, 16), half), :] = ref[...]
    depth = expand_ref.shape[1]
    for i in range(depth // width):
        for r in range(0, width, 256):
            write(
                rest[i * width + r : i * width + r + 256, :].astype(F32),
                expand_ref.at[pl.ds(r, 256), pl.ds(i * width, width)],
            )
    at = depth
    quarter = depth // 4
    for i in range(4):
        for r in range(0, quarter, 256):
            write(
                rest[at + r : at + r + 256, i * 128 : (i + 1) * 128].astype(F32),
                head_ref.at[pl.ds(i * quarter + r, 256), :],
            )
    at += quarter
    quarter = jig_ref.shape[0] // 4
    for i in range(4):
        write(
            rest[at : at + quarter, i * 128 : (i + 1) * 128].astype(F32),
            jig_ref.at[pl.ds(i * quarter, quarter), :],
        )
    at += quarter
    lines = score_ref.shape[0]
    total = jnp.zeros((lines, width), F32)
    for g in range(wide):
        total = total + jnp.where(
            dev_ref[0] == g, rest[at + g * lines : at + (g + 1) * lines, :].astype(F32), 0.0
        )
    scores = jnp.zeros((lines, 128), F32)
    for j in range(4):
        scores = scores + jnp.where(dev_ref[1] == j, total[:, j * 128 : (j + 1) * 128], 0.0)
    score_ref[...] = scores + bias_ref[...]
    finish()


def shape(dims, dtype):
    return jax.ShapeDtypeStruct(dims, dtype)


def held(dims, dtype):
    return pltpu.VMEM(dims, dtype)


def exchange(payload):
    return lax.all_to_all(payload, AXES, 0, 0)


def device_index():
    return lax.axis_index("wide") * lax.axis_size("narrow") + lax.axis_index("narrow")


def swap(value, bits):
    n = lax.axis_size("wide") * lax.axis_size("narrow")
    return lax.ppermute(value, AXES, [(i, i ^ bits[i % 2]) for i in range(n)])


def side_of(bits):
    me = device_index()
    return (me // jnp.where(me % 2 == 1, bits[1], bits[0])) % 2


def halves(ref, side):
    half = ref.shape[0] // 2
    return ref[pl.ds(pl.multiple_of(side * half, 8), half), :]


def merge_kernel(*refs, plan):
    dev_ref = refs[0]
    inputs = iter(refs[1 : 1 + sum(1 + (kind != "pass") for kind, _ in plan)])
    outputs = iter(refs[1 + sum(1 + (kind != "pass") for kind, _ in plan) :])
    for kind, index in plan:
        mine = next(inputs)
        if kind == "pass":
            target = next(outputs)
            target[...] = mine[...]
            continue
        got = next(inputs)
        if kind == "split":
            side = dev_ref[index]
            keep, send = next(outputs), next(outputs)
            keep[...] = halves(mine, side).astype(F32) + halves(got, side).astype(F32)
            send[...] = (
                halves(mine, 1 - side).astype(F32) + halves(got, 1 - side).astype(F32)
            ).astype(BF)
        elif kind == "sum":
            target = next(outputs)
            target[...] = (mine[...].astype(F32) + got[...].astype(F32)).astype(BF)
        else:
            side = dev_ref[index]
            target = next(outputs)
            half = mine.shape[0]
            target[pl.ds(pl.multiple_of(side * half, 16), half), :] = mine[...]
            target[pl.ds(pl.multiple_of((1 - side) * half, 16), half), :] = got[...]


class Sum:
    def __init__(self, keep, send, pairs, first_side):
        self.keep, self.send, self.pairs, self.sides = keep, send, pairs, first_side
        self.at = 0
        self.got = None
        self.gathering = False

    def exchange(self):
        self.got = swap(self.send, self.pairs[self.at])
        return self.got

    def last(self):
        return self.gathering and self.at == 0

    def kind(self):
        if self.gathering:
            return "join", self.sides + self.at
        if self.at + 1 < len(self.pairs):
            return "split", self.sides + self.at + 1
        return "sum", 0

    def shapes(self):
        rows, width = self.got.shape
        kind = self.kind()[0]
        if kind == "split":
            return [shape((rows // 2, width), F32), shape((rows // 2, width), BF)]
        if kind == "sum":
            return [shape((rows, width), BF)]
        return [shape((2 * rows, width), BF)]

    def take(self, results):
        kind = self.kind()[0]
        if kind == "split":
            self.keep, self.send = results
            self.at += 1
        else:
            self.keep = self.send = results[0]
            if kind == "sum":
                self.gathering = True
            else:
                self.at -= 1


def merge(call, numbers, sums, after=(), flops=0):
    shapes = [item.shapes() for item in sums]
    outs = call(
        functools.partial(merge_kernel, plan=tuple(item.kind() for item in sums)),
        [one for each in shapes for one in each],
        [SMEM] + [VMEM, VMEM] * len(sums),
        [VMEM] * sum(map(len, shapes)),
        after=after,
        flops=flops,
    )(numbers, *(value for item in sums for value in (item.keep, item.got)))
    outs = list(outs)
    for item, each in zip(sums, shapes):
        item.take(outs[: len(each)])
        outs = outs[len(each) :]


def is_in(value, values):
    return any(value is v for v in values)


def kernel_call(
    kernel, out_shape, in_specs, out_specs, scratch=(), limit=6, flops=0, bytes_accessed=0,
    after=(), resident=(), far=(), alias=None,
):
    n_in, n_after = len(in_specs), len(after)
    spare = max(0, lax.axis_size("wide") * lax.axis_size("narrow") // 16 - 2)

    def run(*refs):
        kernel(*refs[:n_in], *refs[n_in + n_after :])

    made = pl.pallas_call(
        run,
        out_shape=out_shape,
        in_specs=list(in_specs) + [HBM if is_in(a, far) else ANY for a in after],
        out_specs=out_specs,
        scratch_shapes=list(scratch),
        input_output_aliases=alias or {},
        compiler_params=pltpu.CompilerParams(vmem_limit_bytes=(limit + spare) << 20),
        cost_estimate=pl.CostEstimate(
            flops=max(1, int(flops)), bytes_accessed=1, transcendentals=0
        ),
    )

    def placed(*args):
        fixed = []
        for a, spec in zip(args, in_specs):
            if spec is HBM:
                a = pltpu.with_memory_space_constraint(a, pltpu.HBM)
            elif spec is VMEM and is_in(a, resident):
                a = pltpu.with_memory_space_constraint(a, pltpu.VMEM)
            fixed.append(a)
        for a in after:
            fixed.append(pltpu.with_memory_space_constraint(a, pltpu.HBM) if is_in(a, far) else a)
        outs = made(*fixed)
        if isinstance(out_shape, list):
            for made_shape, spec, out in zip(out_shape, out_specs, outs):
                if not isinstance(made_shape, jax.ShapeDtypeStruct):
                    resident.append(out)
                if spec is HBM:
                    far.append(out)
        elif out_specs is HBM:
            far.append(outs)
        return outs

    return placed


def body(
    block_in,
    weight_reduce,
    gain_reduce,
    shift_reduce,
    weight_spatial,
    gain_spatial,
    shift_spatial,
    weight_expand,
    gain_expand,
    shift_expand,
    head_weight,
    head_bias,
    jigsaw_weight,
    jigsaw_bias,
    resolution,
    tile_slot,
    jigsaw_perm,
    cotangent,
):
    rows, depth = block_in.shape
    width = weight_reduce.shape[1]
    tiles = rows // PIX
    chunks = -(-tiles // CHUNK)
    padded = chunks * CHUNK
    chunk_rows = CHUNK * PIX
    wide, narrow = lax.axis_size("wide"), lax.axis_size("narrow")
    n = wide * narrow
    images = jigsaw_perm.shape[0]
    own = images // narrow
    unit = 16 * n
    assert images // 4 == own
    wide_rank, narrow_rank = lax.axis_index("wide"), lax.axis_index("narrow")
    slots = lax.dynamic_slice_in_dim(tile_slot, narrow_rank * tiles, tiles, 1)
    slots = jnp.pad(slots, ((0, 0), (0, padded - tiles)), constant_values=-1)
    bits = [1 << i for i in range(n.bit_length() - 1)]
    axes = {"y": bits[1:2], "x": bits[2:3], "0": bits[3:4], "1": bits[4:]}

    def pairs_of(even, odd):
        return list(zip(*([bits[0]] + sum((axes[a] for a in order), []) for order in (even, odd))))

    first_side = 2
    dev = jnp.stack(
        [wide_rank, narrow_rank]
        + [side_of(b) for b in pairs_of("xy01", "yx10") + pairs_of("xy01", "yx01")]
    ).astype(jnp.int32)
    row = lambda v: v.reshape(1, -1)
    block3 = lambda last, dtype: held((chunks, chunk_rows, last), dtype)
    call = functools.partial(kernel_call, resident=[], far=[])
    flops = 2 * padded * PIX * width * depth

    xp, pre_one, pay, mask, pick, back_emb, count = call(
        functools.partial(reduce_kernel, tiles=tiles, own=own),
        [
            block3(depth, BF),
            block3(width, F32),
            shape((n, 3, width), F32),
            held((3, padded, 128), F32),
            held((PIX * images, padded), BF),
            held((padded, 128), BF),
            held((8, 128), F32),
        ],
        [HBM, HBM, VMEM, VMEM, HBM, HBM, HBM, SMEM],
        [VMEM] * 7,
        [
            pltpu.VMEM((2, rows, 512), BF),
            pltpu.VMEM((2, 512, width), BF),
            pltpu.VMEM((2, 4, chunk_rows, 128), F32),
            pltpu.VMEM((PIX, images), jnp.int32),
            pltpu.VMEM(cotangent.shape, BF),
            pltpu.VMEM(jigsaw_weight.shape, BF),
            pltpu.SemaphoreType.DMA((2,)),
            pltpu.SemaphoreType.DMA((2,)),
            pltpu.SemaphoreType.DMA((3,)),
        ],
        limit=12,
        flops=flops,
    )(block_in, weight_reduce, slots, row(resolution), jigsaw_perm.T, cotangent, jigsaw_weight, dev)

    offset_scratch = [pltpu.VMEM((PIX, width, width), BF), pltpu.SemaphoreType.DMA((PIX,))]
    w_spatial = weight_spatial.reshape(PIX, width, width)
    hid_one, pre_two, pay, stat_one, jig_total, head_total = call(
        spatial_kernel,
        [
            block3(width, BF),
            block3(width, F32),
            shape((n, 2, width), F32),
            held((8, width), F32),
            shape((1, 128), F32),
            shape((1, 128), F32),
        ],
        [VMEM, VMEM, HBM] + [VMEM] * 4,
        [VMEM] * 6,
        offset_scratch,
        flops=flops * 1.4,
        limit=12,
    )(exchange(pay), pre_one, w_spatial, row(gain_reduce), row(shift_reduce), mask, count)

    hid_two, gram, pay, stat_two = call(
        expand_kernel,
        [
            block3(width, BF),
            held((width, depth), BF),
            shape((n, 2, (width + depth) // 2), F32),
            held((8, width), F32),
        ],
        [VMEM] * 7,
        [VMEM] * 4,
        flops=flops,
    )(exchange(pay), pre_two, weight_expand, row(gain_spatial), row(shift_spatial), mask, count)

    block_out, dy_three, up, part, emb, head, pay, stat_three = call(
        functools.partial(output_kernel, rows=rows),
        [
            shape((rows, depth), BF),
            block3(depth, BF),
            block3(width, F32),
            held((width, depth), F32),
            held((padded, 128), F32),
            held((depth, 128), BF),
            shape((n, 2, depth), BF),
            held((8, depth), F32),
        ],
        [VMEM] * 10,
        [HBM] + [VMEM] * 7,
        [
            pltpu.VMEM((2, chunk_rows, 256), F32),
            pltpu.VMEM((2, 2, chunk_rows, 128), F32),
            pltpu.VMEM((2, rows, 256), BF),
            pltpu.VMEM((chunks, chunk_rows, 256), BF),
            pltpu.VMEM((chunks, chunk_rows, 256), BF),
            pltpu.VMEM((2, padded, 256), BF),
            pltpu.VMEM((2, SUB, 256), F32),
            pltpu.SemaphoreType.DMA((2,)),
        ],
        flops=flops * 4,
        limit=14,
    )(
        exchange(pay), hid_two, xp, weight_expand, row(gain_expand), row(shift_expand),
        head_weight, back_emb, mask, count,
    )

    lines = images // 4
    pay = exchange(pay)
    used = depth + depth // 4 + PIX * 128 // 4 + wide * lines
    grad_rows = -(-used // unit) * unit
    keep, send = call(
        functools.partial(expand_grad_kernel, wide=wide),
        [shape((grad_rows // 2, width), BF)] * 2,
        [VMEM] * 12 + [SMEM],
        [VMEM] * 2,
    )(
        pay, stat_three, count, stat_two, part, gram, head,
        emb, row(head_bias), pick, jigsaw_weight, cotangent, dev,
    )
    one = Sum(keep, send, pairs_of("xy01", "yx10"), first_side)
    one.exchange()
    long = 10**11
    gain_three, shift_three, dy_two, packed = call(
        expand_back_kernel,
        [shape((1, depth), F32)] * 2 + [block3(width, F32), shape((2, width), F32)],
        [VMEM] * 9,
        [VMEM] * 4,
        after=(one.send,),
        flops=long,
    )(pay, stat_three, up, hid_two, weight_expand, pre_two, stat_two, mask, count)

    def send_packed(packed, after):
        return exchange(
            call(payload_kernel, shape((n, 2, width), F32), [VMEM], VMEM, after=after)(packed)
        )

    pay = send_packed(packed, (one.got,))
    merge(call, dev, [one], (pay,))
    one.exchange()

    spatial_rows = -(-(PIX * width) // unit) * unit
    back_spatial, keep, send, gain_two, shift_two = call(
        spatial_grad_kernel,
        [
            block3(width, BF),
            shape((spatial_rows // 2, width), BF),
            shape((spatial_rows // 2, width), BF),
            shape((1, width), F32),
            shape((1, width), F32),
        ],
        [VMEM] * 7 + [SMEM],
        [VMEM] * 5,
        after=(one.send,),
        flops=long,
    )(pay, stat_two, pre_two, dy_two, hid_one, mask, count, dev)
    two = Sum(keep, send, pairs_of("xy01", "yx10"), first_side)
    two.exchange()
    merge(call, dev, [one], (back_spatial,))
    one.exchange()
    partial = call(
        spatial_back_kernel,
        [block3(width, F32)],
        [VMEM, VMEM],
        [VMEM],
        after=(two.send, one.send),
        flops=long,
    )(back_spatial, w_spatial)[0]
    merge(call, dev, [one, two], (partial,))
    one.exchange()
    two.exchange()
    dy_one, packed = call(
        spatial_back_end_kernel,
        [block3(width, F32), shape((2, width), F32)],
        [VMEM] * 6,
        [VMEM] * 2,
        after=(one.send, two.send),
        alias={5: 0},
        flops=long,
    )(back_spatial, w_spatial, pre_one, stat_one, mask, partial)
    pay = send_packed(packed, (one.got,))
    merge(call, dev, [one, two], (pay,))
    one.exchange()
    two.exchange()
    back_reduce, keep, send, gain_one, shift_one = call(
        reduce_grad_kernel,
        [
            block3(width, BF),
            shape((depth // 2, width), BF),
            shape((depth // 2, width), BF),
            shape((1, width), F32),
            shape((1, width), F32),
        ],
        [VMEM] * 7 + [SMEM],
        [VMEM] * 5,
        flops=long,
        after=(one.send, two.send),
    )(pay, stat_one, pre_one, dy_one, xp, mask, count, dev)
    three = Sum(keep, send, pairs_of("xy01", "yx01"), first_side + len(bits))
    three.exchange()
    merge(call, dev, [one, two], (back_reduce,))
    one.exchange()
    two.exchange()
    gradient_input = call(
        functools.partial(input_kernel, rows=rows),
        shape((rows, depth), BF),
        [VMEM] * 3,
        HBM,
        [
            pltpu.VMEM((2, 4, chunk_rows, 128), F32),
            pltpu.VMEM((2, rows, 512), BF),
            pltpu.SemaphoreType.DMA((2,)),
        ],
        flops=long,
        limit=8,
        after=(one.send, two.send),
    )(back_reduce, weight_reduce, dy_three)

    sums = {"E": one, "S": two, "R": three}
    turns = "SRESERSERSRERSRERESRSRR" if len(bits) == 5 else "SRE" * (3 * len(bits))
    late = gradient_input
    for turn in turns:
        item = sums.get(turn)
        if item is None:
            continue
        if not item.last():
            merge(call, dev, [item], (late,), long // 20)
            item.exchange()
            late = item.send
            continue
        del sums[turn]
        if turn == "E":
            gradient_expand, gradient_head, gradient_jigsaw, scores = call(
                functools.partial(unpack_kernel, wide=wide),
                [
                    shape((width, depth), F32),
                    shape((depth, 128), F32),
                    shape((PIX * 128, 128), F32),
                    shape((lines, 128), F32),
                ],
                [VMEM, VMEM, SMEM, VMEM],
                [HBM] * 3 + [VMEM],
                [
                    pltpu.VMEM((grad_rows, width), BF),
                    pltpu.VMEM((8, 288, width), F32),
                    pltpu.SemaphoreType.DMA((8,)),
                ],
                limit=max(12, grad_rows // 512 + 8),
                after=(late,),
            )(one.keep, one.got, dev, row(jigsaw_bias))
            late = gradient_expand
        elif turn == "S" and spatial_rows != PIX * width:
            low = side_of(two.pairs[0]) == 0
            gradient_spatial = jnp.concatenate(
                [jnp.where(low, two.keep, two.got), jnp.where(low, two.got, two.keep)]
            )[: PIX * width].astype(F32)
        elif turn == "S":
            gradient_spatial = late = unpack_plain(call, two, dev, (late,))
        else:
            gradient_reduce = late = unpack_plain(call, three, dev, (late,))
    return (
        block_out,
        scores,
        gradient_input,
        gradient_reduce,
        gain_one.reshape(-1),
        shift_one.reshape(-1),
        gradient_spatial,
        gain_two.reshape(-1),
        shift_two.reshape(-1),
        gradient_expand,
        gain_three.reshape(-1),
        shift_three.reshape(-1),
        gradient_head,
        head_total.reshape(-1),
        gradient_jigsaw,
        jig_total.reshape(-1),
    )


def solution(mesh):
    placed = (P(AXES, None),) + (P(),) * 14 + (P("wide", None),) * 3
    return jax.shard_map(
        body,
        mesh=mesh,
        in_specs=placed,
        out_specs=(P(AXES, None),) * 3 + (P(),) * 13,
        check_vma=False,
    )
```

```python
import functools

import jax
import jax.numpy as jnp
from jax import lax
from jax.experimental import pallas as pl
from jax.experimental.pallas import tpu as pltpu
from jax.sharding import PartitionSpec as P

BF = jnp.bfloat16
F32 = jnp.float32
EPS = 1e-05
AXES = ("wide", "narrow")
PIX = 9
CHUNK = 48
SUB = 16
C1 = 0.7978845608028654
C2 = C1 * 0.044715
VMEM = pl.BlockSpec(memory_space=pltpu.VMEM)
HBM = pl.BlockSpec(memory_space=pltpu.HBM)
SMEM = pl.BlockSpec(memory_space=pltpu.SMEM)
ANY = pl.BlockSpec(memory_space=pl.ANY)


def dot(a, b, ca=1, cb=0):
    return lax.dot_general(a, b, (((ca,), (cb,)), ((), ())), preferred_element_type=F32)


def dot_rows(row, b, cb=0):
    high = row.astype(BF)
    rest = row - high.astype(F32)
    mid = rest.astype(BF)
    low = (rest - mid.astype(F32)).astype(BF)
    stack = jnp.concatenate([high, mid, low, jnp.zeros((13, row.shape[1]), BF)], 0)
    return jnp.sum(dot(stack, b, 1, cb), 0, keepdims=True)


def spread(mask, width):
    return jnp.concatenate([mask] * (width // 128), 1)


def gelu(v):
    squared = v * v
    half = 0.5 * v
    return half + half * jnp.tanh(v * (C1 + C2 * squared))


def gelu_both(v):
    squared = v * v
    gate = 0.5 * jnp.tanh(v * (C1 + C2 * squared)) + 0.5
    value = v * gate
    return value, gate + value * (1.0 - gate) * (2.0 * C1 + 6.0 * C2 * squared)


def gelu_slope(v):
    return gelu_both(v)[1]


def spans(offset):
    down, right = offset // 3 - 1, offset % 3 - 1
    rows = [r for r in range(3) if 0 <= r + down < 3]
    if right == 0:
        return [(rows[0] * 3, (rows[0] + down) * 3, 3 * len(rows))]
    start = max(0, -right)
    return [(r * 3 + start, (r + down) * 3 + start + right, 2) for r in rows]


OFFSETS = (4, 1, 7, 3, 5, 0, 2, 6, 8)


def places(ref, first, count):
    chunks, _, width = ref.shape
    return ref[:, first * CHUNK : (first + count) * CHUNK, :].reshape(
        chunks * count * CHUNK, width
    )


def add_places(ref, first, count, value, start):
    chunks, _, width = ref.shape
    rows = pl.ds(first * CHUNK, count * CHUNK)
    value = value.reshape(chunks, count * CHUNK, width)
    if start:
        ref[:, rows, :] = value
    else:
        ref[:, rows, :] = ref[:, rows, :] + value


def put(keep, send, side, start, value, lane=0):
    half = keep.shape[0]
    lanes = slice(lane, lane + value.shape[1])
    for i in range(2):
        low, high = max(start, i * half), min(start + value.shape[0], (i + 1) * half)
        if low < high:
            piece = value[low - start : high - start]
            rows = slice(low - i * half, high - i * half)

            @pl.when(side == i)
            def _():
                keep[rows, lanes] = piece

            @pl.when(side != i)
            def _():
                send[rows, lanes] = piece


def moments(payload, count):
    total = jnp.sum(payload[...], 0)
    mean = total[0:1] / count
    inv = lax.rsqrt(total[1:2] / count - mean * mean + EPS)
    return total, mean, inv


def reduce_kernel(
    x_ref, w_ref, slots_ref, res_ref, perm_ref, cot_ref, jw_ref, dev_ref,
    xp_ref, pre_ref, pay_ref, mask_ref, pick_ref, back_ref, count_ref, bias_ref,
    buf, wbuf, flat, perm_buf, cot_buf, jw_buf, sems, wsems, ssems, *, tiles, own,
):
    rows, depth = x_ref.shape
    chunks, chunk_rows, _ = xp_ref.shape
    padded = chunks * CHUNK
    block = buf.shape[2]
    blocks = depth // block
    lanes = block // 128

    def copy(d):
        return pltpu.make_async_copy(
            x_ref.at[:, pl.ds(d * block, block)], buf.at[d % 2], sems.at[d % 2]
        )

    def copy_w(d):
        return pltpu.make_async_copy(
            w_ref.at[pl.ds(d * block, block), :], wbuf.at[d % 2], wsems.at[d % 2]
        )

    small = [
        pltpu.make_async_copy(source, target, ssems.at[i])
        for i, (source, target) in enumerate(
            ((perm_ref, perm_buf), (cot_ref, cot_buf), (jw_ref, jw_buf))
        )
    ]
    for one in small:
        one.start()
    for d in range(2):
        copy(d).start()
        copy_w(d).start()
    ids = slots_ref[...]
    image = lax.shift_right_arithmetic(ids * 7282, 16)
    piece = ids - 9 * image
    images = perm_ref.shape[1]
    here = jnp.where(image < 0, -1, image + dev_ref[0] * images)
    all_images = res_ref.shape[1]
    hit_all = lax.broadcasted_iota(jnp.int32, (all_images, padded), 0) == here
    res = res_ref[...].astype(F32)
    flags = dot(
        jnp.broadcast_to(res, (16, all_images)).astype(BF), jnp.where(hit_all, 1.0, 0.0).astype(BF)
    )[0:1]
    eye = lax.broadcasted_iota(jnp.int32, (padded, padded), 0) == lax.broadcasted_iota(
        jnp.int32, (padded, padded), 1
    )
    large = dot(jnp.where(eye, flags, 0.0).astype(BF), jnp.ones((padded, 128), BF))
    exists = lax.broadcasted_iota(jnp.int32, (padded, 128), 0) < tiles
    mask_ref[0] = jnp.where(exists, 1.0, 0.0)
    mask_ref[1] = large
    mask_ref[2] = 1.0 / (4.0 + 5.0 * large)
    total = 9.0 * (4.0 * all_images + 5.0 * jnp.sum(res, 1, keepdims=True))
    count_ref[...] = jnp.broadcast_to(total, (8, 128))
    for one in small:
        one.wait()
    perm_ref, cot_ref, jw_ref = perm_buf, cot_buf, jw_buf
    hit = lax.broadcasted_iota(jnp.int32, (images, padded), 0) == image
    rows_back = dot(cot_ref[...], jw_ref[...], 1, 1).astype(BF)
    back = jnp.zeros((padded, 128), F32)
    small_eye = lax.broadcasted_iota(jnp.int32, (images, images), 0) == lax.broadcasted_iota(
        jnp.int32, (images, images), 1
    )
    perm = dot(jnp.where(small_eye, 1.0, 0.0).astype(BF), perm_ref[...].astype(F32).astype(BF), 1, 1)
    piece = piece.astype(F32)
    for k in range(PIX):
        chosen = jnp.where(hit & (perm[:, k : k + 1] == piece), 1.0, 0.0).astype(BF)
        pick_ref[k * images : (k + 1) * images, :] = chosen
        back = back + dot(chosen, rows_back[:, k * 128 : (k + 1) * 128], 0, 0)
    back = back.astype(BF)
    back_ref[...] = back
    tail = rows - (chunks - 1) * chunk_rows

    def product(d):
        part = dot(
            xp_ref[:, :, d * block : (d + 1) * block].reshape(chunks * chunk_rows, block),
            wbuf[d % 2],
        ).reshape(pre_ref.shape)
        pre_ref[...] = part if d == 0 else pre_ref[...] + part

    for d in range(blocks):
        copy(d).wait()
        if d > 0:
            copy_w(d - 1).wait()
            product(d - 1)
        cols = slice(d * block, (d + 1) * block)
        for c in range(chunks):
            size = chunk_rows if c + 1 < chunks else tail
            for lane in range(lanes):
                flat[c % 2, lane, 0:size, :] = buf[
                    d % 2, c * chunk_rows : c * chunk_rows + size, lane * 128 : (lane + 1) * 128
                ].astype(F32)
                if size < chunk_rows:
                    flat[c % 2, lane, size:, :] = jnp.zeros((chunk_rows - size, 128), F32)
            for p in range(PIX):
                xp_ref[c, p * CHUNK : (p + 1) * CHUNK, cols] = jnp.concatenate(
                    [flat[c % 2, lane, pl.ds(p, CHUNK, stride=PIX), :] for lane in range(lanes)], 1
                ).astype(BF)
        if d + 2 < blocks:
            copy(d + 2).start()
        if 0 < d < blocks - 1:
            copy_w(d + 1).start()
    copy_w(blocks - 1).wait()
    product(blocks - 1)
    width = pre_ref.shape[2]

    def sums(c, carry):
        first, second = carry
        for p in range(PIX):
            a = pre_ref[c, p * CHUNK : (p + 1) * CHUNK, :]
            if p not in (0, 1, 3, 4):
                m = spread(mask_ref[1, pl.ds(pl.multiple_of(c * CHUNK, CHUNK), CHUNK), :], width)
                a = a * m
            first = first + jnp.sum(a.reshape(CHUNK // 8, 8, width), 0)
            second = second + jnp.sum((a * a).reshape(CHUNK // 8, 8, width), 0)
        return first, second

    zero = jnp.zeros((8, width), F32)
    first, second = lax.fori_loop(0, chunks, sums, (zero, zero))
    own_cot = jnp.where(
        lax.broadcasted_iota(jnp.int32, cot_ref.shape, 0) // own == dev_ref[1],
        cot_ref[...].astype(F32),
        0.0,
    )
    biases = jnp.concatenate(
        [
            jnp.sum(own_cot, 0, keepdims=True),
            jnp.sum(back.astype(F32), 0, keepdims=True),
            jnp.zeros((1, width - 256), F32),
        ],
        1,
    )
    bias_ref[...] = biases
    packed = jnp.concatenate(
        [jnp.sum(first, 0, keepdims=True), jnp.sum(second, 0, keepdims=True)], 0
    )
    pay_ref[...] = jnp.broadcast_to(packed[None], pay_ref.shape)


def masks(mask_ref, c, p, width):
    kind = 0 if p in (0, 1, 3, 4) else 1
    return spread(mask_ref[kind, pl.ds(pl.multiple_of(c * CHUNK, CHUNK), CHUNK), :], width)


def load_offsets(w_ref, wbuf, sems):
    loads = {k: pltpu.make_async_copy(w_ref.at[k], wbuf.at[k], sems.at[k]) for k in OFFSETS}
    for k in OFFSETS:
        loads[k].start()
    return loads


def spatial_kernel(
    pay_ref, pre_ref, w_ref, gain_ref, shift_ref, mask_ref, count_ref,
    hid_ref, out_ref, next_ref, stat_ref, wbuf, sems,
):
    chunks, chunk_rows, width = pre_ref.shape
    loads = load_offsets(w_ref, wbuf, sems)
    count = count_ref[0:1, 0:1]
    total, mean, inv = moments(pay_ref, count)
    scale = gain_ref[...] * inv
    base = shift_ref[...] - mean * scale
    stat_ref[...] = jnp.concatenate([mean, inv, scale, base, jnp.zeros((4, width), F32)], 0)

    def act(c, _):
        for p in range(PIX):
            rows = slice(p * CHUNK, (p + 1) * CHUNK)
            a = pre_ref[c, rows, :] * scale + base
            hid_ref[c, rows, :] = (gelu(a) * masks(mask_ref, c, p, width)).astype(BF)
        return 0

    lax.fori_loop(0, chunks, act, 0)
    for k in OFFSETS:
        loads[k].wait()
        for first_out, first_in, n in spans(k):
            for s in range(0, n, 3):
                m = min(3, n - s)
                part = dot(places(hid_ref, first_in + s, m), wbuf[k])
                add_places(out_ref, first_out + s, m, part, k == OFFSETS[0])

    def sums(c, carry):
        first, second = carry
        for p in range(PIX):
            a = out_ref[c, p * CHUNK : (p + 1) * CHUNK, :]
            if p not in (0, 1, 3, 4):
                a = a * masks(mask_ref, c, p, width)
            first = first + jnp.sum(a.reshape(CHUNK // 8, 8, width), 0)
            second = second + jnp.sum((a * a).reshape(CHUNK // 8, 8, width), 0)
        return first, second

    zero = jnp.zeros((8, width), F32)
    first, second = lax.fori_loop(0, chunks, sums, (zero, zero))
    packed = jnp.concatenate(
        [jnp.sum(first, 0, keepdims=True), jnp.sum(second, 0, keepdims=True)], 0
    )
    next_ref[...] = jnp.broadcast_to(packed[None], next_ref.shape)


def expand_kernel(
    pay_ref, pre_ref, w_ref, gain_ref, shift_ref, mask_ref, count_ref,
    hid_ref, gram_ref, next_ref, stat_ref,
):
    chunks, chunk_rows, width = pre_ref.shape
    depth = w_ref.shape[1]
    count = count_ref[0:1, 0:1]
    _, mean, inv = moments(pay_ref, count)
    scale = gain_ref[...] * inv
    base = shift_ref[...] - mean * scale

    def act(c, column):
        for p in range(PIX):
            rows = slice(p * CHUNK, (p + 1) * CHUNK)
            a = pre_ref[c, rows, :] * scale + base
            h = (gelu(a) * masks(mask_ref, c, p, width)).astype(BF)
            hid_ref[c, rows, :] = h
            column = column + jnp.sum(h.astype(F32).reshape(CHUNK // 8, 8, width), 0)
        return column

    column = lax.fori_loop(0, chunks, act, jnp.zeros((8, width), F32))
    column = jnp.sum(column, 0, keepdims=True)
    stat_ref[...] = jnp.concatenate(
        [mean, inv, scale, base, column, jnp.zeros((3, width), F32)], 0
    )
    flat = hid_ref[...].reshape(chunks * chunk_rows, width)
    gram = dot(flat, flat, 0, 0)
    high = gram.astype(BF)
    low = (gram - high.astype(F32)).astype(BF)
    block = width
    packed = [column]
    for d in range(0, depth, block):
        w = w_ref[:, d : d + block]
        product = dot(high, w) + dot(low, w)
        gram_ref[:, d : d + block] = product.astype(BF)
        second = jnp.sum(product * w.astype(F32), 0, keepdims=True)
        packed.append(second)
    packed = jnp.concatenate(packed, 1)
    half = packed.shape[1] // 2
    packed = jnp.concatenate([packed[:, :half], packed[:, half:]], 0)
    next_ref[...] = jnp.broadcast_to(packed[None], next_ref.shape)


def output_kernel(
    pay_ref, hid_ref, xp_ref, w_ref, gain_ref, shift_ref, hw_ref, back_ref, mask_ref, count_ref,
    out_ref, dy_ref, up_ref, part_ref, emb_ref, head_ref, next_ref, stat_ref,
    pre, flat, obuf, dy_even, dy_odd, pool_ref, first_ref, sems, *, rows,
):
    chunks, chunk_rows, depth = xp_ref.shape
    width = hid_ref.shape[2]
    block = pre.shape[2]
    lanes = block // 128
    blocks = depth // block
    tail = rows - (chunks - 1) * chunk_rows
    count = count_ref[0:1, 0:1]

    def copy(d, slot):
        return pltpu.make_async_copy(
            obuf.at[slot], out_ref.at[:, pl.ds(pl.multiple_of(d * block, block), block)], sems.at[slot]
        )

    total = jnp.sum(pay_ref[...], 0)
    total = jnp.concatenate([total[0:1], total[1:2]], 1)
    mean_all = dot_rows(total[:, :width], w_ref[...]) / count
    square_all = total[:, width:] / count
    inv_all = lax.rsqrt(square_all - mean_all * mean_all + EPS)
    scale_all = gain_ref[...] * inv_all
    stat_ref[...] = jnp.concatenate(
        [
            mean_all,
            inv_all,
            scale_all,
            shift_ref[...] - mean_all * scale_all,
            jnp.concatenate([total[:, :width] / count, jnp.zeros((1, depth - width), F32)], 1),
            jnp.zeros((3, depth), F32),
        ],
        0,
    )
    dy_bufs = (dy_even, dy_odd)
    up_ref[...] = jnp.zeros(up_ref.shape, F32)
    emb_ref[...] = jnp.zeros(emb_ref.shape, F32)
    cells = spread(mask_ref[2], block)

    def columns(d):
        return pl.ds(pl.multiple_of(d * block, block), block)

    def forward(d, slot):
        dy_buf = dy_bufs[slot]
        cols = columns(d)
        scale = stat_ref[2:3, cols]
        base = stat_ref[3:4, cols]
        w = w_ref[:, cols]
        back_pool = dot(back_ref[...], hw_ref[cols, :], 1, 1) * cells
        back_large = back_pool * spread(mask_ref[1], block)
        pools = []
        first = jnp.zeros((SUB, block), F32)
        for c in range(chunks):
            pre[c % 2] = dot(hid_ref[c], w)
            for s in range(0, CHUNK, SUB):
                pool = jnp.zeros((SUB, block), F32)
                bp_small = back_pool[c * CHUNK + s : c * CHUNK + s + SUB]
                bp_large = back_large[c * CHUNK + s : c * CHUNK + s + SUB]
                m_large = spread(mask_ref[1, c * CHUNK + s : c * CHUNK + s + SUB, :], block)
                for p in range(PIX):
                    at = p * CHUNK + s
                    v = (
                        pre[c % 2, at : at + SUB, :] * scale
                        + base
                        + xp_ref[c, at : at + SUB, cols].astype(F32)
                    )
                    value, slope = gelu_both(v)
                    if p in (0, 1, 3, 4):
                        dy = slope * bp_small
                    else:
                        value = value * m_large
                        dy = slope * bp_large
                    pool = pool + value
                    first = first + dy
                    dy = dy.astype(BF)
                    dy_ref[c, at : at + SUB, cols] = dy
                    dy_buf[c, at : at + SUB, :] = dy
                    for lane in range(lanes):
                        flat[c % 2, lane, pl.ds(s * PIX + p, SUB, stride=PIX), :] = value[
                            :, lane * 128 : (lane + 1) * 128
                        ]
                pools.append(pool)
            size = chunk_rows if c + 1 < chunks else tail
            for lane in range(lanes):
                obuf[
                    slot, c * chunk_rows : c * chunk_rows + size, lane * 128 : (lane + 1) * 128
                ] = flat[c % 2, lane, 0:size, :].astype(BF)
        pool_ref[slot] = (jnp.concatenate(pools, 0) * cells).astype(BF)
        first_ref[slot] = first

    def backward(d, slot):
        dy_buf = dy_bufs[slot]
        cols = columns(d)
        w = w_ref[:, cols].astype(F32)
        scaled = (w * stat_ref[2:3, cols]).astype(BF)
        for c in range(chunks):
            up_ref[c] = up_ref[c] + dot(dy_buf[c], scaled, 1, 1)
        dy = dy_buf[...].reshape(chunks * chunk_rows, block)
        part = dot(hid_ref[...].reshape(chunks * chunk_rows, width), dy, 0, 0)
        part_ref[:, cols] = part
        first = jnp.sum(first_ref[slot], 0, keepdims=True)
        second = stat_ref[1:2, cols] * (
            jnp.sum(part * w, 0, keepdims=True) - stat_ref[0:1, cols] * first
        )
        next_ref[:, :, cols] = jnp.broadcast_to(
            jnp.concatenate([second, first], 0).astype(BF)[None], (next_ref.shape[0], 2, block)
        )
        pooled = pool_ref[slot]
        emb_ref[...] = emb_ref[...] + dot(pooled, hw_ref[cols, :])
        head_ref[cols, :] = dot(pooled, back_ref[...], 0, 0).astype(BF)

    def pair(i, _):
        for slot in range(2):
            d = 2 * i + slot
            copy(d - 2, slot).wait()
            backward(d - 1, 1 - slot)
            forward(d, slot)
            copy(d, slot).start()
        return 0

    forward(0, 0)
    copy(0, 0).start()
    backward(0, 0)
    forward(1, 1)
    copy(1, 1).start()
    lax.fori_loop(1, blocks // 2, pair, 0)
    backward(blocks - 1, 1)
    copy(blocks - 2, 0).wait()
    copy(blocks - 1, 1).wait()


def backward_terms(pay_ref, stat_ref, count):
    total = jnp.sum(pay_ref[...].astype(F32), 0)
    dgain, dshift = total[0:1], total[1:2]
    mean, inv, scale = stat_ref[0:1], stat_ref[1:2], stat_ref[2:3]
    slope = scale * inv * dgain / count
    level = scale * dshift / count - mean * slope
    return total, scale, slope, level


def expand_back_kernel(
    pay_ref, stat_ref, up_ref, hid_ref, w_ref,
    pre_ref, stat2_ref, mask_ref, count_ref,
    dgain_ref, dshift_ref, dy_ref, next_ref,
):
    chunks, chunk_rows, width = pre_ref.shape
    depth = w_ref.shape[1]
    count = count_ref[0:1, 0:1]
    total, scale, slope, level = backward_terms(pay_ref, stat_ref, count)
    dgain_ref[...] = total[0:1]
    dshift_ref[...] = total[1:2]
    cross = jnp.zeros((width, width), F32)
    block = 512
    per_std = stat_ref[1:2] * total[0:1] / count
    per_row = total[1:2] / count
    constant = jnp.zeros((1, width), F32)
    for d in range(0, depth, block):
        cols = slice(d, d + block)
        w = w_ref[:, cols].astype(F32)
        scaled = (w * scale[:, cols]).astype(BF)
        cross = cross + dot((w * per_std[:, cols]).astype(BF), scaled, 1, 1)
        constant = constant + dot_rows(per_row[:, cols], scaled, 1)
    cross = cross.astype(BF)
    constant = constant - dot_rows(stat_ref[4:5, :width], cross)
    mean2, inv2, scale2, base2 = (stat2_ref[i : i + 1] for i in range(4))

    def step(c, carry):
        first, second = carry
        fix = dot(hid_ref[c], cross)
        for p in range(PIX):
            rows = slice(p * CHUNK, (p + 1) * CHUNK)
            a = pre_ref[c, rows, :]
            g = up_ref[c, rows, :] - fix[rows] - constant
            dy = gelu_slope(a * scale2 + base2) * g * masks(mask_ref, c, p, width)
            dy_ref[c, rows, :] = dy
            first = first + jnp.sum(dy.reshape(CHUNK // 8, 8, width), 0)
            second = second + jnp.sum(
                (dy * ((a - mean2) * inv2)).reshape(CHUNK // 8, 8, width), 0
            )
        return first, second

    zero = jnp.zeros((8, width), F32)
    first, second = lax.fori_loop(0, chunks, step, (zero, zero))
    packed = jnp.concatenate(
        [jnp.sum(second, 0, keepdims=True), jnp.sum(first, 0, keepdims=True)], 0
    )
    next_ref[...] = packed


def expand_grad_kernel(
    pay_ref, stat_ref, count_ref, stat2_ref, part_ref, gram_ref, head_ref,
    emb_ref, hb_ref, pick_ref, jw_ref, cot_ref, bias_ref, dev_ref,
    keep_ref, send_ref, *, wide,
):
    width, depth = part_ref.shape
    put_rows = functools.partial(put, keep_ref, send_ref, dev_ref[2])
    _, scale, slope, level = backward_terms(pay_ref, stat_ref, count_ref[0:1, 0:1])
    tall = dot_rows_t(stat2_ref[4:5], level)
    block = 512
    at = 0
    for d in range(0, depth, block):
        cols = slice(d, d + block)
        grad = (
            part_ref[:, cols] * scale[:, cols]
            - tall[:, cols]
            - gram_ref[:, cols].astype(F32) * slope[:, cols]
        )
        put_rows(at, grad.astype(BF))
        at += width
    embedded = (emb_ref[...] + hb_ref[...]).astype(BF)
    images = cot_ref.shape[0]
    ordered = dot(pick_ref[...], embedded).astype(BF)
    scores = jnp.zeros((images, 128), F32)
    jigs = []
    for k in range(PIX):
        mine = ordered[k * images : (k + 1) * images]
        scores = scores + dot(mine, jw_ref[k * 128 : (k + 1) * 128, :])
        jigs.append(dot(mine, cot_ref[...], 0, 0).astype(BF))
    lines = images // 4
    scores = jnp.concatenate([scores[i * lines : (i + 1) * lines] for i in range(4)], 1)
    for value in (head_ref[...], jnp.concatenate(jigs, 0)):
        quarter = value.shape[0] // 4
        for i in range(4):
            put_rows(at, value[i * quarter : (i + 1) * quarter], i * 128)
        at += quarter
    left = 2 * keep_ref.shape[0] - at - wide * lines
    scores = [jnp.where(dev_ref[0] == g, scores, 0.0) for g in range(wide)]
    scores += [bias_ref[...], jnp.zeros((left - 1, width), F32)]
    put_rows(at, jnp.concatenate(scores, 0).astype(BF))


def dot_rows_t(column, row):
    n = column.shape[1]
    m = row.shape[1]
    tall = jnp.transpose(jnp.broadcast_to(column, (8, n)))[:, 0:1]
    return tall * jnp.broadcast_to(row, (n, m))


def spatial_grad_kernel(
    pay_ref, stat_ref, pre_ref, dy_ref, hid_ref, mask_ref, count_ref,
    dev_ref, back_ref, keep_ref, send_ref, dgain_ref, dshift_ref,
):
    chunks, chunk_rows, width = pre_ref.shape
    count = count_ref[0:1, 0:1]
    total, scale, slope, level = backward_terms(pay_ref, stat_ref, count)
    dgain_ref[...] = total[0:1]
    dshift_ref[...] = total[1:2]

    def step(c, _):
        for p in range(PIX):
            rows = slice(p * CHUNK, (p + 1) * CHUNK)
            b = dy_ref[c, rows, :] * scale - level - pre_ref[c, rows, :] * slope
            back_ref[c, rows, :] = (b * masks(mask_ref, c, p, width)).astype(BF)
        return 0

    lax.fori_loop(0, chunks, step, 0)
    for k in range(PIX):
        runs = spans(k)
        grad = dot(
            jnp.concatenate([places(hid_ref, first_in, n) for _, first_in, n in runs], 0),
            jnp.concatenate([places(back_ref, first_out, n) for first_out, _, n in runs], 0),
            0,
            0,
        )
        put(keep_ref, send_ref, dev_ref[2], k * width, grad.astype(BF))
    left = 2 * keep_ref.shape[0] - PIX * width
    if left > 0:
        put(keep_ref, send_ref, dev_ref[2], PIX * width, jnp.zeros((left, width), BF))


def spread_back(back_ref, w_ref, dy_ref, offsets):
    for k in offsets:
        for first_out, first_in, n in spans(k):
            for s in range(0, n, 3):
                m = min(3, n - s)
                part = dot(places(back_ref, first_out + s, m), w_ref[k], 1, 1)
                add_places(dy_ref, first_in + s, m, part, k == OFFSETS[0])


def spatial_back_kernel(back_ref, w_ref, dy_ref):
    spread_back(back_ref, w_ref, dy_ref, OFFSETS[:5])


def spatial_back_end_kernel(
    back_ref, w_ref, pre_ref, stat_ref, mask_ref, _, dy_ref, next_ref,
):
    chunks, chunk_rows, width = pre_ref.shape
    mean, inv, scale, base = (stat_ref[i : i + 1] for i in range(4))
    spread_back(back_ref, w_ref, dy_ref, OFFSETS[5:])

    def step(c, carry):
        first, second = carry
        for p in range(PIX):
            rows = slice(p * CHUNK, (p + 1) * CHUNK)
            a = pre_ref[c, rows, :]
            dy = gelu_slope(a * scale + base) * dy_ref[c, rows, :] * masks(mask_ref, c, p, width)
            dy_ref[c, rows, :] = dy
            first = first + jnp.sum(dy.reshape(CHUNK // 8, 8, width), 0)
            second = second + jnp.sum((dy * ((a - mean) * inv)).reshape(CHUNK // 8, 8, width), 0)
        return first, second

    zero = jnp.zeros((8, width), F32)
    first, second = lax.fori_loop(0, chunks, step, (zero, zero))
    next_ref[...] = jnp.concatenate(
        [jnp.sum(second, 0, keepdims=True), jnp.sum(first, 0, keepdims=True)], 0
    )


def payload_kernel(packed_ref, next_ref):
    next_ref[...] = jnp.broadcast_to(packed_ref[...][None], next_ref.shape)


def reduce_grad_kernel(
    pay_ref, stat_ref, pre_ref, dy_ref, xp_ref, mask_ref, count_ref, dev_ref,
    back_ref, keep_ref, send_ref, dgain_ref, dshift_ref,
):
    chunks, chunk_rows, width = pre_ref.shape
    depth = xp_ref.shape[2]
    count = count_ref[0:1, 0:1]
    total, scale, slope, level = backward_terms(pay_ref, stat_ref, count)
    dgain_ref[...] = total[0:1]
    dshift_ref[...] = total[1:2]

    def step(c, _):
        for p in range(PIX):
            at = slice(p * CHUNK, (p + 1) * CHUNK)
            b = dy_ref[c, at, :] * scale - level - pre_ref[c, at, :] * slope
            back_ref[c, at, :] = (b * masks(mask_ref, c, p, width)).astype(BF)
        return 0

    lax.fori_loop(0, chunks, step, 0)
    flat_back = back_ref[...].reshape(chunks * chunk_rows, width)
    block = 512
    for d in range(0, depth, block):
        grad = dot(
            xp_ref[:, :, d : d + block].reshape(chunks * chunk_rows, block), flat_back, 0, 0
        )
        put(keep_ref, send_ref, dev_ref[2], d, grad.astype(BF))


def input_kernel(back_ref, w_ref, res_ref, gin_ref, flat, obuf, sems, *, rows):
    chunks, chunk_rows, width = back_ref.shape
    depth = w_ref.shape[0]
    block = obuf.shape[2]
    lanes = block // 128
    blocks = depth // block
    tail = rows - (chunks - 1) * chunk_rows

    def copy(d):
        return pltpu.make_async_copy(
            obuf.at[d % 2], gin_ref.at[:, pl.ds(d * block, block)], sems.at[d % 2]
        )

    for d in range(blocks):
        cols = slice(d * block, (d + 1) * block)
        if d >= 2:
            copy(d - 2).wait()
        for c in range(chunks):
            part = dot(back_ref[c], w_ref[cols, :], 1, 1)
            for p in range(PIX):
                at = slice(p * CHUNK, (p + 1) * CHUNK)
                value = part[at] + res_ref[c, at, cols].astype(F32)
                for lane in range(lanes):
                    flat[c % 2, lane, pl.ds(p, CHUNK, stride=PIX), :] = value[
                        :, lane * 128 : (lane + 1) * 128
                    ]
            size = chunk_rows if c + 1 < chunks else tail
            for lane in range(lanes):
                obuf[
                    d % 2, c * chunk_rows : c * chunk_rows + size, lane * 128 : (lane + 1) * 128
                ] = flat[c % 2, lane, 0:size, :].astype(BF)
        copy(d).start()
    copy(blocks - 2).wait()
    copy(blocks - 1).wait()


def writer(stage, sems):
    pending = []
    slots = stage.shape[0]

    def write(value, target):
        slot = len(pending) % slots
        if len(pending) >= slots:
            pending[-slots].wait()
        part = stage.at[slot, pl.ds(0, value.shape[0]), pl.ds(0, value.shape[1])]
        part[...] = value
        copy = pltpu.make_async_copy(part, target, sems.at[slot])
        copy.start()
        pending.append(copy)

    def finish():
        for copy in pending[-slots:]:
            copy.wait()

    return write, finish


def unpack_half_kernel(half_ref, dev_ref, *refs, other):
    out_ref, stage, sems = refs[-3:]
    half = half_ref.shape[0]
    write, finish = writer(stage, sems)
    step = half // 4
    side = 1 - dev_ref[2] if other else dev_ref[2]
    for r in range(0, half, step):
        start = pl.multiple_of(side * half + r, 16)
        write(half_ref[r : r + step, :].astype(F32), out_ref.at[pl.ds(start, step), :])
    finish()


def unpack_plain(call, item, numbers, after=()):
    half, width = item.keep.shape
    out = shape((2 * half, width), F32)
    scratch = [pltpu.VMEM((4, half // 4, width), F32), pltpu.SemaphoreType.DMA((4,))]
    first = call(
        functools.partial(unpack_half_kernel, other=False),
        out, [VMEM, SMEM], HBM, scratch, limit=8, after=after,
    )(item.keep, numbers)
    return call(
        functools.partial(unpack_half_kernel, other=True),
        out, [VMEM, SMEM, HBM], HBM, scratch, limit=8, alias={2: 0},
    )(item.got, numbers, first)


def unpack_kernel(
    mine_ref, other_ref, dev_ref, bias_ref, expand_ref, head_ref, jig_ref, score_ref,
    jig_bias_ref, head_bias_ref, rest, stage, sems,
    *, wide,
):
    half, width = mine_ref.shape
    write, finish = writer(stage, sems)
    for ref, side in ((mine_ref, dev_ref[2]), (other_ref, 1 - dev_ref[2])):
        rest[pl.ds(pl.multiple_of(side * half, 16), half), :] = ref[...]
    depth = expand_ref.shape[1]
    for i in range(depth // width):
        for r in range(0, width, 256):
            write(
                rest[i * width + r : i * width + r + 256, :].astype(F32),
                expand_ref.at[pl.ds(r, 256), pl.ds(i * width, width)],
            )
    at = depth
    quarter = depth // 4
    for i in range(4):
        for r in range(0, quarter, 256):
            write(
                rest[at + r : at + r + 256, i * 128 : (i + 1) * 128].astype(F32),
                head_ref.at[pl.ds(i * quarter + r, 256), :],
            )
    at += quarter
    quarter = jig_ref.shape[0] // 4
    for i in range(4):
        write(
            rest[at : at + quarter, i * 128 : (i + 1) * 128].astype(F32),
            jig_ref.at[pl.ds(i * quarter, quarter), :],
        )
    at += quarter
    lines = score_ref.shape[0]
    total = jnp.zeros((lines, width), F32)
    for g in range(wide):
        total = total + jnp.where(
            dev_ref[0] == g, rest[at + g * lines : at + (g + 1) * lines, :].astype(F32), 0.0
        )
    scores = jnp.zeros((lines, 128), F32)
    for j in range(4):
        scores = scores + jnp.where(dev_ref[1] == j, total[:, j * 128 : (j + 1) * 128], 0.0)
    score_ref[...] = scores + bias_ref[...]
    at += wide * lines
    biases = rest[at : at + 16, :].astype(F32)[0:1]
    jig_bias_ref[...] = biases[:, 0:128]
    head_bias_ref[...] = biases[:, 128:256]
    finish()


def shape(dims, dtype):
    return jax.ShapeDtypeStruct(dims, dtype)


def held(dims, dtype):
    return pltpu.VMEM(dims, dtype)


def exchange(payload):
    return lax.all_to_all(payload, AXES, 0, 0)


def device_index():
    return lax.axis_index("wide") * lax.axis_size("narrow") + lax.axis_index("narrow")


def swap(value, bits):
    n = lax.axis_size("wide") * lax.axis_size("narrow")
    return lax.ppermute(value, AXES, [(i, i ^ bits[i % 2]) for i in range(n)])


def side_of(bits):
    me = device_index()
    return (me // jnp.where(me % 2 == 1, bits[1], bits[0])) % 2


def halves(ref, side):
    half = ref.shape[0] // 2
    return ref[pl.ds(pl.multiple_of(side * half, 8), half), :]


def merge_kernel(*refs, plan):
    dev_ref = refs[0]
    inputs = iter(refs[1 : 1 + sum(1 + (kind != "pass") for kind, _ in plan)])
    outputs = iter(refs[1 + sum(1 + (kind != "pass") for kind, _ in plan) :])
    for kind, index in plan:
        mine = next(inputs)
        if kind == "pass":
            target = next(outputs)
            target[...] = mine[...]
            continue
        got = next(inputs)
        if kind == "split":
            side = dev_ref[index]
            keep, send = next(outputs), next(outputs)
            keep[...] = halves(mine, side).astype(F32) + halves(got, side).astype(F32)
            send[...] = (
                halves(mine, 1 - side).astype(F32) + halves(got, 1 - side).astype(F32)
            ).astype(BF)
        elif kind == "sum":
            target = next(outputs)
            target[...] = (mine[...].astype(F32) + got[...].astype(F32)).astype(BF)
        else:
            side = dev_ref[index]
            target = next(outputs)
            half = mine.shape[0]
            target[pl.ds(pl.multiple_of(side * half, 16), half), :] = mine[...]
            target[pl.ds(pl.multiple_of((1 - side) * half, 16), half), :] = got[...]


class Sum:
    def __init__(self, keep, send, pairs, first_side):
        self.keep, self.send, self.pairs, self.sides = keep, send, pairs, first_side
        self.at = 0
        self.got = None
        self.gathering = False

    def exchange(self):
        self.got = swap(self.send, self.pairs[self.at])
        return self.got

    def last(self):
        return self.gathering and self.at == 0

    def kind(self):
        if self.gathering:
            return "join", self.sides + self.at
        if self.at + 1 < len(self.pairs):
            return "split", self.sides + self.at + 1
        return "sum", 0

    def shapes(self):
        rows, width = self.got.shape
        kind = self.kind()[0]
        if kind == "split":
            return [shape((rows // 2, width), F32), shape((rows // 2, width), BF)]
        if kind == "sum":
            return [shape((rows, width), BF)]
        return [shape((2 * rows, width), BF)]

    def take(self, results):
        kind = self.kind()[0]
        if kind == "split":
            self.keep, self.send = results
            self.at += 1
        else:
            self.keep = self.send = results[0]
            if kind == "sum":
                self.gathering = True
            else:
                self.at -= 1


def merge(call, numbers, sums, after=(), flops=0):
    shapes = [item.shapes() for item in sums]
    outs = call(
        functools.partial(merge_kernel, plan=tuple(item.kind() for item in sums)),
        [one for each in shapes for one in each],
        [SMEM] + [VMEM, VMEM] * len(sums),
        [VMEM] * sum(map(len, shapes)),
        after=after,
        flops=flops,
    )(numbers, *(value for item in sums for value in (item.keep, item.got)))
    outs = list(outs)
    for item, each in zip(sums, shapes):
        item.take(outs[: len(each)])
        outs = outs[len(each) :]


def is_in(value, values):
    return any(value is v for v in values)


def kernel_call(
    kernel, out_shape, in_specs, out_specs, scratch=(), limit=6, flops=0, bytes_accessed=0,
    after=(), resident=(), far=(), alias=None,
):
    n_in, n_after = len(in_specs), len(after)
    spare = max(0, lax.axis_size("wide") * lax.axis_size("narrow") // 16 - 2)

    def run(*refs):
        kernel(*refs[:n_in], *refs[n_in + n_after :])

    made = pl.pallas_call(
        run,
        out_shape=out_shape,
        in_specs=list(in_specs) + [HBM if is_in(a, far) else ANY for a in after],
        out_specs=out_specs,
        scratch_shapes=list(scratch),
        input_output_aliases=alias or {},
        compiler_params=pltpu.CompilerParams(vmem_limit_bytes=(limit + spare) << 20),
        cost_estimate=pl.CostEstimate(
            flops=max(1, int(flops)), bytes_accessed=1, transcendentals=0
        ),
    )

    def placed(*args):
        fixed = []
        for a, spec in zip(args, in_specs):
            if spec is HBM:
                a = pltpu.with_memory_space_constraint(a, pltpu.HBM)
            elif spec is VMEM and is_in(a, resident):
                a = pltpu.with_memory_space_constraint(a, pltpu.VMEM)
            fixed.append(a)
        for a in after:
            fixed.append(pltpu.with_memory_space_constraint(a, pltpu.HBM) if is_in(a, far) else a)
        outs = made(*fixed)
        if isinstance(out_shape, list):
            for made_shape, spec, out in zip(out_shape, out_specs, outs):
                if not isinstance(made_shape, jax.ShapeDtypeStruct):
                    resident.append(out)
                if spec is HBM:
                    far.append(out)
        elif out_specs is HBM:
            far.append(outs)
        return outs

    return placed


def body(
    block_in,
    weight_reduce,
    gain_reduce,
    shift_reduce,
    weight_spatial,
    gain_spatial,
    shift_spatial,
    weight_expand,
    gain_expand,
    shift_expand,
    head_weight,
    head_bias,
    jigsaw_weight,
    jigsaw_bias,
    resolution,
    tile_slot,
    jigsaw_perm,
    cotangent,
):
    rows, depth = block_in.shape
    width = weight_reduce.shape[1]
    tiles = rows // PIX
    chunks = -(-tiles // CHUNK)
    padded = chunks * CHUNK
    chunk_rows = CHUNK * PIX
    wide, narrow = lax.axis_size("wide"), lax.axis_size("narrow")
    n = wide * narrow
    images = jigsaw_perm.shape[0]
    own = images // narrow
    unit = 16 * n
    assert images // 4 == own
    wide_rank, narrow_rank = lax.axis_index("wide"), lax.axis_index("narrow")
    slots = lax.dynamic_slice_in_dim(tile_slot, narrow_rank * tiles, tiles, 1)
    slots = jnp.pad(slots, ((0, 0), (0, padded - tiles)), constant_values=-1)
    bits = [1 << i for i in range(n.bit_length() - 1)]
    axes = {"y": bits[1:2], "x": bits[2:3], "0": bits[3:4], "1": bits[4:]}

    even, odd = (
        bits[:1] + sum((axes[a] for a in order), []) for order in ("xy01", "yx01")
    )
    pairs = list(zip(even, odd))

    first_side = 2
    dev = jnp.stack(
        [wide_rank, narrow_rank]
        + [side_of(b) for b in pairs]
    ).astype(jnp.int32)
    row = lambda v: v.reshape(1, -1)
    block3 = lambda last, dtype: held((chunks, chunk_rows, last), dtype)
    call = functools.partial(kernel_call, resident=[], far=[])
    flops = 2 * padded * PIX * width * depth

    xp, pre_one, pay, mask, pick, back_emb, count, biases = call(
        functools.partial(reduce_kernel, tiles=tiles, own=own),
        [
            block3(depth, BF),
            block3(width, F32),
            shape((n, 2, width), F32),
            held((3, padded, 128), F32),
            held((PIX * images, padded), BF),
            held((padded, 128), BF),
            held((8, 128), F32),
            held((1, width), F32),
        ],
        [HBM, HBM, VMEM, VMEM, HBM, HBM, HBM, SMEM],
        [VMEM] * 8,
        [
            pltpu.VMEM((2, rows, 512), BF),
            pltpu.VMEM((2, 512, width), BF),
            pltpu.VMEM((2, 4, chunk_rows, 128), F32),
            pltpu.VMEM((PIX, images), jnp.int32),
            pltpu.VMEM(cotangent.shape, BF),
            pltpu.VMEM(jigsaw_weight.shape, BF),
            pltpu.SemaphoreType.DMA((2,)),
            pltpu.SemaphoreType.DMA((2,)),
            pltpu.SemaphoreType.DMA((3,)),
        ],
        limit=12,
        flops=flops,
    )(block_in, weight_reduce, slots, row(resolution), jigsaw_perm.T, cotangent, jigsaw_weight, dev)

    offset_scratch = [pltpu.VMEM((PIX, width, width), BF), pltpu.SemaphoreType.DMA((PIX,))]
    w_spatial = weight_spatial.reshape(PIX, width, width)
    hid_one, pre_two, pay, stat_one = call(
        spatial_kernel,
        [
            block3(width, BF),
            block3(width, F32),
            shape((n, 2, width), F32),
            held((8, width), F32),
        ],
        [VMEM, VMEM, HBM] + [VMEM] * 4,
        [VMEM] * 4,
        offset_scratch,
        flops=flops * 1.4,
        limit=12,
    )(exchange(pay), pre_one, w_spatial, row(gain_reduce), row(shift_reduce), mask, count)

    hid_two, gram, pay, stat_two = call(
        expand_kernel,
        [
            block3(width, BF),
            held((width, depth), BF),
            shape((n, 2, (width + depth) // 2), F32),
            held((8, width), F32),
        ],
        [VMEM] * 7,
        [VMEM] * 4,
        flops=flops,
    )(exchange(pay), pre_two, weight_expand, row(gain_spatial), row(shift_spatial), mask, count)

    block_out, dy_three, up, part, emb, head, pay, stat_three = call(
        functools.partial(output_kernel, rows=rows),
        [
            shape((rows, depth), BF),
            block3(depth, BF),
            block3(width, F32),
            held((width, depth), F32),
            held((padded, 128), F32),
            held((depth, 128), BF),
            shape((n, 2, depth), BF),
            held((8, depth), F32),
        ],
        [VMEM] * 10,
        [HBM] + [VMEM] * 7,
        [
            pltpu.VMEM((2, chunk_rows, 256), F32),
            pltpu.VMEM((2, 2, chunk_rows, 128), F32),
            pltpu.VMEM((2, rows, 256), BF),
            pltpu.VMEM((chunks, chunk_rows, 256), BF),
            pltpu.VMEM((chunks, chunk_rows, 256), BF),
            pltpu.VMEM((2, padded, 256), BF),
            pltpu.VMEM((2, SUB, 256), F32),
            pltpu.SemaphoreType.DMA((2,)),
        ],
        flops=flops * 4,
        limit=14,
    )(
        exchange(pay), hid_two, xp, weight_expand, row(gain_expand), row(shift_expand),
        head_weight, back_emb, mask, count,
    )

    lines = images // 4
    pay = exchange(pay)
    used = depth + depth // 4 + PIX * 128 // 4 + wide * lines + 16
    grad_rows = -(-used // unit) * unit
    keep, send = call(
        functools.partial(expand_grad_kernel, wide=wide),
        [shape((grad_rows // 2, width), BF)] * 2,
        [VMEM] * 13 + [SMEM],
        [VMEM] * 2,
    )(
        pay, stat_three, count, stat_two, part, gram, head,
        emb, row(head_bias), pick, jigsaw_weight, cotangent, biases, dev,
    )
    one = Sum(keep, send, pairs, first_side)
    one.exchange()
    long = 10**11
    gain_three, shift_three, dy_two, packed = call(
        expand_back_kernel,
        [shape((1, depth), F32)] * 2 + [block3(width, F32), shape((2, width), F32)],
        [VMEM] * 9,
        [VMEM] * 4,
        after=(one.send,),
        flops=long,
    )(pay, stat_three, up, hid_two, weight_expand, pre_two, stat_two, mask, count)

    def send_packed(packed, after):
        return exchange(
            call(payload_kernel, shape((n, 2, width), F32), [VMEM], VMEM, after=after)(packed)
        )

    pay = send_packed(packed, (one.got,))
    merge(call, dev, [one], (pay,))
    one.exchange()

    spatial_rows = -(-(PIX * width) // unit) * unit
    back_spatial, keep, send, gain_two, shift_two = call(
        spatial_grad_kernel,
        [
            block3(width, BF),
            shape((spatial_rows // 2, width), BF),
            shape((spatial_rows // 2, width), BF),
            shape((1, width), F32),
            shape((1, width), F32),
        ],
        [VMEM] * 7 + [SMEM],
        [VMEM] * 5,
        after=(one.send,),
        flops=long,
    )(pay, stat_two, pre_two, dy_two, hid_one, mask, count, dev)
    two = Sum(keep, send, pairs, first_side)
    two.exchange()
    merge(call, dev, [one], (back_spatial,))
    one.exchange()
    partial = call(
        spatial_back_kernel,
        [block3(width, F32)],
        [VMEM, VMEM],
        [VMEM],
        after=(two.send, one.send),
        flops=long,
    )(back_spatial, w_spatial)[0]
    merge(call, dev, [one, two], (partial,))
    one.exchange()
    two.exchange()
    dy_one, packed = call(
        spatial_back_end_kernel,
        [block3(width, F32), shape((2, width), F32)],
        [VMEM] * 6,
        [VMEM] * 2,
        after=(one.send, two.send),
        alias={5: 0},
        flops=long,
    )(back_spatial, w_spatial, pre_one, stat_one, mask, partial)
    pay = send_packed(packed, (one.got,))
    merge(call, dev, [one, two], (pay,))
    one.exchange()
    two.exchange()
    back_reduce, keep, send, gain_one, shift_one = call(
        reduce_grad_kernel,
        [
            block3(width, BF),
            shape((depth // 2, width), BF),
            shape((depth // 2, width), BF),
            shape((1, width), F32),
            shape((1, width), F32),
        ],
        [VMEM] * 7 + [SMEM],
        [VMEM] * 5,
        flops=long,
        after=(one.send, two.send),
    )(pay, stat_one, pre_one, dy_one, xp, mask, count, dev)
    three = Sum(keep, send, pairs, first_side)
    three.exchange()
    merge(call, dev, [one, two], (back_reduce,))
    one.exchange()
    two.exchange()
    gradient_input = call(
        functools.partial(input_kernel, rows=rows),
        shape((rows, depth), BF),
        [VMEM] * 3,
        HBM,
        [
            pltpu.VMEM((2, 4, chunk_rows, 128), F32),
            pltpu.VMEM((2, rows, 512), BF),
            pltpu.SemaphoreType.DMA((2,)),
        ],
        flops=long,
        limit=8,
        after=(one.send, two.send),
    )(back_reduce, weight_reduce, dy_three)

    sums = {"E": one, "S": two, "R": three}
    turns = "SRESERSERSRERSRERESRSRR" if len(bits) == 5 else "SRE" * (3 * len(bits))
    late = gradient_input
    for turn in turns:
        item = sums.get(turn)
        if item is None:
            continue
        if not item.last():
            merge(call, dev, [item], (late,), long // 20)
            item.exchange()
            late = item.send
            continue
        del sums[turn]
        if turn == "E":
            gradient_expand, gradient_head, gradient_jigsaw, scores, jig_total, head_total = call(
                functools.partial(unpack_kernel, wide=wide),
                [
                    shape((width, depth), F32),
                    shape((depth, 128), F32),
                    shape((PIX * 128, 128), F32),
                    shape((lines, 128), F32),
                    shape((1, 128), F32),
                    shape((1, 128), F32),
                ],
                [VMEM, VMEM, SMEM, VMEM],
                [HBM] * 3 + [VMEM] * 3,
                [
                    pltpu.VMEM((grad_rows, width), BF),
                    pltpu.VMEM((8, 288, width), F32),
                    pltpu.SemaphoreType.DMA((8,)),
                ],
                limit=max(12, grad_rows // 512 + 8),
                after=(late,),
            )(one.keep, one.got, dev, row(jigsaw_bias))
            late = gradient_expand
        elif turn == "S" and spatial_rows != PIX * width:
            low = side_of(two.pairs[0]) == 0
            gradient_spatial = jnp.concatenate(
                [jnp.where(low, two.keep, two.got), jnp.where(low, two.got, two.keep)]
            )[: PIX * width].astype(F32)
        elif turn == "S":
            gradient_spatial = late = unpack_plain(call, two, dev, (late,))
        else:
            gradient_reduce = late = unpack_plain(call, three, dev, (late,))
    return (
        block_out,
        scores,
        gradient_input,
        gradient_reduce,
        gain_one.reshape(-1),
        shift_one.reshape(-1),
        gradient_spatial,
        gain_two.reshape(-1),
        shift_two.reshape(-1),
        gradient_expand,
        gain_three.reshape(-1),
        shift_three.reshape(-1),
        gradient_head,
        head_total.reshape(-1),
        gradient_jigsaw,
        jig_total.reshape(-1),
    )


def solution(mesh):
    placed = (P(AXES, None),) + (P(),) * 14 + (P("wide", None),) * 3
    return jax.shard_map(
        body,
        mesh=mesh,
        in_specs=placed,
        out_specs=(P(AXES, None),) * 3 + (P(),) * 13,
        check_vma=False,
    )
```

```python
import functools

import jax
import jax.numpy as jnp
from jax import lax
from jax.experimental import pallas as pl
from jax.experimental.pallas import tpu as pltpu
from jax.sharding import PartitionSpec as P

BF = jnp.bfloat16
F32 = jnp.float32
EPS = 1e-05
AXES = ("wide", "narrow")
PIX = 9
CHUNK = 48
SUB = 16
C1 = 0.7978845608028654
C2 = C1 * 0.044715
VMEM = pl.BlockSpec(memory_space=pltpu.VMEM)
HBM = pl.BlockSpec(memory_space=pltpu.HBM)
SMEM = pl.BlockSpec(memory_space=pltpu.SMEM)
ANY = pl.BlockSpec(memory_space=pl.ANY)


def dot(a, b, ca=1, cb=0):
    return lax.dot_general(a, b, (((ca,), (cb,)), ((), ())), preferred_element_type=F32)


def dot_rows(row, b, cb=0):
    high = row.astype(BF)
    rest = row - high.astype(F32)
    mid = rest.astype(BF)
    low = (rest - mid.astype(F32)).astype(BF)
    stack = jnp.concatenate([high, mid, low, jnp.zeros((13, row.shape[1]), BF)], 0)
    return jnp.sum(dot(stack, b, 1, cb), 0, keepdims=True)


def spread(mask, width):
    return jnp.concatenate([mask] * (width // 128), 1)


def gelu(v):
    squared = v * v
    half = 0.5 * v
    return half + half * jnp.tanh(v * (C1 + C2 * squared))


def gelu_both(v):
    squared = v * v
    gate = 0.5 * jnp.tanh(v * (C1 + C2 * squared)) + 0.5
    value = v * gate
    return value, gate + value * (1.0 - gate) * (2.0 * C1 + 6.0 * C2 * squared)


def gelu_slope(v):
    return gelu_both(v)[1]


def spans(offset):
    down, right = offset // 3 - 1, offset % 3 - 1
    rows = [r for r in range(3) if 0 <= r + down < 3]
    if right == 0:
        return [(rows[0] * 3, (rows[0] + down) * 3, 3 * len(rows))]
    start = max(0, -right)
    return [(r * 3 + start, (r + down) * 3 + start + right, 2) for r in rows]


OFFSETS = (4, 1, 7, 3, 5, 0, 2, 6, 8)


def places(ref, first, count):
    chunks, _, width = ref.shape
    return ref[:, first * CHUNK : (first + count) * CHUNK, :].reshape(
        chunks * count * CHUNK, width
    )


def add_places(ref, first, count, value, start):
    chunks, _, width = ref.shape
    rows = pl.ds(first * CHUNK, count * CHUNK)
    value = value.reshape(chunks, count * CHUNK, width)
    if start:
        ref[:, rows, :] = value
    else:
        ref[:, rows, :] = ref[:, rows, :] + value


def put(keep, send, side, start, value, lane=0):
    half = keep.shape[0]
    lanes = slice(lane, lane + value.shape[1])
    for i in range(2):
        low, high = max(start, i * half), min(start + value.shape[0], (i + 1) * half)
        if low < high:
            piece = value[low - start : high - start]
            rows = slice(low - i * half, high - i * half)

            @pl.when(side == i)
            def _():
                keep[rows, lanes] = piece

            @pl.when(side != i)
            def _():
                send[rows, lanes] = piece


def moments(payload, count):
    total = jnp.sum(payload[...], 0)
    mean = total[0:1] / count
    inv = lax.rsqrt(total[1:2] / count - mean * mean + EPS)
    return total, mean, inv


def reduce_kernel(
    x_ref, w_ref, slots_ref, res_ref, perm_ref, cot_ref, jw_ref, dev_ref,
    xp_ref, pre_ref, pay_ref, mask_ref, pick_ref, back_ref, count_ref, bias_ref,
    buf, wbuf, flat, perm_buf, cot_buf, jw_buf, sems, wsems, ssems, *, tiles, own,
):
    rows, depth = x_ref.shape
    chunks, chunk_rows, _ = xp_ref.shape
    padded = chunks * CHUNK
    block = buf.shape[2]
    blocks = depth // block
    lanes = block // 128

    def copy(d):
        return pltpu.make_async_copy(
            x_ref.at[:, pl.ds(d * block, block)], buf.at[d % 2], sems.at[d % 2]
        )

    def copy_w(d):
        return pltpu.make_async_copy(
            w_ref.at[pl.ds(d * block, block), :], wbuf.at[d % 2], wsems.at[d % 2]
        )

    small = [
        pltpu.make_async_copy(source, target, ssems.at[i])
        for i, (source, target) in enumerate(
            ((perm_ref, perm_buf), (cot_ref, cot_buf), (jw_ref, jw_buf))
        )
    ]
    for one in small:
        one.start()
    for d in range(2):
        copy(d).start()
        copy_w(d).start()
    ids = slots_ref[...]
    image = lax.shift_right_arithmetic(ids * 7282, 16)
    piece = ids - 9 * image
    images = perm_ref.shape[1]
    here = jnp.where(image < 0, -1, image + dev_ref[0] * images)
    all_images = res_ref.shape[1]
    hit_all = lax.broadcasted_iota(jnp.int32, (all_images, padded), 0) == here
    res = res_ref[...].astype(F32)
    flags = dot(
        jnp.broadcast_to(res, (16, all_images)).astype(BF), jnp.where(hit_all, 1.0, 0.0).astype(BF)
    )[0:1]
    eye = lax.broadcasted_iota(jnp.int32, (padded, padded), 0) == lax.broadcasted_iota(
        jnp.int32, (padded, padded), 1
    )
    large = dot(jnp.where(eye, flags, 0.0).astype(BF), jnp.ones((padded, 128), BF))
    exists = lax.broadcasted_iota(jnp.int32, (padded, 128), 0) < tiles
    mask_ref[0] = jnp.where(exists, 1.0, 0.0)
    mask_ref[1] = large
    mask_ref[2] = 1.0 / (4.0 + 5.0 * large)
    total = 9.0 * (4.0 * all_images + 5.0 * jnp.sum(res, 1, keepdims=True))
    count_ref[...] = jnp.broadcast_to(total, (8, 128))
    for one in small:
        one.wait()
    perm_ref, cot_ref, jw_ref = perm_buf, cot_buf, jw_buf
    hit = lax.broadcasted_iota(jnp.int32, (images, padded), 0) == image
    rows_back = dot(cot_ref[...], jw_ref[...], 1, 1).astype(BF)
    back = jnp.zeros((padded, 128), F32)
    small_eye = lax.broadcasted_iota(jnp.int32, (images, images), 0) == lax.broadcasted_iota(
        jnp.int32, (images, images), 1
    )
    perm = dot(jnp.where(small_eye, 1.0, 0.0).astype(BF), perm_ref[...].astype(F32).astype(BF), 1, 1)
    piece = piece.astype(F32)
    for k in range(PIX):
        chosen = jnp.where(hit & (perm[:, k : k + 1] == piece), 1.0, 0.0).astype(BF)
        pick_ref[k * images : (k + 1) * images, :] = chosen
        back = back + dot(chosen, rows_back[:, k * 128 : (k + 1) * 128], 0, 0)
    back = back.astype(BF)
    back_ref[...] = back
    tail = rows - (chunks - 1) * chunk_rows

    def product(d):
        part = dot(
            xp_ref[:, :, d * block : (d + 1) * block].reshape(chunks * chunk_rows, block),
            wbuf[d % 2],
        ).reshape(pre_ref.shape)
        pre_ref[...] = part if d == 0 else pre_ref[...] + part

    for d in range(blocks):
        copy(d).wait()
        if d > 0:
            copy_w(d - 1).wait()
            product(d - 1)
        cols = slice(d * block, (d + 1) * block)
        for c in range(chunks):
            size = chunk_rows if c + 1 < chunks else tail
            for lane in range(lanes):
                flat[c % 2, lane, 0:size, :] = buf[
                    d % 2, c * chunk_rows : c * chunk_rows + size, lane * 128 : (lane + 1) * 128
                ].astype(F32)
                if size < chunk_rows:
                    flat[c % 2, lane, size:, :] = jnp.zeros((chunk_rows - size, 128), F32)
            for p in range(PIX):
                xp_ref[c, p * CHUNK : (p + 1) * CHUNK, cols] = jnp.concatenate(
                    [flat[c % 2, lane, pl.ds(p, CHUNK, stride=PIX), :] for lane in range(lanes)], 1
                ).astype(BF)
        if d + 2 < blocks:
            copy(d + 2).start()
        if 0 < d < blocks - 1:
            copy_w(d + 1).start()
    copy_w(blocks - 1).wait()
    product(blocks - 1)
    width = pre_ref.shape[2]

    def sums(c, carry):
        first, second = carry
        for p in range(PIX):
            a = pre_ref[c, p * CHUNK : (p + 1) * CHUNK, :]
            if p not in (0, 1, 3, 4):
                m = spread(mask_ref[1, pl.ds(pl.multiple_of(c * CHUNK, CHUNK), CHUNK), :], width)
                a = a * m
            first = first + jnp.sum(a.reshape(CHUNK // 8, 8, width), 0)
            second = second + jnp.sum((a * a).reshape(CHUNK // 8, 8, width), 0)
        return first, second

    zero = jnp.zeros((8, width), F32)
    first, second = lax.fori_loop(0, chunks, sums, (zero, zero))
    own_cot = jnp.where(
        lax.broadcasted_iota(jnp.int32, cot_ref.shape, 0) // own == dev_ref[1],
        cot_ref[...].astype(F32),
        0.0,
    )
    biases = jnp.concatenate(
        [
            jnp.sum(own_cot, 0, keepdims=True),
            jnp.sum(back.astype(F32), 0, keepdims=True),
            jnp.zeros((1, width - 256), F32),
        ],
        1,
    )
    bias_ref[...] = biases
    packed = jnp.concatenate(
        [jnp.sum(first, 0, keepdims=True), jnp.sum(second, 0, keepdims=True)], 0
    )
    pay_ref[...] = jnp.broadcast_to(packed[None], pay_ref.shape)


def masks(mask_ref, c, p, width):
    kind = 0 if p in (0, 1, 3, 4) else 1
    return spread(mask_ref[kind, pl.ds(pl.multiple_of(c * CHUNK, CHUNK), CHUNK), :], width)


def load_offsets(w_ref, wbuf, sems):
    loads = {k: pltpu.make_async_copy(w_ref.at[k], wbuf.at[k], sems.at[k]) for k in OFFSETS}
    for k in OFFSETS:
        loads[k].start()
    return loads


def spatial_kernel(
    pay_ref, pre_ref, w_ref, gain_ref, shift_ref, mask_ref, count_ref,
    hid_ref, out_ref, next_ref, stat_ref, wbuf, sems,
):
    chunks, chunk_rows, width = pre_ref.shape
    loads = load_offsets(w_ref, wbuf, sems)
    count = count_ref[0:1, 0:1]
    total, mean, inv = moments(pay_ref, count)
    scale = gain_ref[...] * inv
    base = shift_ref[...] - mean * scale
    stat_ref[...] = jnp.concatenate([mean, inv, scale, base, jnp.zeros((4, width), F32)], 0)

    def act(c, _):
        for p in range(PIX):
            rows = slice(p * CHUNK, (p + 1) * CHUNK)
            a = pre_ref[c, rows, :] * scale + base
            hid_ref[c, rows, :] = (gelu(a) * masks(mask_ref, c, p, width)).astype(BF)
        return 0

    lax.fori_loop(0, chunks, act, 0)
    for k in OFFSETS:
        loads[k].wait()
    for k in OFFSETS:
        for first_out, first_in, n in spans(k):
            for s in range(0, n, 3):
                m = min(3, n - s)
                part = dot(places(hid_ref, first_in + s, m), wbuf[k])
                add_places(out_ref, first_out + s, m, part, k == OFFSETS[0])

    def sums(c, carry):
        first, second = carry
        for p in range(PIX):
            a = out_ref[c, p * CHUNK : (p + 1) * CHUNK, :]
            if p not in (0, 1, 3, 4):
                a = a * masks(mask_ref, c, p, width)
            first = first + jnp.sum(a.reshape(CHUNK // 8, 8, width), 0)
            second = second + jnp.sum((a * a).reshape(CHUNK // 8, 8, width), 0)
        return first, second

    zero = jnp.zeros((8, width), F32)
    first, second = lax.fori_loop(0, chunks, sums, (zero, zero))
    packed = jnp.concatenate(
        [jnp.sum(first, 0, keepdims=True), jnp.sum(second, 0, keepdims=True)], 0
    )
    next_ref[...] = jnp.broadcast_to(packed[None], next_ref.shape)


def expand_kernel(
    pay_ref, pre_ref, w_ref, gain_ref, shift_ref, mask_ref, count_ref,
    hid_ref, gram_ref, next_ref, stat_ref,
):
    chunks, chunk_rows, width = pre_ref.shape
    depth = w_ref.shape[1]
    count = count_ref[0:1, 0:1]
    _, mean, inv = moments(pay_ref, count)
    scale = gain_ref[...] * inv
    base = shift_ref[...] - mean * scale

    def act(c, column):
        for p in range(PIX):
            rows = slice(p * CHUNK, (p + 1) * CHUNK)
            a = pre_ref[c, rows, :] * scale + base
            h = (gelu(a) * masks(mask_ref, c, p, width)).astype(BF)
            hid_ref[c, rows, :] = h
            column = column + jnp.sum(h.astype(F32).reshape(CHUNK // 8, 8, width), 0)
        return column

    column = lax.fori_loop(0, chunks, act, jnp.zeros((8, width), F32))
    column = jnp.sum(column, 0, keepdims=True)
    stat_ref[...] = jnp.concatenate(
        [mean, inv, scale, base, column, jnp.zeros((3, width), F32)], 0
    )
    flat = hid_ref[...].reshape(chunks * chunk_rows, width)
    gram = dot(flat, flat, 0, 0)
    high = gram.astype(BF)
    low = (gram - high.astype(F32)).astype(BF)
    block = width
    packed = [column]
    for d in range(0, depth, block):
        w = w_ref[:, d : d + block]
        product = dot(high, w) + dot(low, w)
        gram_ref[:, d : d + block] = product.astype(BF)
        second = jnp.sum(product * w.astype(F32), 0, keepdims=True)
        packed.append(second)
    packed = jnp.concatenate(packed, 1)
    half = packed.shape[1] // 2
    packed = jnp.concatenate([packed[:, :half], packed[:, half:]], 0)
    next_ref[...] = jnp.broadcast_to(packed[None], next_ref.shape)


def output_kernel(
    pay_ref, hid_ref, xp_ref, w_ref, gain_ref, shift_ref, hw_ref, back_ref, mask_ref, count_ref,
    out_ref, dy_ref, up_ref, part_ref, emb_ref, head_ref, next_ref, stat_ref,
    pre, flat, obuf, dy_even, dy_odd, pool_ref, first_ref, sems, *, rows,
):
    chunks, chunk_rows, depth = xp_ref.shape
    width = hid_ref.shape[2]
    block = pre.shape[2]
    lanes = block // 128
    blocks = depth // block
    tail = rows - (chunks - 1) * chunk_rows
    count = count_ref[0:1, 0:1]

    def copy(d, slot):
        return pltpu.make_async_copy(
            obuf.at[slot], out_ref.at[:, pl.ds(pl.multiple_of(d * block, block), block)], sems.at[slot]
        )

    total = jnp.sum(pay_ref[...], 0)
    total = jnp.concatenate([total[0:1], total[1:2]], 1)
    mean_all = dot_rows(total[:, :width], w_ref[...]) / count
    square_all = total[:, width:] / count
    inv_all = lax.rsqrt(square_all - mean_all * mean_all + EPS)
    scale_all = gain_ref[...] * inv_all
    stat_ref[...] = jnp.concatenate(
        [
            mean_all,
            inv_all,
            scale_all,
            shift_ref[...] - mean_all * scale_all,
            jnp.concatenate([total[:, :width] / count, jnp.zeros((1, depth - width), F32)], 1),
            jnp.zeros((3, depth), F32),
        ],
        0,
    )
    dy_bufs = (dy_even, dy_odd)
    up_ref[...] = jnp.zeros(up_ref.shape, F32)
    emb_ref[...] = jnp.zeros(emb_ref.shape, F32)
    cells = spread(mask_ref[2], block)

    def columns(d):
        return pl.ds(pl.multiple_of(d * block, block), block)

    def forward(d, slot):
        dy_buf = dy_bufs[slot]
        cols = columns(d)
        scale = stat_ref[2:3, cols]
        base = stat_ref[3:4, cols]
        w = w_ref[:, cols]
        back_pool = dot(back_ref[...], hw_ref[cols, :], 1, 1) * cells
        back_large = back_pool * spread(mask_ref[1], block)
        pools = []
        first = jnp.zeros((SUB, block), F32)
        for c in range(chunks):
            pre[c % 2] = dot(hid_ref[c], w)
            for s in range(0, CHUNK, SUB):
                pool = jnp.zeros((SUB, block), F32)
                bp_small = back_pool[c * CHUNK + s : c * CHUNK + s + SUB]
                bp_large = back_large[c * CHUNK + s : c * CHUNK + s + SUB]
                m_large = spread(mask_ref[1, c * CHUNK + s : c * CHUNK + s + SUB, :], block)
                for p in range(PIX):
                    at = p * CHUNK + s
                    v = (
                        pre[c % 2, at : at + SUB, :] * scale
                        + base
                        + xp_ref[c, at : at + SUB, cols].astype(F32)
                    )
                    value, slope = gelu_both(v)
                    if p in (0, 1, 3, 4):
                        dy = slope * bp_small
                    else:
                        value = value * m_large
                        dy = slope * bp_large
                    pool = pool + value
                    first = first + dy
                    dy = dy.astype(BF)
                    dy_ref[c, at : at + SUB, cols] = dy
                    dy_buf[c, at : at + SUB, :] = dy
                    for lane in range(lanes):
                        flat[c % 2, lane, pl.ds(s * PIX + p, SUB, stride=PIX), :] = value[
                            :, lane * 128 : (lane + 1) * 128
                        ]
                pools.append(pool)
            size = chunk_rows if c + 1 < chunks else tail
            for lane in range(lanes):
                obuf[
                    slot, c * chunk_rows : c * chunk_rows + size, lane * 128 : (lane + 1) * 128
                ] = flat[c % 2, lane, 0:size, :].astype(BF)
        pool_ref[slot] = (jnp.concatenate(pools, 0) * cells).astype(BF)
        first_ref[slot] = first

    def backward(d, slot):
        dy_buf = dy_bufs[slot]
        cols = columns(d)
        w = w_ref[:, cols].astype(F32)
        scaled = (w * stat_ref[2:3, cols]).astype(BF)
        for c in range(chunks):
            up_ref[c] = up_ref[c] + dot(dy_buf[c], scaled, 1, 1)
        dy = dy_buf[...].reshape(chunks * chunk_rows, block)
        part = dot(hid_ref[...].reshape(chunks * chunk_rows, width), dy, 0, 0)
        part_ref[:, cols] = part
        first = jnp.sum(first_ref[slot], 0, keepdims=True)
        second = stat_ref[1:2, cols] * (
            jnp.sum(part * w, 0, keepdims=True) - stat_ref[0:1, cols] * first
        )
        next_ref[:, :, cols] = jnp.broadcast_to(
            jnp.concatenate([second, first], 0).astype(BF)[None], (next_ref.shape[0], 2, block)
        )
        pooled = pool_ref[slot]
        emb_ref[...] = emb_ref[...] + dot(pooled, hw_ref[cols, :])
        head_ref[cols, :] = dot(pooled, back_ref[...], 0, 0).astype(BF)

    def pair(i, _):
        for slot in range(2):
            d = 2 * i + slot
            copy(d - 2, slot).wait()
            backward(d - 1, 1 - slot)
            forward(d, slot)
            copy(d, slot).start()
        return 0

    forward(0, 0)
    copy(0, 0).start()
    backward(0, 0)
    forward(1, 1)
    copy(1, 1).start()
    lax.fori_loop(1, blocks // 2, pair, 0)
    backward(blocks - 1, 1)
    copy(blocks - 2, 0).wait()
    copy(blocks - 1, 1).wait()


def backward_terms(pay_ref, stat_ref, count):
    total = jnp.sum(pay_ref[...].astype(F32), 0)
    dgain, dshift = total[0:1], total[1:2]
    mean, inv, scale = stat_ref[0:1], stat_ref[1:2], stat_ref[2:3]
    slope = scale * inv * dgain / count
    level = scale * dshift / count - mean * slope
    return total, scale, slope, level


def expand_back_kernel(
    pay_ref, stat_ref, up_ref, hid_ref, w_ref,
    pre_ref, stat2_ref, mask_ref, count_ref,
    tot_ref, dy_ref, next_ref,
):
    chunks, chunk_rows, width = pre_ref.shape
    depth = w_ref.shape[1]
    count = count_ref[0:1, 0:1]
    total, scale, slope, level = backward_terms(pay_ref, stat_ref, count)
    tot_ref[...] = total
    cross = jnp.zeros((width, width), F32)
    block = 512
    per_std = stat_ref[1:2] * total[0:1] / count
    per_row = total[1:2] / count
    constant = jnp.zeros((1, width), F32)
    for d in range(0, depth, block):
        cols = slice(d, d + block)
        w = w_ref[:, cols].astype(F32)
        scaled = (w * scale[:, cols]).astype(BF)
        cross = cross + dot((w * per_std[:, cols]).astype(BF), scaled, 1, 1)
        constant = constant + dot_rows(per_row[:, cols], scaled, 1)
    cross = cross.astype(BF)
    constant = constant - dot_rows(stat_ref[4:5, :width], cross)
    mean2, inv2, scale2, base2 = (stat2_ref[i : i + 1] for i in range(4))

    def step(c, carry):
        first, second = carry
        fix = dot(hid_ref[c], cross)
        for p in range(PIX):
            rows = slice(p * CHUNK, (p + 1) * CHUNK)
            a = pre_ref[c, rows, :]
            g = up_ref[c, rows, :] - fix[rows] - constant
            dy = gelu_slope(a * scale2 + base2) * g * masks(mask_ref, c, p, width)
            dy_ref[c, rows, :] = dy
            first = first + jnp.sum(dy.reshape(CHUNK // 8, 8, width), 0)
            second = second + jnp.sum(
                (dy * ((a - mean2) * inv2)).reshape(CHUNK // 8, 8, width), 0
            )
        return first, second

    zero = jnp.zeros((8, width), F32)
    first, second = lax.fori_loop(0, chunks, step, (zero, zero))
    packed = jnp.concatenate(
        [jnp.sum(second, 0, keepdims=True), jnp.sum(first, 0, keepdims=True)], 0
    )
    next_ref[...] = packed


def expand_grad_kernel(
    pay_ref, stat_ref, count_ref, stat2_ref, part_ref, gram_ref, head_ref,
    emb_ref, hb_ref, pick_ref, jw_ref, cot_ref, bias_ref, dev_ref,
    keep_ref, send_ref, *, wide,
):
    width, depth = part_ref.shape
    put_rows = functools.partial(put, keep_ref, send_ref, dev_ref[2])
    _, scale, slope, level = backward_terms(pay_ref, stat_ref, count_ref[0:1, 0:1])
    tall = dot_rows_t(stat2_ref[4:5], level)
    block = 512
    at = 0
    for d in range(0, depth, block):
        cols = slice(d, d + block)
        grad = (
            part_ref[:, cols] * scale[:, cols]
            - tall[:, cols]
            - gram_ref[:, cols].astype(F32) * slope[:, cols]
        )
        put_rows(at, grad.astype(BF))
        at += width
    embedded = (emb_ref[...] + hb_ref[...]).astype(BF)
    images = cot_ref.shape[0]
    ordered = dot(pick_ref[...], embedded).astype(BF)
    scores = jnp.zeros((images, 128), F32)
    jigs = []
    for k in range(PIX):
        mine = ordered[k * images : (k + 1) * images]
        scores = scores + dot(mine, jw_ref[k * 128 : (k + 1) * 128, :])
        jigs.append(dot(mine, cot_ref[...], 0, 0).astype(BF))
    lines = images // 4
    scores = jnp.concatenate([scores[i * lines : (i + 1) * lines] for i in range(4)], 1)
    for value in (head_ref[...], jnp.concatenate(jigs, 0)):
        quarter = value.shape[0] // 4
        for i in range(4):
            put_rows(at, value[i * quarter : (i + 1) * quarter], i * 128)
        at += quarter
    left = 2 * keep_ref.shape[0] - at - wide * lines
    scores = [jnp.where(dev_ref[0] == g, scores, 0.0) for g in range(wide)]
    scores += [bias_ref[...], jnp.zeros((left - 1, width), F32)]
    put_rows(at, jnp.concatenate(scores, 0).astype(BF))


def dot_rows_t(column, row):
    n = column.shape[1]
    m = row.shape[1]
    tall = jnp.transpose(jnp.broadcast_to(column, (8, n)))[:, 0:1]
    return tall * jnp.broadcast_to(row, (n, m))


def spatial_grad_kernel(
    pay_ref, stat_ref, pre_ref, dy_ref, hid_ref, mask_ref, count_ref,
    dev_ref, back_ref, keep_ref, send_ref, tot_ref,
):
    chunks, chunk_rows, width = pre_ref.shape
    count = count_ref[0:1, 0:1]
    total, scale, slope, level = backward_terms(pay_ref, stat_ref, count)
    tot_ref[...] = total

    def step(c, _):
        for p in range(PIX):
            rows = slice(p * CHUNK, (p + 1) * CHUNK)
            b = dy_ref[c, rows, :] * scale - level - pre_ref[c, rows, :] * slope
            back_ref[c, rows, :] = (b * masks(mask_ref, c, p, width)).astype(BF)
        return 0

    lax.fori_loop(0, chunks, step, 0)
    for k in range(PIX):
        runs = spans(k)
        grad = dot(
            jnp.concatenate([places(hid_ref, first_in, n) for _, first_in, n in runs], 0),
            jnp.concatenate([places(back_ref, first_out, n) for first_out, _, n in runs], 0),
            0,
            0,
        )
        put(keep_ref, send_ref, dev_ref[2], k * width, grad.astype(BF))
    left = 2 * keep_ref.shape[0] - PIX * width
    if left > 0:
        put(keep_ref, send_ref, dev_ref[2], PIX * width, jnp.zeros((left, width), BF))


def spread_back(back_ref, w_ref, dy_ref, offsets):
    for k in offsets:
        for first_out, first_in, n in spans(k):
            for s in range(0, n, 3):
                m = min(3, n - s)
                part = dot(places(back_ref, first_out + s, m), w_ref[k], 1, 1)
                add_places(dy_ref, first_in + s, m, part, k == OFFSETS[0])


def spatial_back_kernel(back_ref, w_ref, dy_ref):
    spread_back(back_ref, w_ref, dy_ref, OFFSETS[:5])


def spatial_back_end_kernel(
    back_ref, w_ref, pre_ref, stat_ref, mask_ref, _, dy_ref, next_ref,
):
    chunks, chunk_rows, width = pre_ref.shape
    mean, inv, scale, base = (stat_ref[i : i + 1] for i in range(4))
    spread_back(back_ref, w_ref, dy_ref, OFFSETS[5:])

    def step(c, carry):
        first, second = carry
        for p in range(PIX):
            rows = slice(p * CHUNK, (p + 1) * CHUNK)
            a = pre_ref[c, rows, :]
            dy = gelu_slope(a * scale + base) * dy_ref[c, rows, :] * masks(mask_ref, c, p, width)
            dy_ref[c, rows, :] = dy
            first = first + jnp.sum(dy.reshape(CHUNK // 8, 8, width), 0)
            second = second + jnp.sum((dy * ((a - mean) * inv)).reshape(CHUNK // 8, 8, width), 0)
        return first, second

    zero = jnp.zeros((8, width), F32)
    first, second = lax.fori_loop(0, chunks, step, (zero, zero))
    next_ref[...] = jnp.concatenate(
        [jnp.sum(second, 0, keepdims=True), jnp.sum(first, 0, keepdims=True)], 0
    )


def payload_kernel(packed_ref, next_ref):
    next_ref[...] = jnp.broadcast_to(packed_ref[...][None], next_ref.shape)


def reduce_grad_kernel(
    pay_ref, stat_ref, pre_ref, dy_ref, xp_ref, mask_ref, count_ref, dev_ref,
    back_ref, keep_ref, send_ref, tot_ref,
):
    chunks, chunk_rows, width = pre_ref.shape
    depth = xp_ref.shape[2]
    count = count_ref[0:1, 0:1]
    total, scale, slope, level = backward_terms(pay_ref, stat_ref, count)
    tot_ref[...] = total

    def step(c, _):
        for p in range(PIX):
            at = slice(p * CHUNK, (p + 1) * CHUNK)
            b = dy_ref[c, at, :] * scale - level - pre_ref[c, at, :] * slope
            back_ref[c, at, :] = (b * masks(mask_ref, c, p, width)).astype(BF)
        return 0

    lax.fori_loop(0, chunks, step, 0)
    flat_back = back_ref[...].reshape(chunks * chunk_rows, width)
    block = 512
    for d in range(0, depth, block):
        grad = dot(
            xp_ref[:, :, d : d + block].reshape(chunks * chunk_rows, block), flat_back, 0, 0
        )
        put(keep_ref, send_ref, dev_ref[2], d, grad.astype(BF))


def input_kernel(back_ref, w_ref, res_ref, gin_ref, flat, obuf, sems, *, rows):
    chunks, chunk_rows, width = back_ref.shape
    depth = w_ref.shape[0]
    block = obuf.shape[2]
    lanes = block // 128
    blocks = depth // block
    tail = rows - (chunks - 1) * chunk_rows

    def copy(d):
        return pltpu.make_async_copy(
            obuf.at[d % 2], gin_ref.at[:, pl.ds(d * block, block)], sems.at[d % 2]
        )

    for d in range(blocks):
        cols = slice(d * block, (d + 1) * block)
        if d >= 2:
            copy(d - 2).wait()
        for c in range(chunks):
            part = dot(back_ref[c], w_ref[cols, :], 1, 1)
            for p in range(PIX):
                at = slice(p * CHUNK, (p + 1) * CHUNK)
                value = part[at] + res_ref[c, at, cols].astype(F32)
                for lane in range(lanes):
                    flat[c % 2, lane, pl.ds(p, CHUNK, stride=PIX), :] = value[
                        :, lane * 128 : (lane + 1) * 128
                    ]
            size = chunk_rows if c + 1 < chunks else tail
            for lane in range(lanes):
                obuf[
                    d % 2, c * chunk_rows : c * chunk_rows + size, lane * 128 : (lane + 1) * 128
                ] = flat[c % 2, lane, 0:size, :].astype(BF)
        copy(d).start()
    copy(blocks - 2).wait()
    copy(blocks - 1).wait()


def writer(stage, sems):
    pending = []
    slots = stage.shape[0]

    def write(value, target):
        slot = len(pending) % slots
        if len(pending) >= slots:
            pending[-slots].wait()
        part = stage.at[slot, pl.ds(0, value.shape[0]), pl.ds(0, value.shape[1])]
        part[...] = value
        copy = pltpu.make_async_copy(part, target, sems.at[slot])
        copy.start()
        pending.append(copy)

    def finish():
        for copy in pending[-slots:]:
            copy.wait()

    return write, finish


def unpack_half_kernel(half_ref, dev_ref, *refs, other):
    out_ref, stage, sems = refs[-3:]
    half = half_ref.shape[0]
    write, finish = writer(stage, sems)
    step = half // 4
    side = 1 - dev_ref[2] if other else dev_ref[2]
    for r in range(0, half, step):
        start = pl.multiple_of(side * half + r, 16)
        write(half_ref[r : r + step, :].astype(F32), out_ref.at[pl.ds(start, step), :])
    finish()


def unpack_plain(call, item, numbers, after=()):
    half, width = item.keep.shape
    out = shape((2 * half, width), F32)
    scratch = [pltpu.VMEM((4, half // 4, width), F32), pltpu.SemaphoreType.DMA((4,))]
    first = call(
        functools.partial(unpack_half_kernel, other=False),
        out, [VMEM, SMEM], HBM, scratch, limit=8, after=after,
    )(item.keep, numbers)
    return call(
        functools.partial(unpack_half_kernel, other=True),
        out, [VMEM, SMEM, HBM], HBM, scratch, limit=8, alias={2: 0},
    )(item.got, numbers, first)


def unpack_kernel(
    mine_ref, other_ref, dev_ref, bias_ref, one_ref, two_ref, three_ref,
    expand_ref, head_ref, jig_ref, score_ref, jig_bias_ref, head_bias_ref,
    gain_one, shift_one, gain_two, shift_two, gain_three, shift_three, rest, stage, sems,
    *, wide,
):
    half, width = mine_ref.shape
    write, finish = writer(stage, sems)
    for ref, side in ((mine_ref, dev_ref[2]), (other_ref, 1 - dev_ref[2])):
        rest[pl.ds(pl.multiple_of(side * half, 16), half), :] = ref[...]
    depth = expand_ref.shape[1]
    for i in range(depth // width):
        for r in range(0, width, 256):
            write(
                rest[i * width + r : i * width + r + 256, :].astype(F32),
                expand_ref.at[pl.ds(r, 256), pl.ds(i * width, width)],
            )
    at = depth
    quarter = depth // 4
    for i in range(4):
        for r in range(0, quarter, 256):
            write(
                rest[at + r : at + r + 256, i * 128 : (i + 1) * 128].astype(F32),
                head_ref.at[pl.ds(i * quarter + r, 256), :],
            )
    at += quarter
    quarter = jig_ref.shape[0] // 4
    for i in range(4):
        write(
            rest[at : at + quarter, i * 128 : (i + 1) * 128].astype(F32),
            jig_ref.at[pl.ds(i * quarter, quarter), :],
        )
    at += quarter
    lines = score_ref.shape[0]
    total = jnp.zeros((lines, width), F32)
    for g in range(wide):
        total = total + jnp.where(
            dev_ref[0] == g, rest[at + g * lines : at + (g + 1) * lines, :].astype(F32), 0.0
        )
    scores = jnp.zeros((lines, 128), F32)
    for j in range(4):
        scores = scores + jnp.where(dev_ref[1] == j, total[:, j * 128 : (j + 1) * 128], 0.0)
    score_ref[...] = scores + bias_ref[...]
    at += wide * lines
    biases = rest[at : at + 16, :].astype(F32)[0:1]
    jig_bias_ref[...] = biases[:, 0:128]
    head_bias_ref[...] = biases[:, 128:256]
    for ref, gain, shift in (
        (one_ref, gain_one, shift_one),
        (two_ref, gain_two, shift_two),
        (three_ref, gain_three, shift_three),
    ):
        gain[...] = ref[0:1, :]
        shift[...] = ref[1:2, :]
    finish()


def shape(dims, dtype):
    return jax.ShapeDtypeStruct(dims, dtype)


def held(dims, dtype):
    return pltpu.VMEM(dims, dtype)


def exchange(payload):
    return lax.all_to_all(payload, AXES, 0, 0)


def device_index():
    return lax.axis_index("wide") * lax.axis_size("narrow") + lax.axis_index("narrow")


def swap(value, bits):
    n = lax.axis_size("wide") * lax.axis_size("narrow")
    return lax.ppermute(value, AXES, [(i, i ^ bits[i % 2]) for i in range(n)])


def side_of(bits):
    me = device_index()
    return (me // jnp.where(me % 2 == 1, bits[1], bits[0])) % 2


def halves(ref, side):
    half = ref.shape[0] // 2
    return ref[pl.ds(pl.multiple_of(side * half, 8), half), :]


def merge_kernel(*refs, plan):
    dev_ref = refs[0]
    inputs = iter(refs[1 : 1 + sum(1 + (kind != "pass") for kind, _ in plan)])
    outputs = iter(refs[1 + sum(1 + (kind != "pass") for kind, _ in plan) :])
    for kind, index in plan:
        mine = next(inputs)
        if kind == "pass":
            target = next(outputs)
            target[...] = mine[...]
            continue
        got = next(inputs)
        if kind == "split":
            side = dev_ref[index]
            keep, send = next(outputs), next(outputs)
            keep[...] = halves(mine, side).astype(F32) + halves(got, side).astype(F32)
            send[...] = (
                halves(mine, 1 - side).astype(F32) + halves(got, 1 - side).astype(F32)
            ).astype(BF)
        elif kind == "sum":
            target = next(outputs)
            target[...] = (mine[...].astype(F32) + got[...].astype(F32)).astype(BF)
        else:
            side = dev_ref[index]
            target = next(outputs)
            half = mine.shape[0]
            target[pl.ds(pl.multiple_of(side * half, 16), half), :] = mine[...]
            target[pl.ds(pl.multiple_of((1 - side) * half, 16), half), :] = got[...]


class Sum:
    def __init__(self, keep, send, pairs, first_side):
        self.keep, self.send, self.pairs, self.sides = keep, send, pairs, first_side
        self.at = 0
        self.got = None
        self.gathering = False

    def exchange(self):
        self.got = swap(self.send, self.pairs[self.at])
        return self.got

    def last(self):
        return self.gathering and self.at == 0

    def kind(self):
        if self.gathering:
            return "join", self.sides + self.at
        if self.at + 1 < len(self.pairs):
            return "split", self.sides + self.at + 1
        return "sum", 0

    def shapes(self):
        rows, width = self.got.shape
        kind = self.kind()[0]
        if kind == "split":
            return [shape((rows // 2, width), F32), shape((rows // 2, width), BF)]
        if kind == "sum":
            return [shape((rows, width), BF)]
        return [shape((2 * rows, width), BF)]

    def take(self, results):
        kind = self.kind()[0]
        if kind == "split":
            self.keep, self.send = results
            self.at += 1
        else:
            self.keep = self.send = results[0]
            if kind == "sum":
                self.gathering = True
            else:
                self.at -= 1


def merge(call, numbers, sums, after=(), flops=0):
    shapes = [item.shapes() for item in sums]
    outs = call(
        functools.partial(merge_kernel, plan=tuple(item.kind() for item in sums)),
        [one for each in shapes for one in each],
        [SMEM] + [VMEM, VMEM] * len(sums),
        [VMEM] * sum(map(len, shapes)),
        after=after,
        flops=flops,
    )(numbers, *(value for item in sums for value in (item.keep, item.got)))
    outs = list(outs)
    for item, each in zip(sums, shapes):
        item.take(outs[: len(each)])
        outs = outs[len(each) :]


def is_in(value, values):
    return any(value is v for v in values)


def kernel_call(
    kernel, out_shape, in_specs, out_specs, scratch=(), limit=6, flops=0, bytes_accessed=0,
    after=(), resident=(), far=(), alias=None,
):
    n_in, n_after = len(in_specs), len(after)
    spare = max(0, lax.axis_size("wide") * lax.axis_size("narrow") // 16 - 2)

    def run(*refs):
        kernel(*refs[:n_in], *refs[n_in + n_after :])

    made = pl.pallas_call(
        run,
        out_shape=out_shape,
        in_specs=list(in_specs) + [HBM if is_in(a, far) else ANY for a in after],
        out_specs=out_specs,
        scratch_shapes=list(scratch),
        input_output_aliases=alias or {},
        compiler_params=pltpu.CompilerParams(vmem_limit_bytes=(limit + spare) << 20),
        cost_estimate=pl.CostEstimate(
            flops=max(1, int(flops)), bytes_accessed=1, transcendentals=0
        ),
    )

    def placed(*args):
        fixed = []
        for a, spec in zip(args, in_specs):
            if spec is HBM:
                a = pltpu.with_memory_space_constraint(a, pltpu.HBM)
            elif spec is VMEM and is_in(a, resident):
                a = pltpu.with_memory_space_constraint(a, pltpu.VMEM)
            fixed.append(a)
        for a in after:
            fixed.append(pltpu.with_memory_space_constraint(a, pltpu.HBM) if is_in(a, far) else a)
        outs = made(*fixed)
        if isinstance(out_shape, list):
            for made_shape, spec, out in zip(out_shape, out_specs, outs):
                if not isinstance(made_shape, jax.ShapeDtypeStruct):
                    resident.append(out)
                if spec is HBM:
                    far.append(out)
        elif out_specs is HBM:
            far.append(outs)
        return outs

    return placed


def body(
    block_in,
    weight_reduce,
    gain_reduce,
    shift_reduce,
    weight_spatial,
    gain_spatial,
    shift_spatial,
    weight_expand,
    gain_expand,
    shift_expand,
    head_weight,
    head_bias,
    jigsaw_weight,
    jigsaw_bias,
    resolution,
    tile_slot,
    jigsaw_perm,
    cotangent,
):
    rows, depth = block_in.shape
    width = weight_reduce.shape[1]
    tiles = rows // PIX
    chunks = -(-tiles // CHUNK)
    padded = chunks * CHUNK
    chunk_rows = CHUNK * PIX
    wide, narrow = lax.axis_size("wide"), lax.axis_size("narrow")
    n = wide * narrow
    images = jigsaw_perm.shape[0]
    own = images // narrow
    unit = 16 * n
    assert images // 4 == own
    wide_rank, narrow_rank = lax.axis_index("wide"), lax.axis_index("narrow")
    slots = lax.dynamic_slice_in_dim(tile_slot, narrow_rank * tiles, tiles, 1)
    slots = jnp.pad(slots, ((0, 0), (0, padded - tiles)), constant_values=-1)
    bits = [1 << i for i in range(n.bit_length() - 1)]
    axes = {"y": bits[1:2], "x": bits[2:3], "0": bits[3:4], "1": bits[4:]}

    even, odd = (
        bits[:1] + sum((axes[a] for a in order), []) for order in ("xy01", "yx01")
    )
    pairs = list(zip(even, odd))

    first_side = 2
    dev = jnp.stack(
        [wide_rank, narrow_rank]
        + [side_of(b) for b in pairs]
    ).astype(jnp.int32)
    row = lambda v: v.reshape(1, -1)
    block3 = lambda last, dtype: held((chunks, chunk_rows, last), dtype)
    call = functools.partial(kernel_call, resident=[], far=[])
    flops = 2 * padded * PIX * width * depth

    xp, pre_one, pay, mask, pick, back_emb, count, biases = call(
        functools.partial(reduce_kernel, tiles=tiles, own=own),
        [
            block3(depth, BF),
            block3(width, F32),
            shape((n, 2, width), F32),
            held((3, padded, 128), F32),
            held((PIX * images, padded), BF),
            held((padded, 128), BF),
            held((8, 128), F32),
            held((1, width), F32),
        ],
        [HBM, HBM, VMEM, VMEM, HBM, HBM, HBM, SMEM],
        [VMEM] * 8,
        [
            pltpu.VMEM((2, rows, 512), BF),
            pltpu.VMEM((2, 512, width), BF),
            pltpu.VMEM((2, 4, chunk_rows, 128), F32),
            pltpu.VMEM((PIX, images), jnp.int32),
            pltpu.VMEM(cotangent.shape, BF),
            pltpu.VMEM(jigsaw_weight.shape, BF),
            pltpu.SemaphoreType.DMA((2,)),
            pltpu.SemaphoreType.DMA((2,)),
            pltpu.SemaphoreType.DMA((3,)),
        ],
        limit=12,
        flops=flops,
    )(block_in, weight_reduce, slots, row(resolution), jigsaw_perm.T, cotangent, jigsaw_weight, dev)

    offset_scratch = [pltpu.VMEM((PIX, width, width), BF), pltpu.SemaphoreType.DMA((PIX,))]
    w_spatial = weight_spatial.reshape(PIX, width, width)
    hid_one, pre_two, pay, stat_one = call(
        spatial_kernel,
        [
            block3(width, BF),
            block3(width, F32),
            shape((n, 2, width), F32),
            held((8, width), F32),
        ],
        [VMEM, VMEM, HBM] + [VMEM] * 4,
        [VMEM] * 4,
        offset_scratch,
        flops=flops * 1.4,
        limit=12,
    )(exchange(pay), pre_one, w_spatial, row(gain_reduce), row(shift_reduce), mask, count)

    hid_two, gram, pay, stat_two = call(
        expand_kernel,
        [
            block3(width, BF),
            held((width, depth), BF),
            shape((n, 2, (width + depth) // 2), F32),
            held((8, width), F32),
        ],
        [VMEM] * 7,
        [VMEM] * 4,
        flops=flops,
    )(exchange(pay), pre_two, weight_expand, row(gain_spatial), row(shift_spatial), mask, count)

    block_out, dy_three, up, part, emb, head, pay, stat_three = call(
        functools.partial(output_kernel, rows=rows),
        [
            shape((rows, depth), BF),
            block3(depth, BF),
            block3(width, F32),
            held((width, depth), F32),
            held((padded, 128), F32),
            held((depth, 128), BF),
            shape((n, 2, depth), BF),
            held((8, depth), F32),
        ],
        [VMEM] * 10,
        [HBM] + [VMEM] * 7,
        [
            pltpu.VMEM((2, chunk_rows, 256), F32),
            pltpu.VMEM((2, 2, chunk_rows, 128), F32),
            pltpu.VMEM((2, rows, 256), BF),
            pltpu.VMEM((chunks, chunk_rows, 256), BF),
            pltpu.VMEM((chunks, chunk_rows, 256), BF),
            pltpu.VMEM((2, padded, 256), BF),
            pltpu.VMEM((2, SUB, 256), F32),
            pltpu.SemaphoreType.DMA((2,)),
        ],
        flops=flops * 4,
        limit=14,
    )(
        exchange(pay), hid_two, xp, weight_expand, row(gain_expand), row(shift_expand),
        head_weight, back_emb, mask, count,
    )

    lines = images // 4
    pay = exchange(pay)
    used = depth + depth // 4 + PIX * 128 // 4 + wide * lines + 16
    grad_rows = -(-used // unit) * unit
    keep, send = call(
        functools.partial(expand_grad_kernel, wide=wide),
        [shape((grad_rows // 2, width), BF)] * 2,
        [VMEM] * 13 + [SMEM],
        [VMEM] * 2,
    )(
        pay, stat_three, count, stat_two, part, gram, head,
        emb, row(head_bias), pick, jigsaw_weight, cotangent, biases, dev,
    )
    one = Sum(keep, send, pairs, first_side)
    one.exchange()
    long = 10**11
    total_three, dy_two, packed = call(
        expand_back_kernel,
        [held((2, depth), F32), block3(width, F32), shape((2, width), F32)],
        [VMEM] * 9,
        [VMEM] * 3,
        after=(one.send,),
        flops=long,
    )(pay, stat_three, up, hid_two, weight_expand, pre_two, stat_two, mask, count)

    def send_packed(packed, after):
        return exchange(
            call(payload_kernel, shape((n, 2, width), F32), [VMEM], VMEM, after=after)(packed)
        )

    pay = send_packed(packed, (one.got,))
    merge(call, dev, [one], (pay,))
    one.exchange()

    spatial_rows = -(-(PIX * width) // unit) * unit
    back_spatial, keep, send, total_two = call(
        spatial_grad_kernel,
        [
            block3(width, BF),
            shape((spatial_rows // 2, width), BF),
            shape((spatial_rows // 2, width), BF),
            held((2, width), F32),
        ],
        [VMEM] * 7 + [SMEM],
        [VMEM] * 4,
        after=(one.send,),
        flops=long,
    )(pay, stat_two, pre_two, dy_two, hid_one, mask, count, dev)
    two = Sum(keep, send, pairs, first_side)
    two.exchange()
    merge(call, dev, [one], (back_spatial,))
    one.exchange()
    partial = call(
        spatial_back_kernel,
        [block3(width, F32)],
        [VMEM, VMEM],
        [VMEM],
        after=(two.send, one.send),
        flops=long,
    )(back_spatial, w_spatial)[0]
    merge(call, dev, [one, two], (partial,))
    one.exchange()
    two.exchange()
    dy_one, packed = call(
        spatial_back_end_kernel,
        [block3(width, F32), shape((2, width), F32)],
        [VMEM] * 6,
        [VMEM] * 2,
        after=(one.send, two.send),
        alias={5: 0},
        flops=long,
    )(back_spatial, w_spatial, pre_one, stat_one, mask, partial)
    pay = send_packed(packed, (one.got,))
    merge(call, dev, [one, two], (pay,))
    one.exchange()
    two.exchange()
    back_reduce, keep, send, total_one = call(
        reduce_grad_kernel,
        [
            block3(width, BF),
            shape((depth // 2, width), BF),
            shape((depth // 2, width), BF),
            held((2, width), F32),
        ],
        [VMEM] * 7 + [SMEM],
        [VMEM] * 4,
        flops=long,
        after=(one.send, two.send),
    )(pay, stat_one, pre_one, dy_one, xp, mask, count, dev)
    three = Sum(keep, send, pairs, first_side)
    three.exchange()
    merge(call, dev, [one, two], (back_reduce,))
    one.exchange()
    two.exchange()
    gradient_input = call(
        functools.partial(input_kernel, rows=rows),
        shape((rows, depth), BF),
        [VMEM] * 3,
        HBM,
        [
            pltpu.VMEM((2, 4, chunk_rows, 128), F32),
            pltpu.VMEM((2, rows, 512), BF),
            pltpu.SemaphoreType.DMA((2,)),
        ],
        flops=long,
        limit=8,
        after=(one.send, two.send),
    )(back_reduce, weight_reduce, dy_three)

    sums = {"E": one, "S": two, "R": three}
    turns = "SRESERSERSRERSRERESRSRR" if len(bits) == 5 else "SRE" * (3 * len(bits))
    late = gradient_input
    for turn in turns:
        item = sums.get(turn)
        if item is None:
            continue
        if not item.last():
            merge(call, dev, [item], (late,), long // 20)
            item.exchange()
            late = item.send
            continue
        del sums[turn]
        if turn == "E":
            (
                gradient_expand, gradient_head, gradient_jigsaw, scores, jig_total, head_total,
                gain_one, shift_one, gain_two, shift_two, gain_three, shift_three,
            ) = call(
                functools.partial(unpack_kernel, wide=wide),
                [
                    shape((width, depth), F32),
                    shape((depth, 128), F32),
                    shape((PIX * 128, 128), F32),
                    shape((lines, 128), F32),
                    shape((1, 128), F32),
                    shape((1, 128), F32),
                ]
                + [shape((1, width), F32)] * 4
                + [shape((1, depth), F32)] * 2,
                [VMEM, VMEM, SMEM] + [VMEM] * 4,
                [HBM] * 3 + [VMEM] * 9,
                [
                    pltpu.VMEM((grad_rows, width), BF),
                    pltpu.VMEM((8, 288, width), F32),
                    pltpu.SemaphoreType.DMA((8,)),
                ],
                limit=max(12, grad_rows // 512 + 8),
                after=(late,),
            )(one.keep, one.got, dev, row(jigsaw_bias), total_one, total_two, total_three)
            late = gradient_expand
        elif turn == "S" and spatial_rows != PIX * width:
            low = side_of(two.pairs[0]) == 0
            gradient_spatial = jnp.concatenate(
                [jnp.where(low, two.keep, two.got), jnp.where(low, two.got, two.keep)]
            )[: PIX * width].astype(F32)
        elif turn == "S":
            gradient_spatial = late = unpack_plain(call, two, dev, (late,))
        else:
            gradient_reduce = late = unpack_plain(call, three, dev, (late,))
    return (
        block_out,
        scores,
        gradient_input,
        gradient_reduce,
        gain_one.reshape(-1),
        shift_one.reshape(-1),
        gradient_spatial,
        gain_two.reshape(-1),
        shift_two.reshape(-1),
        gradient_expand,
        gain_three.reshape(-1),
        shift_three.reshape(-1),
        gradient_head,
        head_total.reshape(-1),
        gradient_jigsaw,
        jig_total.reshape(-1),
    )


def solution(mesh):
    placed = (P(AXES, None),) + (P(),) * 14 + (P("wide", None),) * 3
    return jax.shard_map(
        body,
        mesh=mesh,
        in_specs=placed,
        out_specs=(P(AXES, None),) * 3 + (P(),) * 13,
        check_vma=False,
    )
```
